128 devices in a mesh: tm: 32 (over x, y_hi, z), space: 4 (over y_lo, core).
Axes of the slice: x: 4, y: 4 (y_hi: 2, y_lo: 2; y = y_hi * 2 + y_lo), z: 4, core: 2. Of those that a mesh axis runs over, the one named last changes fastest.
Arguments:
- video: bfloat16 [64, 32, 32, 384], P('tm', 'space'), may hold values from -6 to 6
- conv_weight: bfloat16 [3, 3, 3, 384, 384], replicated, may hold values from -0.0625 to 0.0625
- embed_weight: bfloat16 [384, 1152], replicated, may hold values from -0.3125 to 0.3125
- q_weight: bfloat16 [1152, 1152], replicated, may hold values from -0.1875 to 0.1875
- k_weight: bfloat16 [1152, 1152], replicated, may hold values from -0.1875 to 0.1875
- v_weight: bfloat16 [1152, 1152], replicated, may hold values from -0.1875 to 0.1875
- initial_state: float32 [16, 72, 72], P('space'), may hold values from -6144 to 6144
- probe_in: int32 [64, 32, 32, 1152], P('tm', 'space'), may hold values from -1 to 1, as said below
- probe_out: int32 [64, 32, 32, 1152], P('tm', None, None, 'space'), may hold values from -1 to 1, as said below
Outputs:
- flow: bfloat16 [64, 32, 32, 1152], P('tm', None, None, 'space')
- tangent: bfloat16 [64, 32, 32, 1152], P('tm', None, None, 'space')
- adjoint: bfloat16 [64, 32, 32, 1152], P('tm', 'space')
- state_cotangent: float32 [256, 16, 72, 72], P('tm', 'space')
The draws below stay inside these ranges and needn't reach their ends.
Inputs may be any that keep to these rules, and one draw needn't show every extreme that they name: `probe_in`: every entry is -1 or +1. `probe_out`: every entry is -1 or +1.
All inputs are finite; a program needn't handle non-finite values.
Results may differ from the reference program's by a relative error of at most 0.012.
Values may be sent and summed in bfloat16 or wider, within the bound.
A program may use at most 128 MiB of HBM per device.

```python
import jax
import jax.numpy as jnp
from jax import lax

C = 384
D = 1152
HEADS = 16
SPAN = 256
FRAME_H = 32
FRAME_W = 32
FRAMES = 64
HEAD_DIM = 72


def draw_probe_in(key, part):
    coins = jax.random.randint(jax.random.fold_in(key, 101), (FRAMES, FRAME_H, FRAME_W, D), 0, 2, dtype=jnp.int32)
    return 2 * coins - 1


def draw_probe_out(key, part):
    coins = jax.random.randint(jax.random.fold_in(key, 202), (FRAMES, FRAME_H, FRAME_W, D), 0, 2, dtype=jnp.int32)
    return 2 * coins - 1


def level_of(stream_key, extent, cuts, low, high):
    level = 1.0
    for axis_at, blocks in cuts:
        draws = jax.random.uniform(jax.random.fold_in(jax.random.fold_in(stream_key, 6), axis_at), (blocks,), jnp.float32, low / len(cuts), high / len(cuts))
        level = level * jnp.repeat(jnp.exp(draws), extent[axis_at] // blocks).reshape((-1,) + (1,) * (len(extent) - 1 - axis_at))
    return level


def noise(rng, shape, width, bound, shards=(), held_as=jnp.bfloat16):
    factor_of = level_of(rng, shape, shards, -0.22, 0.18) if shards else 1.0
    entries = jax.random.normal(rng, shape, jnp.float32) * width * factor_of
    return jnp.minimum(jnp.maximum(entries, -bound), bound).astype(held_as)


def setup_inputs(seed: int = 0) -> dict:
    seeds = jax.random.split(jax.random.key(seed), 10)
    return {
        "video": noise(seeds[0], (FRAMES, FRAME_H, FRAME_W, C), 1.0, 6.0, ((0, 32), (1, 4))),
        "conv_weight": noise(seeds[1], (3, 3, 3, C, C), (27 * C) ** -0.5, 0.0625),
        "embed_weight": noise(seeds[2], (C, D), C ** -0.5, 0.3125),
        "q_weight": noise(seeds[3], (D, D), D ** -0.5, 0.1875),
        "k_weight": noise(seeds[4], (D, D), D ** -0.5, 0.1875),
        "v_weight": noise(seeds[5], (D, D), D ** -0.5, 0.1875),
        "initial_state": noise(seeds[6], (HEADS, HEAD_DIM, HEAD_DIM), (0.015 * FRAMES * FRAME_H * FRAME_W), 6144.0, ((0, 4),), jnp.float32),
        "probe_in": draw_probe_in(jax.random.fold_in(seeds[9], 71), 0),
        "probe_out": draw_probe_out(jax.random.fold_in(seeds[9], 71), 0),
    }


def flat_dot(operand, matrix):
    dims_in = operand.shape
    result = jnp.dot(operand.reshape(-1, dims_in[-1]), matrix, preferred_element_type=jnp.float32)
    return result.reshape(dims_in[:-1] + (matrix.shape[1],))

def product(form, first, second):
    return jnp.einsum(form, first.astype(jnp.float32), second.astype(jnp.float32), precision=lax.Precision.HIGHEST)

def encode(video, conv_weight, embed_weight):
    padded = jnp.pad(video, ((2, 0), (1, 1), (1, 1), (0, 0)))
    frames, height, columns = (video.shape[0], video.shape[1], video.shape[2])
    summed = jnp.zeros((frames, height, columns, conv_weight.shape[4]), jnp.float32)
    for tap_time in range(3):
        for tap_row in range(3):
            for tap_col in range(3):
                window = padded[tap_time:tap_time + frames, tap_row:tap_row + height, tap_col:tap_col + columns]
                summed = summed + flat_dot(window, conv_weight[tap_time, tap_row, tap_col])
    active = jax.nn.silu(summed).astype(jnp.bfloat16)
    return flat_dot(active, embed_weight).astype(jnp.bfloat16)

def reference(video, conv_weight, embed_weight, q_weight, k_weight, v_weight, initial_state, probe_in, probe_out):
    latent = encode(video, conv_weight, embed_weight)
    direction = probe_in.astype(jnp.bfloat16)
    blocks = FRAMES * FRAME_H * FRAME_W // SPAN

    def split(array):
        return array.reshape(blocks, SPAN, HEADS, D // HEADS)
    query_rows = split(flat_dot(latent, q_weight).astype(jnp.bfloat16))
    key_rows = split(flat_dot(latent, k_weight).astype(jnp.bfloat16))
    value_rows = split(flat_dot(latent, v_weight).astype(jnp.bfloat16))
    query_dot = split(flat_dot(direction, q_weight).astype(jnp.bfloat16))
    key_dot = split(flat_dot(direction, k_weight).astype(jnp.bfloat16))
    value_dot = split(flat_dot(direction, v_weight).astype(jnp.bfloat16))
    states = product('cthd,cthe->chde', key_rows, value_rows)
    state_dot = product('cthd,cthe->chde', key_dot, value_rows) + product('cthd,cthe->chde', key_rows, value_dot)
    prefix = initial_state[None] + jnp.cumsum(states, 0)
    prefix_dot = jnp.cumsum(state_dot, 0)
    mixed = product('cthd,chde->cthe', query_rows, prefix)
    mixed_dot = product('cthd,chde->cthe', query_dot, prefix) + product('cthd,chde->cthe', query_rows, prefix_dot)
    scale_inv = lax.rsqrt(lax.optimization_barrier(jnp.mean(mixed * mixed, -1, keepdims=True)) + 1e-06)
    cubed = scale_inv * scale_inv * scale_inv
    flow = (mixed * scale_inv).astype(jnp.bfloat16)
    along = lax.optimization_barrier(jnp.mean(mixed * mixed_dot, -1, keepdims=True))
    tangent = (mixed_dot * scale_inv - mixed * cubed * along).astype(jnp.bfloat16)
    cotangent = split(probe_out.astype(jnp.float32))
    across = lax.optimization_barrier(jnp.mean(mixed * cotangent, -1, keepdims=True))
    mixed_bar = cotangent * scale_inv - mixed * cubed * across
    query_bar = product('cthe,chde->cthd', mixed_bar, prefix).astype(jnp.bfloat16)
    prefix_bar = product('cthd,cthe->chde', query_rows, mixed_bar)
    state_bar = jnp.cumsum(prefix_bar[::-1], 0)[::-1]
    key_bar = product('cthe,chde->cthd', value_rows, state_bar).astype(jnp.bfloat16)
    value_bar = product('cthd,chde->cthe', key_rows, state_bar).astype(jnp.bfloat16)
    full_shape = (FRAMES, FRAME_H, FRAME_W, D)
    summed = flat_dot(query_bar.reshape(full_shape), q_weight.T)
    summed = summed + flat_dot(key_bar.reshape(full_shape), k_weight.T)
    summed = summed + flat_dot(value_bar.reshape(full_shape), v_weight.T)
    return (flow.reshape(full_shape), tangent.reshape(full_shape), summed.astype(jnp.bfloat16), state_bar)
```

```python
import functools

import jax
import jax.numpy as jnp
from jax import lax
from jax.experimental import pallas as pl
from jax.experimental.pallas import tpu as pltpu
from jax.sharding import PartitionSpec as P

MESH = pl.DeviceIdType.MESH
F32 = jnp.float32
BF16 = jnp.bfloat16
D = 1152
HEADS = 16
HD = 72
C = 384
TOK = 256
TILES = D // 128
WINDOWS = (
    (0, (0, 1, 2)),
    (1, (3, 4)),
    (2, (5, 6)),
    (3, (7,)),
    (4, (8, 9)),
    (5, (10, 11)),
    (6, (12, 13)),
    (7, (14, 15)),
)
VMEM_LIMIT = 60 * 1024 * 1024


def vmem():
    return pl.BlockSpec(memory_space=pltpu.VMEM)


def anywhere():
    return pl.BlockSpec(memory_space=pl.ANY)


def dot(a, b, dims=((1,), (0,))):
    return lax.dot_general(a, b, (dims, ((), ())), preferred_element_type=F32)


def head_mask(h, tile, rows):
    lane = lax.broadcasted_iota(jnp.int32, (rows, 128), 1) + 128 * tile
    return (lane >= HD * h) & (lane < HD * (h + 1))


def compact_add(tiles, t, heads, g):
    for half in range(2):
        j = t + half
        for h in heads:
            if HD * h < 128 * (j + 1) and HD * (h + 1) > 128 * j:
                r = HD * h - 128 * t
                piece = g[r : r + HD, 128 * half : 128 * half + 128]
                piece = jnp.where(head_mask(h, j, HD), piece, 0.0)
                tiles[j] = piece if tiles[j] is None else tiles[j] + piece


def block_diagonal(tiles, t, heads):
    halves = []
    for half in range(2):
        j = t + half
        parts = []
        at = 0
        for h in heads:
            r = HD * h - 128 * t
            if r > at:
                parts.append(jnp.zeros((r - at, 128), F32))
            if HD * h < 128 * (j + 1) and HD * (h + 1) > 128 * j:
                parts.append(jnp.where(head_mask(h, j, HD), tiles[j], 0.0))
            else:
                parts.append(jnp.zeros((HD, 128), F32))
            at = r + HD
        if at < 256:
            parts.append(jnp.zeros((256 - at, 128), F32))
        halves.append(jnp.concatenate(parts, 0))
    return jnp.concatenate(halves, 1).astype(BF16)


def same_head(t, heads):
    row = lax.broadcasted_iota(jnp.int32, (256, 256), 0) + 128 * t
    col = lax.broadcasted_iota(jnp.int32, (256, 256), 1) + 128 * t
    ok = None
    for h in heads:
        low, high = HD * h, HD * (h + 1)
        both = (row >= low) & (row < high) & (col >= low) & (col < high)
        ok = both if ok is None else ok | both
    return jnp.where(ok, 1.0, 0.0).astype(BF16)


def window_out(ref, f, t, value):
    if t == 0:
        ref[f, :, 0:256] = value
    else:
        ref[f, :, 128 * t : 128 * t + 128] = ref[f, :, 128 * t : 128 * t + 128] + value[:, :128]
        ref[f, :, 128 * t + 128 : 128 * t + 256] = value[:, 128:]


def window(ref, f, t):
    return ref[f, :, 128 * t : 128 * t + 256]


def halo_kernel(ntm, nsp, video, slab, send, recv, local):
    tm, sp = lax.axis_index("tm"), lax.axis_index("space")
    later, earlier = tm + 1 < ntm, tm > 0
    down, up = sp + 1 < nsp, sp > 0
    last, first = pl.ds(TOK - 32, 32), pl.ds(0, 32)
    top, mid, bottom = pl.ds(0, 32), pl.ds(32, TOK), pl.ds(32 + TOK, 32)
    whole = pl.ds(0, TOK)
    prev, own = pl.ds(0, 2), pl.ds(2, 2)
    moves = (
        (later, earlier, whole, prev, mid, (tm + 1, sp), (tm - 1, sp)),
        (down, up, last, own, top, (tm, sp + 1), (tm, sp - 1)),
        (up, down, first, own, bottom, (tm, sp - 1), (tm, sp + 1)),
        (down & later, up & earlier, last, prev, top, (tm + 1, sp + 1), (tm - 1, sp - 1)),
        (up & later, down & earlier, first, prev, bottom, (tm + 1, sp - 1), (tm - 1, sp + 1)),
    )
    barrier = pltpu.get_barrier_semaphore()
    for _, may_recv, _, _, _, _, source in moves:

        @pl.when(may_recv)
        def _():
            pl.semaphore_signal(barrier, inc=1, device_id=source, device_id_type=MESH)

    keep = pltpu.make_async_copy(video, slab.at[own, mid], local)
    keep.start()
    pl.semaphore_wait(barrier, sum(m[0].astype(jnp.int32) for m in moves))

    copies = []
    for k, (may_send, may_recv, rows, frames, there, target, _) in enumerate(moves):
        copy = pltpu.make_async_remote_copy(
            src_ref=video.at[:, rows],
            dst_ref=slab.at[frames, there],
            send_sem=send.at[k],
            recv_sem=recv.at[k],
            device_id=target,
            device_id_type=MESH,
        )
        copies.append(copy)

        @pl.when(may_send)
        def _():
            copy.start()

        @pl.when(jnp.logical_not(may_recv))
        def _():
            slab[frames, there] = jnp.zeros((2, there.size, C), BF16)

    keep.wait()
    for copy, (may_send, may_recv, *_) in zip(copies, moves):

        @pl.when(may_send)
        def _():
            copy.wait_send()

        @pl.when(may_recv)
        def _():
            copy.wait_recv()


def halo(mesh, video):
    return pl.pallas_call(
        functools.partial(halo_kernel, mesh.shape["tm"], mesh.shape["space"]),
        out_shape=jax.ShapeDtypeStruct((4, TOK + 64, C), BF16),
        in_specs=[vmem()],
        out_specs=vmem(),
        scratch_shapes=[
            pltpu.SemaphoreType.DMA((5,)),
            pltpu.SemaphoreType.DMA((5,)),
            pltpu.SemaphoreType.DMA,
        ],
        compiler_params=pltpu.CompilerParams(
            collective_id=0, has_side_effects=True, vmem_limit_bytes=VMEM_LIMIT
        ),
        name="halo",
    )(video.reshape(2, TOK, C))


def encode_kernel(
    slab, probe_h, conv_h, embed_h, q_h, k_h, v_h,
    q_out, qd_out, k_out, v_out, st_out,
    conv_w, embed_w, q_w, k_w, v_w, probe, taps, acc, kd, vd, sems,
):
    moves = [
        pltpu.make_async_copy(src, dst, sems.at[i])
        for i, (src, dst) in enumerate(
            (
                (probe_h, probe),
                (q_h, q_w),
                (k_h, k_w),
                (v_h, v_w),
                (conv_h, conv_w),
                (embed_h, embed_w),
            )
        )
    ]
    for move in moves:
        move.start()

    col = lax.broadcasted_iota(jnp.int32, (TOK + 64, C), 0) % 32
    for f in range(4):
        here = slab[f].astype(F32)
        left = jnp.where(col == 0, 0.0, pltpu.roll(here, 1, 0))
        right = jnp.where(col == 31, 0.0, pltpu.roll(here, TOK + 63, 0))
        taps[f, :, 0:C] = left.astype(BF16)
        taps[f, :, C : 2 * C] = slab[f]
        taps[f, :, 2 * C : 3 * C] = right.astype(BF16)

    moves[0].wait()
    direction = probe[...].astype(F32).astype(BF16)
    for move, weight, out in zip(moves[1:4], (q_w, k_w, v_w), (qd_out, kd, vd)):
        move.wait()
        out[...] = dot(direction, weight[...]).astype(BF16).reshape(2, TOK, D)

    moves[4].wait()
    acc[...] = jnp.zeros_like(acc)

    @pl.loop(0, 9)
    def _(tap):
        a, b = tap // 3, tap % 3
        rows = pl.ds(pl.multiple_of(b * 32, 32), TOK)
        x = taps[pl.ds(a, 2), rows, :].reshape(2 * TOK, 3 * C)
        acc[...] += dot(x, conv_w[tap])

    u = acc[...]
    active = (u / (1.0 + jnp.exp(-u))).astype(BF16)
    moves[5].wait()
    latent = dot(active, embed_w[...]).astype(BF16)
    for weight, out in zip((q_w, k_w, v_w), (q_out, k_out, v_out)):
        out[...] = dot(latent, weight[...]).astype(BF16).reshape(2, TOK, D)

    st_out[:, TILES * 144 :, :] = jnp.zeros((2, st_out.shape[1] - TILES * 144, 128), BF16)

    @pl.loop(0, 2)
    def _(f):
        st, sd = [None] * TILES, [None] * TILES
        over = ((0,), (0,))
        for t, heads in WINDOWS:
            kw, vw = window(k_out, f, t), window(v_out, f, t)
            compact_add(st, t, heads, dot(kw, vw, over))
            both = dot(window(kd, f, t), vw, over) + dot(kw, window(vd, f, t), over)
            compact_add(sd, t, heads, both)
        for j in range(TILES):
            st_out[f, 144 * j : 144 * j + 144, :] = jnp.concatenate([st[j], sd[j]], 0).astype(BF16)


def encode(slab, probe_in, conv_weight, embed_weight, q_weight, k_weight, v_weight, padded):
    rows = jax.ShapeDtypeStruct((2, TOK, D), BF16)
    return pl.pallas_call(
        encode_kernel,
        out_shape=[rows] * 4 + [jax.ShapeDtypeStruct((2, padded, 128), BF16)],
        in_specs=[vmem()] + [anywhere()] * 6,
        out_specs=[vmem()] * 5,
        scratch_shapes=[
            pltpu.VMEM((9, 3 * C, C), BF16),
            pltpu.VMEM((C, D), BF16),
            pltpu.VMEM((D, D), BF16),
            pltpu.VMEM((D, D), BF16),
            pltpu.VMEM((D, D), BF16),
            pltpu.VMEM((2 * TOK, D), jnp.int32),
            pltpu.VMEM((4, TOK + 64, 3 * C), BF16),
            pltpu.VMEM((2 * TOK, C), F32),
            pltpu.VMEM((2, TOK, D), BF16),
            pltpu.VMEM((2, TOK, D), BF16),
            pltpu.SemaphoreType.DMA((6,)),
        ],
        compiler_params=pltpu.CompilerParams(vmem_limit_bytes=VMEM_LIMIT),
        name="encode",
    )(
        slab,
        probe_in.reshape(2 * TOK, D),
        conv_weight.reshape(9, 3 * C, C),
        embed_weight,
        q_weight,
        k_weight,
        v_weight,
    )


def scan_kernel(ntm, nsp, nz, share, reverse, blocks, out, got, sums, answer, totals, total,
                send1, recv1, send2, recv2, send3, recv3):
    tm, sp = lax.axis_index("tm"), lax.axis_index("space")
    peers, groups = nz * nsp, ntm // nz
    group, z = tm // nz, tm % nz
    me = z * nsp + sp

    def peer(k):
        p = lax.rem(me + k, peers)
        return p, (group * nz + p // nsp, p % nsp)

    def other(k):
        g = lax.rem(group + k, groups)
        return g, (g * nz + z, sp)

    barrier = pltpu.get_barrier_semaphore()

    @pl.loop(1, peers)
    def _(k):
        pl.semaphore_signal(barrier, inc=1, device_id=peer(k)[1], device_id_type=MESH)

    @pl.loop(1, groups)
    def _(k):
        pl.semaphore_signal(barrier, inc=1, device_id=other(k)[1], device_id_type=MESH)

    pl.semaphore_wait(barrier, peers + groups - 2)

    def first(k):
        p, device = peer(k)
        return pltpu.make_async_remote_copy(
            src_ref=blocks.at[:, pl.ds(pl.multiple_of(p * share, share), share)],
            dst_ref=got.at[me],
            send_sem=send1.at[p],
            recv_sem=recv1.at[me],
            device_id=device,
            device_id_type=MESH,
        )

    @pl.loop(1, peers)
    def _(k):
        first(k).start()

    got[me] = blocks[:, pl.ds(pl.multiple_of(me * share, share), share)]

    @pl.loop(1, peers)
    def _(k):
        p, _ = peer(k)
        pltpu.make_async_copy(got.at[p], got.at[p], recv1.at[p]).wait()

    running = jnp.zeros((share, 128), F32)
    order = [(zz, f) for zz in range(nz) for f in range(2)]
    for zz, f in reversed(order) if reverse else order:
        for s in reversed(range(nsp)) if reverse else range(nsp):
            running = running + got[zz * nsp + s, f].astype(F32)
            sums[zz * nsp + s, f] = running
    total[...] = running.astype(BF16)

    def second(k):
        g, device = other(k)
        return pltpu.make_async_remote_copy(
            src_ref=total,
            dst_ref=totals.at[group],
            send_sem=send2.at[g],
            recv_sem=recv2.at[group],
            device_id=device,
            device_id_type=MESH,
        )

    @pl.loop(1, groups)
    def _(k):
        second(k).start()

    totals[group] = jnp.zeros((share, 128), BF16)

    @pl.loop(1, groups)
    def _(k):
        g, _ = other(k)
        pltpu.make_async_copy(totals.at[g], totals.at[g], recv2.at[g]).wait()

    before = jnp.zeros((share, 128), F32)
    for g in range(groups):
        counts = g > group if reverse else g < group
        before = before + jnp.where(counts, totals[g].astype(F32), 0.0)
    for p in range(peers):
        answer[p] = (sums[p] + before[None]).astype(BF16)

    def third(k):
        p, device = peer(k)
        return pltpu.make_async_remote_copy(
            src_ref=answer.at[p],
            dst_ref=out.at[:, pl.ds(pl.multiple_of(me * share, share), share)],
            send_sem=send3.at[p],
            recv_sem=recv3.at[me],
            device_id=device,
            device_id_type=MESH,
        )

    @pl.loop(1, peers)
    def _(k):
        third(k).start()

    out[:, pl.ds(pl.multiple_of(me * share, share), share)] = answer[me]

    @pl.loop(1, peers)
    def _(k):
        p, _ = peer(k)
        pltpu.make_async_copy(answer.at[p], answer.at[p], recv3.at[p]).wait()

    @pl.loop(1, peers)
    def _(k):
        first(k).wait_send()
        third(k).wait_send()

    @pl.loop(1, groups)
    def _(k):
        second(k).wait_send()


def scan(mesh, blocks, reverse, collective_id):
    ntm, nsp = mesh.shape["tm"], mesh.shape["space"]
    nz = min(4, ntm)
    peers, groups = nz * nsp, ntm // nz
    share = blocks.shape[1] // peers
    dma = pltpu.SemaphoreType.DMA
    return pl.pallas_call(
        functools.partial(scan_kernel, ntm, nsp, nz, share, reverse),
        out_shape=jax.ShapeDtypeStruct(blocks.shape, BF16),
        in_specs=[vmem()],
        out_specs=vmem(),
        scratch_shapes=[
            pltpu.VMEM((peers, 2, share, 128), BF16),
            pltpu.VMEM((peers, 2, share, 128), F32),
            pltpu.VMEM((peers, 2, share, 128), BF16),
            pltpu.VMEM((groups, share, 128), BF16),
            pltpu.VMEM((share, 128), BF16),
            dma((peers,)),
            dma((peers,)),
            dma((groups,)),
            dma((groups,)),
            dma((peers,)),
            dma((peers,)),
        ],
        compiler_params=pltpu.CompilerParams(
            collective_id=collective_id, has_side_effects=True, vmem_limit_bytes=VMEM_LIMIT
        ),
        name="scan_back" if reverse else "scan",
    )(blocks)


def padded_rows(mesh, rows):
    peers = min(4, mesh.shape["tm"]) * mesh.shape["space"]
    return -(-rows // (16 * peers)) * 16 * peers


def mix_kernel(q, qd, prefix, init, po, flow, tangent, q_bar, pb_out,
               bd, m_ref, md_ref, po_ref, s1, s2, s3, mbar, acc):
    @pl.loop(0, 2)
    def _(f):
        pt, pdt = [], []
        for j in range(TILES):
            both = prefix[f, 144 * j : 144 * j + 144, :].astype(F32)
            pt.append(both[:HD] + init[:, 128 * j : 128 * j + 128])
            pdt.append(both[HD:])
        for s in range(4):
            po_ref[:, 288 * s : 288 * s + 288] = po[f, s].astype(F32)
        for t, heads in WINDOWS:
            bd[t] = block_diagonal(pt, t, heads)
            bdd = block_diagonal(pdt, t, heads)
            qw, qdw = window(q, f, t), window(qd, f, t)
            window_out(m_ref, 0, t, dot(qw, bd[t]))
            window_out(md_ref, 0, t, dot(qdw, bd[t]) + dot(qw, bdd))
        for t, heads in WINDOWS:
            ones = same_head(t, heads)
            lanes = slice(128 * t, 128 * t + 256)
            m, md, p = m_ref[0, :, lanes], md_ref[0, :, lanes], po_ref[:, lanes]
            window_out(s1, 0, t, dot((m * m).astype(BF16), ones))
            window_out(s2, 0, t, dot((m * md).astype(BF16), ones))
            window_out(s3, 0, t, dot((m * p).astype(BF16), ones))
        m, md, p = m_ref[0], md_ref[0], po_ref[...]
        scale = lax.rsqrt(s1[0] * (1.0 / HD) + 1e-6)
        pulled = m * (scale * scale * scale) * (1.0 / HD)
        mbar[0] = (p * scale - pulled * s3[0]).astype(BF16)
        fl = (m * scale).astype(BF16)
        tg = (md * scale - pulled * s2[0]).astype(BF16)
        for s in range(4):
            flow[f, s] = fl[:, 288 * s : 288 * s + 288]
            tangent[f, s] = tg[:, 288 * s : 288 * s + 288]
        pb = [None] * TILES
        for t, heads in WINDOWS:
            mw = window(mbar, 0, t)
            window_out(acc, 0, t, dot(mw, bd[t], ((1,), (1,))))
            compact_add(pb, t, heads, dot(window(q, f, t), mw, ((0,), (0,))))
        q_bar[f] = acc[0].astype(BF16)
        pb.append(jnp.zeros((pb_out.shape[1] - TILES * HD, 128), F32))
        pb_out[f] = jnp.concatenate(pb, 0).astype(BF16)


def mix(q, qd, prefix, init, po, padded):
    rows = jax.ShapeDtypeStruct((2, TOK, D), BF16)
    heads = jax.ShapeDtypeStruct((2, 4, TOK, D // 4), BF16)
    wide = pltpu.VMEM((1, TOK, D), F32)
    return pl.pallas_call(
        mix_kernel,
        out_shape=[heads, heads, rows, jax.ShapeDtypeStruct((2, padded, 128), BF16)],
        in_specs=[vmem()] * 5,
        out_specs=[vmem()] * 4,
        scratch_shapes=[
            pltpu.VMEM((8, 256, 256), BF16),
            wide,
            wide,
            pltpu.VMEM((TOK, D), F32),
            wide,
            wide,
            wide,
            pltpu.VMEM((1, TOK, D), BF16),
            wide,
        ],
        compiler_params=pltpu.CompilerParams(vmem_limit_bytes=VMEM_LIMIT),
        name="mix",
    )(q, qd, prefix, init, po)


def adjoint_kernel(q_bar, k, v, sc, q_h, k_h, v_h, out, q_w, k_w, v_w, k_bar, v_bar, acc1, acc2, sems):
    moves = [
        pltpu.make_async_copy(src, dst, sems.at[i])
        for i, (src, dst) in enumerate(((q_h, q_w), (k_h, k_w), (v_h, v_w)))
    ]
    for move in moves:
        move.start()

    @pl.loop(0, 2)
    def _(f):
        rows = sc[f].astype(F32)
        tiles = [rows[HD * j : HD * j + HD] for j in range(TILES)]
        for t, heads in WINDOWS:
            b = block_diagonal(tiles, t, heads)
            window_out(acc1, 0, t, dot(window(v, f, t), b, ((1,), (1,))))
            window_out(acc2, 0, t, dot(window(k, f, t), b))
        k_bar[f] = acc1[0].astype(BF16)
        v_bar[f] = acc2[0].astype(BF16)

    for move in moves:
        move.wait()
    total = dot(q_bar[...].reshape(2 * TOK, D), q_w[...], ((1,), (1,)))
    total = total + dot(k_bar[...].reshape(2 * TOK, D), k_w[...], ((1,), (1,)))
    total = total + dot(v_bar[...].reshape(2 * TOK, D), v_w[...], ((1,), (1,)))
    out[...] = total.astype(BF16)


def adjoint_of(q_bar, k, v, sc, q_weight, k_weight, v_weight):
    return pl.pallas_call(
        adjoint_kernel,
        out_shape=jax.ShapeDtypeStruct((2 * TOK, D), BF16),
        in_specs=[vmem()] * 4 + [anywhere()] * 3,
        out_specs=vmem(),
        scratch_shapes=[
            pltpu.VMEM((D, D), BF16),
            pltpu.VMEM((D, D), BF16),
            pltpu.VMEM((D, D), BF16),
            pltpu.VMEM((2, TOK, D), BF16),
            pltpu.VMEM((2, TOK, D), BF16),
            pltpu.VMEM((1, TOK, D), F32),
            pltpu.VMEM((1, TOK, D), F32),
            pltpu.SemaphoreType.DMA((3,)),
        ],
        compiler_params=pltpu.CompilerParams(vmem_limit_bytes=VMEM_LIMIT),
        name="adjoint",
    )(q_bar, k, v, sc, q_weight, k_weight, v_weight)


def on_device(mesh, video, conv_weight, embed_weight, q_weight, k_weight, v_weight, initial_state, probe_in, probe_out):
    po = probe_out.astype(BF16).reshape(2, 4, TOK, D // 4)
    po = lax.all_to_all(po, "space", split_axis=1, concat_axis=1, tiled=True)
    init = lax.all_gather(initial_state, "space", axis=0, tiled=True)
    init = init.transpose(1, 0, 2).reshape(HD, D)
    slab = halo(mesh, video)
    q, qd, k, v, st = encode(
        slab, probe_in, conv_weight, embed_weight, q_weight, k_weight, v_weight,
        padded_rows(mesh, TILES * 2 * HD),
    )
    prefix = scan(mesh, st, False, 1)
    flow, tangent, q_bar, pb = mix(q, qd, prefix, init, po, padded_rows(mesh, TILES * HD))
    flow = lax.all_to_all(flow, "space", split_axis=1, concat_axis=1, tiled=True)
    tangent = lax.all_to_all(tangent, "space", split_axis=1, concat_axis=1, tiled=True)
    sc = scan(mesh, pb, True, 2)
    adjoint = adjoint_of(q_bar, k, v, sc, q_weight, k_weight, v_weight)
    cot = sc[:, : TILES * HD].reshape(2, TILES, HD, 128).transpose(0, 2, 1, 3).reshape(2, HD, HEADS, HD)
    cot = cot.transpose(0, 2, 1, 3).reshape(2, 4, 4, HD, HD)
    cot = lax.all_to_all(cot, "space", split_axis=1, concat_axis=1, tiled=True)
    cot = cot.reshape(8, 4, HD, HD).astype(F32)
    full = (2, 32, 32, D // 4)
    return (flow.reshape(full), tangent.reshape(full), adjoint.reshape(2, 8, 32, D), cot)


def solution(mesh):
    by_rows = P("tm", "space", None, None)
    by_heads = P("tm", None, None, "space")
    return jax.shard_map(
        functools.partial(on_device, mesh),
        mesh=mesh,
        in_specs=(by_rows, P(), P(), P(), P(), P(), P("space", None, None), by_rows, by_heads),
        out_specs=(by_heads, by_heads, by_rows, by_rows),
        check_vma=False,
    )
```

```python
import functools

import jax
import jax.numpy as jnp
from jax import lax
from jax.experimental import pallas as pl
from jax.experimental.pallas import tpu as pltpu
from jax.sharding import PartitionSpec as P

MESH = pl.DeviceIdType.MESH
F32 = jnp.float32
BF16 = jnp.bfloat16
D = 1152
HEADS = 16
HD = 72
C = 384
TOK = 256
TILES = D // 128
WINDOWS = (
    (0, (0, 1, 2)),
    (1, (3, 4)),
    (2, (5, 6)),
    (3, (7,)),
    (4, (8, 9)),
    (5, (10, 11)),
    (6, (12, 13)),
    (7, (14, 15)),
)
VMEM_LIMIT = 60 * 1024 * 1024


PACK = 2 * TOK + TOK // 4


def vmem():
    return pl.BlockSpec(memory_space=pltpu.VMEM)


def anywhere():
    return pl.BlockSpec(memory_space=pl.ANY)


def dot(a, b, dims=((1,), (0,))):
    return lax.dot_general(a, b, (dims, ((), ())), preferred_element_type=F32)


def head_mask(h, tile, rows):
    lane = lax.broadcasted_iota(jnp.int32, (rows, 128), 1) + 128 * tile
    return (lane >= HD * h) & (lane < HD * (h + 1))


def compact_add(tiles, t, heads, g):
    for half in range(2):
        j = t + half
        for h in heads:
            if HD * h < 128 * (j + 1) and HD * (h + 1) > 128 * j:
                r = HD * h - 128 * t
                piece = g[r : r + HD, 128 * half : 128 * half + 128]
                piece = jnp.where(head_mask(h, j, HD), piece, 0.0)
                tiles[j] = piece if tiles[j] is None else tiles[j] + piece


def block_diagonal(tiles, t, heads):
    halves = []
    for half in range(2):
        j = t + half
        parts = []
        at = 0
        for h in heads:
            r = HD * h - 128 * t
            if r > at:
                parts.append(jnp.zeros((r - at, 128), F32))
            if HD * h < 128 * (j + 1) and HD * (h + 1) > 128 * j:
                parts.append(jnp.where(head_mask(h, j, HD), tiles[j], 0.0))
            else:
                parts.append(jnp.zeros((HD, 128), F32))
            at = r + HD
        if at < 256:
            parts.append(jnp.zeros((256 - at, 128), F32))
        halves.append(jnp.concatenate(parts, 0))
    return jnp.concatenate(halves, 1).astype(BF16)


def same_head(t, heads):
    row = lax.broadcasted_iota(jnp.int32, (256, 256), 0) + 128 * t
    col = lax.broadcasted_iota(jnp.int32, (256, 256), 1) + 128 * t
    ok = None
    for h in heads:
        low, high = HD * h, HD * (h + 1)
        both = (row >= low) & (row < high) & (col >= low) & (col < high)
        ok = both if ok is None else ok | both
    return jnp.where(ok, 1.0, 0.0).astype(BF16)


def window_out(ref, f, t, value):
    if t == 0:
        ref[f, :, 0:256] = value
    else:
        ref[f, :, 128 * t : 128 * t + 128] = ref[f, :, 128 * t : 128 * t + 128] + value[:, :128]
        ref[f, :, 128 * t + 128 : 128 * t + 256] = value[:, 128:]


def pack(x):
    rest = x[:, 256:]
    rest = jnp.concatenate([rest[64 * i : 64 * i + 64] for i in range(4)], 1)
    return jnp.concatenate([x[:, :128], x[:, 128:256], rest], 0)


def unpack(x):
    rest = jnp.concatenate([x[2 * TOK :, 32 * i : 32 * i + 32] for i in range(4)], 0)
    return jnp.concatenate([x[:TOK], x[TOK : 2 * TOK], rest], 1)


def arrived(ref, sem):
    pltpu.make_async_copy(ref, ref, sem).wait()


def window(ref, f, t):
    return ref[f, :, 128 * t : 128 * t + 256]


class Scan:
    def __init__(self, place, reverse, blocks, out, got, sums, answer, totals, total, s1, r1, s2, r2, s3, r3):
        self.place, self.reverse = place, reverse
        self.blocks, self.out, self.got, self.sums, self.answer = blocks, out, got, sums, answer
        self.totals, self.total = totals, total
        self.s1, self.r1, self.s2, self.r2, self.s3, self.r3 = s1, r1, s2, r2, s3, r3
        self.share = got.shape[2]

    def rows(self, p):
        return pl.ds(pl.multiple_of(p * self.share, self.share), self.share)

    def first(self, k):
        p, device = self.place.peer(k)
        return pltpu.make_async_remote_copy(
            src_ref=self.blocks.at[:, self.rows(p)],
            dst_ref=self.got.at[self.place.me],
            send_sem=self.s1.at[p],
            recv_sem=self.r1.at[self.place.me],
            device_id=device,
            device_id_type=MESH,
        )

    def second(self, k):
        g, device = self.place.other(k)
        return pltpu.make_async_remote_copy(
            src_ref=self.total,
            dst_ref=self.totals.at[self.place.group],
            send_sem=self.s2.at[g],
            recv_sem=self.r2.at[self.place.group],
            device_id=device,
            device_id_type=MESH,
        )

    def third(self, k):
        p, device = self.place.peer(k)
        return pltpu.make_async_remote_copy(
            src_ref=self.answer.at[p],
            dst_ref=self.out.at[:, self.rows(self.place.me)],
            send_sem=self.s3.at[p],
            recv_sem=self.r3.at[self.place.me],
            device_id=device,
            device_id_type=MESH,
        )

    def start(self):
        @pl.loop(1, self.place.peers)
        def _(k):
            self.first(k).start()

        self.got[self.place.me] = self.blocks[:, self.rows(self.place.me)]

    def group_sums(self):
        @pl.loop(1, self.place.peers)
        def _(k):
            p, _ = self.place.peer(k)
            arrived(self.got.at[p], self.r1.at[p])

        nsp = self.place.nsp
        running = jnp.zeros((self.share, 128), F32)
        order = [(zz * nsp + s, f) for zz in range(self.place.nz) for f in range(2) for s in range(nsp)]
        for p, f in reversed(order) if self.reverse else order:
            running = running + self.got[p, f].astype(F32)
            self.sums[p, f] = running
        self.total[...] = running.astype(BF16)

        @pl.loop(1, self.place.groups)
        def _(k):
            self.second(k).start()

        self.totals[self.place.group] = jnp.zeros((self.share, 128), BF16)

    def send_back(self):
        @pl.loop(1, self.place.groups)
        def _(k):
            g, _ = self.place.other(k)
            arrived(self.totals.at[g], self.r2.at[g])

        group = self.place.group
        before = jnp.zeros((self.share, 128), F32)
        for g in range(self.place.groups):
            counts = g > group if self.reverse else g < group
            before = before + jnp.where(counts, self.totals[g].astype(F32), 0.0)
        for p in range(self.place.peers):
            self.answer[p] = (self.sums[p] + before[None]).astype(BF16)

        @pl.loop(1, self.place.peers)
        def _(k):
            self.third(k).start()

        self.out[:, self.rows(self.place.me)] = self.answer[self.place.me]

    def finish(self):
        @pl.loop(1, self.place.peers)
        def _(k):
            p, _ = self.place.peer(k)
            arrived(self.answer.at[p], self.r3.at[p])

    def drain(self):
        @pl.loop(1, self.place.peers)
        def _(k):
            self.first(k).wait_send()
            self.third(k).wait_send()

        @pl.loop(1, self.place.groups)
        def _(k):
            self.second(k).wait_send()


class Place:
    def __init__(self, ntm, nsp):
        self.ntm, self.nsp = ntm, nsp
        self.nz = min(4, ntm)
        self.tm, self.sp = lax.axis_index("tm"), lax.axis_index("space")
        self.peers, self.groups = self.nz * nsp, ntm // self.nz
        self.group, self.z = self.tm // self.nz, self.tm % self.nz
        self.me = self.z * nsp + self.sp

    def peer(self, k):
        p = lax.rem(self.me + k, self.peers)
        return p, (self.group * self.nz + p // self.nsp, p % self.nsp)

    def other(self, k):
        g = lax.rem(self.group + k, self.groups)
        return g, (g * self.nz + self.z, self.sp)

    def mate(self, k):
        s = lax.rem(self.sp + k, self.nsp)
        return s, (self.tm, s)


def scan_scratch(place_shape, share):
    ntm, nsp = place_shape
    nz = min(4, ntm)
    peers, groups = nz * nsp, ntm // nz
    dma = pltpu.SemaphoreType.DMA
    return [
        pltpu.VMEM((2, peers * share, 128), BF16),
        pltpu.VMEM((2, peers * share, 128), BF16),
        pltpu.VMEM((peers, 2, share, 128), BF16),
        pltpu.VMEM((peers, 2, share, 128), F32),
        pltpu.VMEM((peers, 2, share, 128), BF16),
        pltpu.VMEM((groups, share, 128), BF16),
        pltpu.VMEM((share, 128), BF16),
        dma((peers,)),
        dma((peers,)),
        dma((groups,)),
        dma((groups,)),
        dma((peers,)),
        dma((peers,)),
    ]


def exchange(place, send, recv, send_sem, recv_sem, k):
    s, device = place.mate(k)
    return pltpu.make_async_remote_copy(
        src_ref=send.at[s],
        dst_ref=recv.at[place.sp],
        send_sem=send_sem.at[s],
        recv_sem=recv_sem.at[place.sp],
        device_id=device,
        device_id_type=MESH,
    )


def kernel(
    shape,
    video, conv_h, embed_h, q_h, k_h, v_h, init_in, probe_h, po_h,
    flow_out, tangent_out, adj_out, cot_out,
    slab, q_w, k_w, v_w, q, qd, k, v, latent, po_send, po_recv, po, init_send, init_recv, init,
    out_send, out_recv, cot_send, cot_recv,
    halo_send, halo_recv, load, keep_sem, po_s, po_r, init_s, init_r, out_s, out_r, cot_s, cot_r,
    *scans,
):
    ntm, nsp = shape
    place = Place(ntm, nsp)
    tm, sp = place.tm, place.sp
    forward = Scan(place, False, *scans[: len(scans) // 2])
    backward = Scan(place, True, *scans[len(scans) // 2 :])

    later, earlier = tm + 1 < ntm, tm > 0
    down, up = sp + 1 < nsp, sp > 0
    last, first = pl.ds(TOK - 32, 32), pl.ds(0, 32)
    top, mid, bottom = pl.ds(0, 32), pl.ds(32, TOK), pl.ds(32 + TOK, 32)
    whole = pl.ds(0, TOK)
    prev, own = pl.ds(0, 2), pl.ds(2, 2)
    moves = (
        (down, up, last, own, top, (tm, sp + 1), (tm, sp - 1)),
        (up, down, first, own, bottom, (tm, sp - 1), (tm, sp + 1)),
        (later, earlier, whole, prev, mid, (tm + 1, sp), (tm - 1, sp)),
        (down & later, up & earlier, last, prev, top, (tm + 1, sp + 1), (tm - 1, sp - 1)),
        (up & later, down & earlier, first, prev, bottom, (tm + 1, sp - 1), (tm - 1, sp + 1)),
    )

    barrier = pltpu.get_barrier_semaphore()
    for _, may_recv, _, _, _, _, source in moves:

        @pl.when(may_recv)
        def _():
            pl.semaphore_signal(barrier, inc=1, device_id=source, device_id_type=MESH)

    @pl.loop(1, place.peers)
    def _(i):
        pl.semaphore_signal(barrier, inc=1, device_id=place.peer(i)[1], device_id_type=MESH)

    @pl.loop(1, place.groups)
    def _(i):
        pl.semaphore_signal(barrier, inc=1, device_id=place.other(i)[1], device_id_type=MESH)

    def encode(conv_w, embed_w, probe, po_i, taps, acc, kd, vd):
        loads = [
            pltpu.make_async_copy(src, dst, load.at[i])
            for i, (src, dst) in enumerate(
                (
                    (po_h, po_i),
                    (probe_h, probe),
                    (k_h, k_w),
                    (v_h, v_w),
                    (conv_h, conv_w),
                    (embed_h, embed_w),
                    (q_h, q_w),
                )
            )
        ]
        keep = pltpu.make_async_copy(video, slab.at[own, mid], keep_sem)
        keep.start()
        for one in loads:
            one.start()

        for _, may_recv, _, frames, there, _, _ in moves:

            @pl.when(jnp.logical_not(may_recv))
            def _():
                slab[frames, there] = jnp.zeros((2, there.size, C), BF16)

        heads = [init_in[j] for j in range(4)]
        init_send[...] = jnp.concatenate(heads + [jnp.zeros((HD, 96), F32)], 1)

        pl.semaphore_wait(barrier, sum(m[0].astype(jnp.int32) for m in moves) + place.peers + place.groups - 2)

        copies = []
        for i, (may_send, _, rows, frames, there, target, _) in enumerate(moves):
            copy = pltpu.make_async_remote_copy(
                src_ref=video.at[:, rows],
                dst_ref=slab.at[frames, there],
                send_sem=halo_send.at[i],
                recv_sem=halo_recv.at[i],
                device_id=target,
                device_id_type=MESH,
            )
            copies.append(copy)

            @pl.when(may_send)
            def _():
                copy.start()

        loads[0].wait()
        for f in range(2):
            for s in range(nsp):
                po_send[s, f] = pack(po_i[f, TOK * s : TOK * s + TOK, :].astype(F32)).astype(BF16)

        @pl.loop(1, nsp)
        def _(i):
            exchange(place, po_send, po_recv, po_s, po_r, i).start()

        po_recv[sp] = po_send[sp]

        @pl.loop(1, nsp)
        def _(i):
            init_move(i).start()

        init_recv[sp] = init_send[...]

        loads[1].wait()
        direction = probe[...].astype(F32).astype(BF16)
        for one, weight, out in zip(loads[2:4], (k_w, v_w), (kd, vd)):
            one.wait()
            out[...] = dot(direction, weight[...]).astype(BF16).reshape(2, TOK, D)

        def halo_wait(i):
            @pl.when(moves[i][1])
            def _():
                copies[i].wait_recv()

        col = lax.broadcasted_iota(jnp.int32, (TOK + 64, C), 0) % 32

        def build(f):
            here = slab[f].astype(F32)
            left = jnp.where(col == 0, 0.0, pltpu.roll(here, 1, 0))
            right = jnp.where(col == 31, 0.0, pltpu.roll(here, TOK + 63, 0))
            taps[f, :, 0:C] = left.astype(BF16)
            taps[f, :, C : 2 * C] = slab[f]
            taps[f, :, 2 * C : 3 * C] = right.astype(BF16)

        def convolve(low, high):
            @pl.loop(low, high)
            def _(tap):
                a, b = tap // 3, tap % 3
                rows = pl.ds(pl.multiple_of(b * 32, 32), TOK)
                x = taps[pl.ds(a, 2), rows, :].reshape(2 * TOK, 3 * C)
                acc[...] += dot(x, conv_w[tap])

        acc[...] = jnp.zeros_like(acc)
        keep.wait()
        halo_wait(0)
        halo_wait(1)
        build(2)
        build(3)
        loads[4].wait()
        convolve(6, 9)
        halo_wait(2)
        halo_wait(3)
        halo_wait(4)
        build(0)
        build(1)
        convolve(0, 6)

        u = acc[...]
        active = (u / (1.0 + jnp.exp(-u))).astype(BF16)
        loads[5].wait()
        latent[...] = dot(active, embed_w[...]).astype(BF16)
        for weight, out in zip((k_w, v_w), (k, v)):
            out[...] = dot(latent[...], weight[...]).astype(BF16).reshape(2, TOK, D)

        blocks = forward.blocks
        blocks[:, TILES * 144 :, :] = jnp.zeros((2, blocks.shape[1] - TILES * 144, 128), BF16)

        @pl.loop(0, 2)
        def _(f):
            st, sd = [None] * TILES, [None] * TILES
            over = ((0,), (0,))
            for t, heads in WINDOWS:
                kw, vw = window(k, f, t), window(v, f, t)
                compact_add(st, t, heads, dot(kw, vw, over))
                both = dot(window(kd, f, t), vw, over) + dot(kw, window(vd, f, t), over)
                compact_add(sd, t, heads, both)
            for j in range(TILES):
                blocks[f, 144 * j : 144 * j + 144, :] = jnp.concatenate([st[j], sd[j]], 0).astype(BF16)

        forward.start()
        loads[6].wait()
        q[...] = dot(latent[...], q_w[...]).astype(BF16).reshape(2, TOK, D)
        qd[...] = dot(direction, q_w[...]).astype(BF16).reshape(2, TOK, D)
        for copy, (may_send, *_) in zip(copies, moves):

            @pl.when(may_send)
            def _():
                copy.wait_send()

    def init_move(i):
        _, device = place.mate(i)
        return pltpu.make_async_remote_copy(
            src_ref=init_send,
            dst_ref=init_recv.at[sp],
            send_sem=init_s.at[i],
            recv_sem=init_r.at[sp],
            device_id=device,
            device_id_type=MESH,
        )

    pl.run_scoped(
        encode,
        pltpu.VMEM((9, 3 * C, C), BF16),
        pltpu.VMEM((C, D), BF16),
        pltpu.VMEM((2 * TOK, D), jnp.int32),
        pltpu.VMEM((2, 4 * TOK, D // 4), jnp.int32),
        pltpu.VMEM((4, TOK + 64, 3 * C), BF16),
        pltpu.VMEM((2 * TOK, C), F32),
        pltpu.VMEM((2, TOK, D), BF16),
        pltpu.VMEM((2, TOK, D), BF16),
    )

    forward.group_sums()

    @pl.loop(1, nsp)
    def _(i):
        s, _ = place.mate(i)
        arrived(po_recv.at[s], po_r.at[s])
        arrived(init_recv.at[s], init_r.at[s])

    for s in range(nsp):
        init[:, 288 * s : 288 * s + 288] = init_recv[s, :, 0:288]
        for f in range(2):
            po[f, :, 288 * s : 288 * s + 288] = unpack(po_recv[s, f].astype(F32)).astype(BF16)

    forward.send_back()
    forward.finish()
    prefix = forward.out

    def mixing(bd, m_ref, md_ref, s1, s2, s3, mbar, q_bar, adj):
        blocks = backward.blocks

        @pl.loop(0, 2)
        def _(f):
            pt, pdt = [], []
            for j in range(TILES):
                both = prefix[f, 144 * j : 144 * j + 144, :].astype(F32)
                pt.append(both[:HD] + init[:, 128 * j : 128 * j + 128])
                pdt.append(both[HD:])
            for t, heads in WINDOWS:
                bd[t] = block_diagonal(pt, t, heads)
                bdd = block_diagonal(pdt, t, heads)
                qw, qdw = window(q, f, t), window(qd, f, t)
                window_out(m_ref, 0, t, dot(qw, bd[t]))
                window_out(md_ref, 0, t, dot(qdw, bd[t]) + dot(qw, bdd))
            for t, heads in WINDOWS:
                ones = same_head(t, heads)
                lanes = slice(128 * t, 128 * t + 256)
                m, md, p = m_ref[0, :, lanes], md_ref[0, :, lanes], po[f, :, lanes].astype(F32)
                window_out(s1, 0, t, dot((m * m).astype(BF16), ones))
                window_out(s2, 0, t, dot((m * md).astype(BF16), ones))
                window_out(s3, 0, t, dot((m * p).astype(BF16), ones))
            m, md, p = m_ref[0], md_ref[0], po[f].astype(F32)
            scale = lax.rsqrt(s1[0] * (1.0 / HD) + 1e-6)
            pulled = m * (scale * scale * scale) * (1.0 / HD)
            mbar[0] = (p * scale - pulled * s3[0]).astype(BF16)
            fl = m * scale
            tg = md * scale - pulled * s2[0]
            for s in range(nsp):
                out_send[s, 0, f] = pack(fl[:, 288 * s : 288 * s + 288]).astype(BF16)
                out_send[s, 1, f] = pack(tg[:, 288 * s : 288 * s + 288]).astype(BF16)
            pb = [None] * TILES
            for t, heads in WINDOWS:
                mw = window(mbar, 0, t)
                window_out(s1, 0, t, dot(mw, bd[t], ((1,), (1,))))
                compact_add(pb, t, heads, dot(window(q, f, t), mw, ((0,), (0,))))
            q_bar[f] = s1[0].astype(BF16)
            pb.append(jnp.zeros((blocks.shape[1] - TILES * HD, 128), F32))
            blocks[f] = jnp.concatenate(pb, 0).astype(BF16)

        backward.start()

        @pl.loop(1, nsp)
        def _(i):
            exchange(place, out_send, out_recv, out_s, out_r, i).start()

        out_recv[sp] = out_send[sp]

        @pl.loop(0, 2)
        def _(f):
            adj[f] = dot(q_bar[f], q_w[...], ((1,), (1,)))

        backward.group_sums()
        backward.send_back()
        backward.finish()
        sc = backward.out

        @pl.loop(0, 2)
        def _(f):
            rows = sc[f].astype(F32)
            tiles = [rows[HD * j : HD * j + HD] for j in range(TILES)]
            for s in range(nsp):
                wide = jnp.concatenate(tiles[2 * s : 2 * s + 3], 1)[:, 32 * s : 32 * s + 288]
                parts = [wide[:, :128], wide[:, 128:256]]
                parts.append(jnp.concatenate([wide[:, 256:], jnp.zeros((HD, 96), F32)], 1))
                parts.append(jnp.zeros((8, 128), F32))
                cot_send[s, f] = jnp.concatenate(parts, 0).astype(BF16)

        @pl.loop(1, nsp)
        def _(i):
            exchange(place, cot_send, cot_recv, cot_s, cot_r, i).start()

        cot_recv[sp] = cot_send[sp]

        @pl.loop(0, 2)
        def _(f):
            rows = sc[f].astype(F32)
            tiles = [rows[HD * j : HD * j + HD] for j in range(TILES)]
            for t, heads in WINDOWS:
                b = block_diagonal(tiles, t, heads)
                window_out(s1, 0, t, dot(window(v, f, t), b, ((1,), (1,))))
                window_out(s2, 0, t, dot(window(k, f, t), b))
            total = adj[f] + dot(s1[0].astype(BF16), k_w[...], ((1,), (1,)))
            total = total + dot(s2[0].astype(BF16), v_w[...], ((1,), (1,)))
            adj_out[f] = total.astype(BF16)

    wide = pltpu.VMEM((1, TOK, D), F32)
    pl.run_scoped(
        mixing,
        pltpu.VMEM((8, 256, 256), BF16),
        wide,
        wide,
        wide,
        wide,
        wide,
        pltpu.VMEM((1, TOK, D), BF16),
        pltpu.VMEM((2, TOK, D), BF16),
        pltpu.VMEM((2, TOK, D), F32),
    )

    @pl.loop(1, nsp)
    def _(i):
        s, _ = place.mate(i)
        arrived(out_recv.at[s], out_r.at[s])
        arrived(cot_recv.at[s], cot_r.at[s])

    @pl.loop(0, nsp)
    def _(s):
        for f in range(2):
            flow_out[f, s] = unpack(out_recv[s, 0, f].astype(F32)).astype(BF16)
            tangent_out[f, s] = unpack(out_recv[s, 1, f].astype(F32)).astype(BF16)
            rows = cot_recv[s, f].astype(F32)
            lanes = jnp.concatenate([rows[HD * i : HD * i + HD] for i in range(3)], 1)
            for j in range(4):
                cot_out[f, s, j] = lanes[:, HD * j : HD * j + HD]

    @pl.loop(1, nsp)
    def _(i):
        exchange(place, po_send, po_recv, po_s, po_r, i).wait_send()
        init_move(i).wait_send()
        exchange(place, out_send, out_recv, out_s, out_r, i).wait_send()
        exchange(place, cot_send, cot_recv, cot_s, cot_r, i).wait_send()

    forward.drain()
    backward.drain()


def padded_rows(shape, rows):
    peers = min(4, shape[0]) * shape[1]
    return -(-rows // (16 * peers)) * 16 * peers


def on_device(shape, video, conv_weight, embed_weight, q_weight, k_weight, v_weight, initial_state, probe_in, probe_out):
    ntm, nsp = shape
    peers = min(4, ntm) * nsp
    dma = pltpu.SemaphoreType.DMA
    heads = jax.ShapeDtypeStruct((2, nsp, TOK, D // 4), BF16)
    rows = pltpu.VMEM((2, TOK, D), BF16)
    square = pltpu.VMEM((D, D), BF16)
    packed = pltpu.VMEM((nsp, 2, PACK, 128), BF16)
    twice = pltpu.VMEM((nsp, 2, 2, PACK, 128), BF16)
    cots = pltpu.VMEM((nsp, 2, 224, 128), BF16)
    four = dma((nsp,))
    flow, tangent, adjoint, cot = pl.pallas_call(
        functools.partial(kernel, shape),
        out_shape=[
            heads,
            heads,
            jax.ShapeDtypeStruct((2, TOK, D), BF16),
            jax.ShapeDtypeStruct((2, nsp, 4, HD, HD), F32),
        ],
        in_specs=[anywhere()] * 6 + [vmem()] + [anywhere()] * 2,
        out_specs=[vmem()] * 4,
        scratch_shapes=[
            pltpu.VMEM((4, TOK + 64, C), BF16),
            square,
            square,
            square,
            rows,
            rows,
            rows,
            rows,
            pltpu.VMEM((2 * TOK, D), BF16),
            packed,
            packed,
            rows,
            pltpu.VMEM((HD, 384), F32),
            pltpu.VMEM((nsp, HD, 384), F32),
            pltpu.VMEM((HD, D), F32),
            twice,
            twice,
            cots,
            cots,
            dma((5,)),
            dma((5,)),
            dma((7,)),
            dma,
            four,
            four,
            four,
            four,
            four,
            four,
            four,
            four,
        ]
        + scan_scratch(shape, padded_rows(shape, TILES * 2 * HD) // peers)
        + scan_scratch(shape, padded_rows(shape, TILES * HD) // peers),
        compiler_params=pltpu.CompilerParams(
            collective_id=0, has_side_effects=True, vmem_limit_bytes=VMEM_LIMIT
        ),
        name="flow_layer",
    )(
        video.reshape(2, TOK, C),
        conv_weight.reshape(9, 3 * C, C),
        embed_weight,
        q_weight,
        k_weight,
        v_weight,
        initial_state,
        probe_in.reshape(2 * TOK, D),
        probe_out.reshape(2, 4 * TOK, D // 4),
    )
    full = (2, 32, 32, D // 4)
    return (
        flow.reshape(full),
        tangent.reshape(full),
        adjoint.reshape(2, 8, 32, D),
        cot.reshape(8, 4, HD, HD),
    )


def solution(mesh):
    by_rows = P("tm", "space", None, None)
    by_heads = P("tm", None, None, "space")
    return jax.shard_map(
        functools.partial(on_device, (mesh.shape["tm"], mesh.shape["space"])),
        mesh=mesh,
        in_specs=(by_rows, P(), P(), P(), P(), P(), P("space", None, None), by_rows, by_heads),
        out_specs=(by_heads, by_heads, by_rows, by_rows),
        check_vma=False,
    )
```

```python
import functools

import jax
import jax.numpy as jnp
from jax import lax
from jax.experimental import pallas as pl
from jax.experimental.pallas import tpu as pltpu
from jax.sharding import PartitionSpec as P

MESH = pl.DeviceIdType.MESH
F32 = jnp.float32
BF16 = jnp.bfloat16
D = 1152
HEADS = 16
HD = 72
C = 384
TOK = 256
TILES = D // 128
WINDOWS = (
    (0, (0, 1, 2)),
    (1, (3, 4)),
    (2, (5, 6)),
    (3, (7,)),
    (4, (8, 9)),
    (5, (10, 11)),
    (6, (12, 13)),
    (7, (14, 15)),
)
VMEM_LIMIT = 60 * 1024 * 1024


PARTS = ((WINDOWS[:4], 0, 5, (0, 1)), (WINDOWS[4:], 4, 5, (2, 3)))
COT = 176
PACK = 2 * TOK + TOK // 4


def vmem():
    return pl.BlockSpec(memory_space=pltpu.VMEM)


def anywhere():
    return pl.BlockSpec(memory_space=pl.ANY)


def dot(a, b, dims=((1,), (0,))):
    return lax.dot_general(a, b, (dims, ((), ())), preferred_element_type=F32)


def head_mask(h, tile, rows):
    lane = lax.broadcasted_iota(jnp.int32, (rows, 128), 1) + 128 * tile
    return (lane >= HD * h) & (lane < HD * (h + 1))


def compact_add(tiles, t, heads, g):
    for half in range(2):
        j = t + half
        for h in heads:
            if HD * h < 128 * (j + 1) and HD * (h + 1) > 128 * j:
                r = HD * h - 128 * t
                piece = g[r : r + HD, 128 * half : 128 * half + 128]
                piece = jnp.where(head_mask(h, j, HD), piece, 0.0)
                tiles[j] = tiles[j] + piece if j in tiles else piece


def block_diagonal(tiles, t, heads):
    halves = []
    for half in range(2):
        j = t + half
        parts = []
        at = 0
        for h in heads:
            r = HD * h - 128 * t
            if r > at:
                parts.append(jnp.zeros((r - at, 128), F32))
            if HD * h < 128 * (j + 1) and HD * (h + 1) > 128 * j:
                parts.append(jnp.where(head_mask(h, j, HD), tiles[j], 0.0))
            else:
                parts.append(jnp.zeros((HD, 128), F32))
            at = r + HD
        if at < 256:
            parts.append(jnp.zeros((256 - at, 128), F32))
        halves.append(jnp.concatenate(parts, 0))
    return jnp.concatenate(halves, 1).astype(BF16)


def same_head(t, heads):
    row = lax.broadcasted_iota(jnp.int32, (256, 256), 0) + 128 * t
    col = lax.broadcasted_iota(jnp.int32, (256, 256), 1) + 128 * t
    ok = None
    for h in heads:
        low, high = HD * h, HD * (h + 1)
        both = (row >= low) & (row < high) & (col >= low) & (col < high)
        ok = both if ok is None else ok | both
    return jnp.where(ok, 1.0, 0.0).astype(BF16)


def window_out(ref, t, value):
    if t == 0:
        ref[:, 0:256] = value
    else:
        ref[:, 128 * t : 128 * t + 128] = ref[:, 128 * t : 128 * t + 128] + value[:, :128]
        ref[:, 128 * t + 128 : 128 * t + 256] = value[:, 128:]


def pack(x):
    rest = x[:, 256:]
    rest = jnp.concatenate([rest[64 * i : 64 * i + 64] for i in range(4)], 1)
    return jnp.concatenate([x[:, :128], x[:, 128:256], rest], 0)


def unpack(x):
    rest = jnp.concatenate([x[2 * TOK :, 32 * i : 32 * i + 32] for i in range(4)], 0)
    return jnp.concatenate([x[:TOK], x[TOK : 2 * TOK], rest], 1)


def arrived(ref, sem):
    pltpu.make_async_copy(ref, ref, sem).wait()


def window(ref, f, t):
    return ref[f, :, 128 * t : 128 * t + 256]


class Place:
    def __init__(self, ntm, nsp):
        self.ntm, self.nsp = ntm, nsp
        self.nz, self.ny = min(4, ntm), nsp // 2
        self.tm, self.sp = lax.axis_index("tm"), lax.axis_index("space")
        self.peers, self.groups = self.nz * self.ny, ntm // self.nz
        self.group, self.z = self.tm // self.nz, self.tm % self.nz
        self.y, self.core = self.sp // 2, self.sp % 2
        self.me = self.z * self.ny + self.y
        self.twin = (self.tm, self.sp + 1 - 2 * self.core)

    def peer(self, k):
        p = lax.rem(self.me + k, self.peers)
        return p, (self.group * self.nz + p // self.ny, 2 * (p % self.ny) + self.core)

    def other(self, k):
        g = lax.rem(self.group + k, self.groups)
        return g, (g * self.nz + self.z, self.sp)

    def mate(self, k):
        s = lax.rem(self.sp + k, self.nsp)
        return s, (self.tm, s)


def remote(src, dst, send_sem, recv_sem, device):
    return pltpu.make_async_remote_copy(
        src_ref=src,
        dst_ref=dst,
        send_sem=send_sem,
        recv_sem=recv_sem,
        device_id=device,
        device_id_type=MESH,
    )


class Scan:
    def __init__(self, place, reverse, rows, blocks, out, pair, chip, got, sums, answer, back, theirs, totals, total,
                 s0, r0, s1, r1, s2, r2, s3, r3, s4, r4):
        self.place, self.reverse, self.rows = place, reverse, rows
        self.blocks, self.out, self.pair, self.chip, self.got = blocks, out, pair, chip, got
        self.sums, self.answer, self.back, self.theirs = sums, answer, back, theirs
        self.totals, self.total = totals, total
        self.s0, self.r0, self.s1, self.r1, self.s2, self.r2 = s0, r0, s1, r1, s2, r2
        self.s3, self.r3, self.s4, self.r4 = s3, r3, s4, r4
        self.share = got.shape[2]

    def half(self, c):
        n = self.chip.shape[1]
        return pl.ds(pl.multiple_of(c * n, n), n)

    def part(self, p):
        return pl.ds(pl.multiple_of(p * self.share, self.share), self.share)

    def used(self, p):
        return (self.place.core * self.place.peers + p) * self.share < self.rows

    def swap(self):
        return remote(
            self.blocks.at[:, self.half(1 - self.place.core)], self.pair, self.s0, self.r0, self.place.twin
        )

    def first(self, k):
        p, device = self.place.peer(k)
        me = self.place.me
        return remote(self.chip.at[:, self.part(p)], self.got.at[me], self.s1.at[p], self.r1.at[me], device)

    def second(self, k):
        g, device = self.place.other(k)
        mine = self.place.group
        return remote(self.total, self.totals.at[mine], self.s2.at[g], self.r2.at[mine], device)

    def third(self, k):
        p, device = self.place.peer(k)
        me = self.place.me
        return remote(self.answer.at[p], self.back.at[:, self.part(me)], self.s3.at[p], self.r3.at[me], device)

    def fourth(self):
        return remote(self.theirs, self.out.at[:, self.half(self.place.core)], self.s4, self.r4, self.place.twin)

    def start(self):
        self.swap().start()

    def spread(self):
        arrived(self.pair, self.r0)
        own = self.blocks[:, self.half(self.place.core)].astype(F32)
        self.chip[...] = (own + self.pair[...].astype(F32)).astype(BF16)

        @pl.loop(1, self.place.peers)
        def _(k):
            @pl.when(self.used(self.place.peer(k)[0]))
            def _():
                self.first(k).start()

    def group_sums(self):
        @pl.when(self.used(self.place.me))
        def _():
            self.got[self.place.me] = self.chip[:, self.part(self.place.me)]

            @pl.loop(1, self.place.peers)
            def _(k):
                p, _ = self.place.peer(k)
                arrived(self.got.at[p], self.r1.at[p])

            ny = self.place.ny
            running = jnp.zeros((self.share, 128), F32)
            order = [(zz * ny + y, f) for zz in range(self.place.nz) for f in range(2) for y in range(ny)]
            for p, f in reversed(order) if self.reverse else order:
                self.sums[p, f] = running
                running = running + self.got[p, f].astype(F32)
            self.total[...] = running.astype(BF16)

            @pl.loop(1, self.place.groups)
            def _(k):
                self.second(k).start()

            self.totals[self.place.group] = jnp.zeros((self.share, 128), BF16)

    def send_back(self):
        @pl.when(self.used(self.place.me))
        def _():
            @pl.loop(1, self.place.groups)
            def _(k):
                g, _ = self.place.other(k)
                arrived(self.totals.at[g], self.r2.at[g])

            group = self.place.group
            before = jnp.zeros((self.share, 128), F32)
            for g in range(self.place.groups):
                counts = g > group if self.reverse else g < group
                before = before + jnp.where(counts, self.totals[g].astype(F32), 0.0)
            for p in range(self.place.peers):
                self.answer[p] = (self.sums[p] + before[None]).astype(BF16)

            @pl.loop(1, self.place.peers)
            def _(k):
                self.third(k).start()

            self.back[:, self.part(self.place.me)] = self.answer[self.place.me]

    def pair_back(self):
        @pl.loop(1, self.place.peers)
        def _(k):
            p, _ = self.place.peer(k)

            @pl.when(self.used(p))
            def _():
                arrived(self.answer.at[p], self.r3.at[p])

        core = self.place.core
        here = self.half(core)
        before = self.back[...].astype(F32)
        own, pair = self.blocks[:, here].astype(F32), self.pair[...].astype(F32)
        after = core == (0 if self.reverse else 1)
        self.theirs[...] = (before + pair + jnp.where(after, 0.0, own)).astype(BF16)
        self.fourth().start()
        self.out[:, here] = (before + own + jnp.where(after, pair, 0.0)).astype(BF16)

    def finish(self):
        arrived(self.theirs, self.r4)

    def drain(self):
        self.swap().wait_send()
        self.fourth().wait_send()

        @pl.loop(1, self.place.peers)
        def _(k):
            @pl.when(self.used(self.place.peer(k)[0]))
            def _():
                self.first(k).wait_send()

        @pl.when(self.used(self.place.me))
        def _():
            @pl.loop(1, self.place.peers)
            def _(k):
                self.third(k).wait_send()

            @pl.loop(1, self.place.groups)
            def _(k):
                self.second(k).wait_send()


def scan_share(shape, rows):
    return -(-rows // (16 * 2 * min(4, shape[0]) * (shape[1] // 2))) * 16


def scan_scratch(shape, rows):
    ntm, nsp = shape
    nz = min(4, ntm)
    peers, groups = nz * (nsp // 2), ntm // nz
    share = scan_share(shape, rows)
    dma = pltpu.SemaphoreType.DMA
    full, half = pltpu.VMEM((2, 2 * peers * share, 128), BF16), pltpu.VMEM((2, peers * share, 128), BF16)
    shares = pltpu.VMEM((peers, 2, share, 128), BF16)
    return [
        full,
        full,
        half,
        half,
        shares,
        pltpu.VMEM((peers, 2, share, 128), F32),
        shares,
        half,
        half,
        pltpu.VMEM((groups, share, 128), BF16),
        pltpu.VMEM((share, 128), BF16),
        dma,
        dma,
        dma((peers,)),
        dma((peers,)),
        dma((groups,)),
        dma((groups,)),
        dma((peers,)),
        dma((peers,)),
        dma,
        dma,
    ]


def to_mate(place, send, recv, send_sem, recv_sem, s):
    me = place.sp
    return remote(send.at[s], recv.at[me], send_sem.at[s], recv_sem.at[me], (place.tm, s))


def give(place, send, recv, send_sem, recv_sem, targets):
    for s in targets:

        @pl.when(place.sp != s)
        def _():
            to_mate(place, send, recv, send_sem, recv_sem, s).start()

        @pl.when(place.sp == s)
        def _():
            recv[s] = send[s]


def kernel(
    shape,
    video, conv_h, embed_h, q_h, k_h, v_h, init_in, probe_h, po_h,
    flow_out, tangent_out, adj_out, cot_out,
    slab, q_w, k_w, v_w, q, qd, k, v, latent, po_send, po_recv, po, init_send, init_recv, init,
    out_send, out_recv, cot_send, cot_recv,
    halo_send, halo_recv, load, keep_sem, po_s, po_r, init_s, init_r, out_s, out_r, cot_s, cot_r,
    *scans,
):
    ntm, nsp = shape
    place = Place(ntm, nsp)
    tm, sp = place.tm, place.sp
    n = len(scans) // 4
    forward = [Scan(place, False, 5 * 2 * HD, *scans[i * n : i * n + n]) for i in range(2)]
    backward = [Scan(place, True, 5 * HD, *scans[i * n : i * n + n]) for i in range(2, 4)]

    later, earlier = tm + 1 < ntm, tm > 0
    down, up = sp + 1 < nsp, sp > 0
    last, first = pl.ds(TOK - 32, 32), pl.ds(0, 32)
    top, mid, bottom = pl.ds(0, 32), pl.ds(32, TOK), pl.ds(32 + TOK, 32)
    whole = pl.ds(0, TOK)
    prev, own = pl.ds(0, 2), pl.ds(2, 2)
    moves = (
        (down, up, last, own, top, (tm, sp + 1), (tm, sp - 1)),
        (up, down, first, own, bottom, (tm, sp - 1), (tm, sp + 1)),
        (later, earlier, whole, prev, mid, (tm + 1, sp), (tm - 1, sp)),
        (down & later, up & earlier, last, prev, top, (tm + 1, sp + 1), (tm - 1, sp - 1)),
        (up & later, down & earlier, first, prev, bottom, (tm + 1, sp - 1), (tm - 1, sp + 1)),
    )

    barrier = pltpu.get_barrier_semaphore()
    for _, may_recv, _, _, _, _, source in moves:

        @pl.when(may_recv)
        def _():
            pl.semaphore_signal(barrier, inc=1, device_id=source, device_id_type=MESH)

    def greet(count, device_of):
        @pl.loop(1, count)
        def _(i):
            pl.semaphore_signal(barrier, inc=1, device_id=device_of(i)[1], device_id_type=MESH)

    greet(place.groups, place.other)
    greet(place.peers, place.peer)
    greet(nsp, place.mate)

    def encode(conv_w, embed_w, probe, po_i, taps, acc, kd, vd):
        loads = [
            pltpu.make_async_copy(src, dst, load.at[i])
            for i, (src, dst) in enumerate(
                (
                    (po_h, po_i),
                    (probe_h, probe),
                    (k_h, k_w),
                    (v_h, v_w),
                    (conv_h, conv_w),
                    (q_h, q_w),
                    (embed_h, embed_w),
                )
            )
        ]
        keep = pltpu.make_async_copy(video, slab.at[own, mid], keep_sem)
        keep.start()
        for one in loads:
            one.start()

        for _, may_recv, _, frames, there, _, _ in moves:

            @pl.when(jnp.logical_not(may_recv))
            def _():
                slab[frames, there] = jnp.zeros((2, there.size, C), BF16)

        heads = [init_in[j] for j in range(4)]
        init_send[...] = jnp.concatenate(heads + [jnp.zeros((HD, 96), F32)], 1)
        for scan in forward:
            at = 5 * 2 * HD
            scan.blocks[:, at:, :] = jnp.zeros((2, scan.blocks.shape[1] - at, 128), BF16)

        greeted = place.groups + place.peers + nsp - 3
        pl.semaphore_wait(barrier, sum(m[0].astype(jnp.int32) for m in moves) + greeted)

        copies = []
        for i, (may_send, _, rows, frames, there, target, _) in enumerate(moves):
            copy = remote(video.at[:, rows], slab.at[frames, there], halo_send.at[i], halo_recv.at[i], target)
            copies.append(copy)

            @pl.when(may_send)
            def _():
                copy.start()

        loads[0].wait()
        for s in range(nsp):
            for f in range(2):
                po_send[s, f] = pack(po_i[f, TOK * s : TOK * s + TOK, :].astype(F32)).astype(BF16)
        give(place, po_send, po_recv, po_s, po_r, range(nsp))

        @pl.loop(1, nsp)
        def _(i):
            init_move(i).start()

        init_recv[sp] = init_send[...]

        col = lax.broadcasted_iota(jnp.int32, (TOK + 64, C), 0) % 32

        def build(f):
            here = slab[f].astype(F32)
            left = jnp.where(col == 0, 0.0, pltpu.roll(here, 1, 0))
            right = jnp.where(col == 31, 0.0, pltpu.roll(here, TOK + 63, 0))
            taps[f, :, 0:C] = left.astype(BF16)
            taps[f, :, C : 2 * C] = slab[f]
            taps[f, :, 2 * C : 3 * C] = right.astype(BF16)

        def halo_wait(i):
            @pl.when(moves[i][1])
            def _():
                copies[i].wait_recv()

        def convolve(a, out):
            @pl.loop(0, 3)
            def _(b):
                rows = pl.ds(pl.multiple_of(b * 32, 32), TOK)
                x = taps[a + out[0] : a + out[-1] + 1, rows, :].reshape(len(out) * TOK, 3 * C)
                here = slice(out[0] * TOK, (out[-1] + 1) * TOK)
                acc[here] += dot(x, conv_w[3 * a + b])

        acc[...] = jnp.zeros_like(acc)
        keep.wait()
        halo_wait(0)
        halo_wait(1)
        build(2)
        build(3)

        loads[1].wait()
        direction = probe[...].astype(F32).astype(BF16)
        for one, weight, out in zip(loads[2:4], (k_w, v_w), (kd, vd)):
            one.wait()
            out[...] = dot(direction, weight[...]).astype(BF16).reshape(2, TOK, D)

        loads[4].wait()
        convolve(2, (0, 1))
        convolve(1, (1,))
        loads[5].wait()
        qd[...] = dot(direction, q_w[...]).astype(BF16).reshape(2, TOK, D)
        halo_wait(2)
        halo_wait(3)
        halo_wait(4)
        build(0)
        build(1)
        convolve(1, (0,))
        convolve(0, (0, 1))

        u = acc[...]
        active = (u / (1.0 + jnp.exp(-u))).astype(BF16)
        loads[6].wait()
        latent[...] = dot(active, embed_w[...]).astype(BF16)
        for weight, out in zip((k_w, v_w), (k, v)):
            out[...] = dot(latent[...], weight[...]).astype(BF16).reshape(2, TOK, D)

        for scan, (windows, base, tiles, _) in zip(forward, PARTS):

            @pl.loop(0, 2)
            def _(f):
                st, sd = {}, {}
                over = ((0,), (0,))
                for t, heads in windows:
                    kw, vw = window(k, f, t), window(v, f, t)
                    compact_add(st, t, heads, dot(kw, vw, over))
                    both = dot(window(kd, f, t), vw, over) + dot(kw, window(vd, f, t), over)
                    compact_add(sd, t, heads, both)
                for j in range(tiles):
                    both = jnp.concatenate([st[base + j], sd[base + j]], 0)
                    scan.blocks[f, 144 * j : 144 * j + 144, :] = both.astype(BF16)

            scan.start()

        forward[0].spread()
        q[...] = dot(latent[...], q_w[...]).astype(BF16).reshape(2, TOK, D)
        for copy, (may_send, *_) in zip(copies, moves):

            @pl.when(may_send)
            def _():
                copy.wait_send()

    def init_move(i):
        _, device = place.mate(i)
        return remote(init_send, init_recv.at[sp], init_s.at[i], init_r.at[sp], device)

    pl.run_scoped(
        encode,
        pltpu.VMEM((9, 3 * C, C), BF16),
        pltpu.VMEM((C, D), BF16),
        pltpu.VMEM((2 * TOK, D), jnp.int32),
        pltpu.VMEM((2, 4 * TOK, D // 4), jnp.int32),
        pltpu.VMEM((4, TOK + 64, 3 * C), BF16),
        pltpu.VMEM((2 * TOK, C), F32),
        pltpu.VMEM((2, TOK, D), BF16),
        pltpu.VMEM((2, TOK, D), BF16),
    )

    forward[1].spread()
    forward[0].group_sums()
    forward[1].group_sums()

    @pl.loop(1, nsp)
    def _(i):
        s, _ = place.mate(i)
        arrived(po_recv.at[s], po_r.at[s])
        arrived(init_recv.at[s], init_r.at[s])

    for s in range(nsp):
        init[:, 288 * s : 288 * s + 288] = init_recv[s, :, 0:288]
        for f in range(2):
            po[f, :, 288 * s : 288 * s + 288] = unpack(po_recv[s, f].astype(F32)).astype(BF16)

    forward[0].send_back()
    forward[1].send_back()
    forward[0].pair_back()

    def mixing(bd, m_ref, md_ref, s1, s2, s3, mbar, q_bar, adj):
        def mix(i):
            windows, base, tiles, targets = PARTS[i]
            prefix, blocks = forward[i].out, backward[i].blocks
            part = slice(128 * base, 128 * (base + tiles))

            @pl.loop(0, 2)
            def _(f):
                pt, pdt = {}, {}
                for j in range(base, base + tiles):
                    both = prefix[f, 144 * (j - base) : 144 * (j - base) + 144, :].astype(F32)
                    pt[j] = both[:HD] + init[:, 128 * j : 128 * j + 128]
                    pdt[j] = both[HD:]
                for w, (t, heads) in enumerate(windows):
                    bd[w] = block_diagonal(pt, t, heads)
                    bdd = block_diagonal(pdt, t, heads)
                    qw, qdw = window(q, f, t), window(qd, f, t)
                    window_out(m_ref, t - base, dot(qw, bd[w]))
                    window_out(md_ref, t - base, dot(qdw, bd[w]) + dot(qw, bdd))
                for t, heads in windows:
                    ones = same_head(t, heads)
                    lanes = slice(128 * (t - base), 128 * (t - base) + 256)
                    m, md, p = m_ref[:, lanes], md_ref[:, lanes], window(po, f, t).astype(F32)
                    window_out(s1, t - base, dot((m * m).astype(BF16), ones))
                    window_out(s2, t - base, dot((m * md).astype(BF16), ones))
                    window_out(s3, t - base, dot((m * p).astype(BF16), ones))
                m, md, p = m_ref[...], md_ref[...], po[f, :, part].astype(F32)
                scale = lax.rsqrt(s1[...] * (1.0 / HD) + 1e-6)
                pulled = m * (scale * scale * scale) * (1.0 / HD)
                mbar[...] = (p * scale - pulled * s3[...]).astype(BF16)
                fl = m * scale
                tg = md * scale - pulled * s2[...]
                for s in targets:
                    at = 288 * s - 128 * base
                    out_send[s, 0, f] = pack(fl[:, at : at + 288]).astype(BF16)
                    out_send[s, 1, f] = pack(tg[:, at : at + 288]).astype(BF16)
                pb = {}
                for w, (t, heads) in enumerate(windows):
                    mw = mbar[:, 128 * (t - base) : 128 * (t - base) + 256]
                    window_out(s1, t - base, dot(mw, bd[w], ((1,), (1,))))
                    compact_add(pb, t, heads, dot(window(q, f, t), mw, ((0,), (0,))))
                q_bar[i, f] = s1[...].astype(BF16)
                pb = [pb[j] for j in range(base, base + tiles)]
                pb.append(jnp.zeros((blocks.shape[1] - tiles * HD, 128), F32))
                blocks[f] = jnp.concatenate(pb, 0).astype(BF16)

            backward[i].start()

        def settle(i, last):
            windows, base, tiles, targets = PARTS[i]
            sc = backward[i].out
            part = slice(128 * base, 128 * (base + tiles))

            def tiles_of(f):
                rows = sc[f].astype(F32)
                return {base + j: rows[HD * j : HD * j + HD] for j in range(tiles)}

            @pl.loop(0, 2)
            def _(f):
                state = tiles_of(f)
                for s in targets:
                    wide = jnp.concatenate([state[2 * s + j] for j in range(3)], 1)[:, 32 * s : 32 * s + 288]
                    rest = [wide[24 * j : 24 * j + 24, 256:] for j in range(3)]
                    rest = jnp.concatenate(rest + [jnp.zeros((24, 32), F32)], 1)
                    parts = [wide[:, :128], wide[:, 128:256], rest, jnp.zeros((8, 128), F32)]
                    cot_send[s, f] = jnp.concatenate(parts, 0).astype(BF16)

            give(place, cot_send, cot_recv, cot_s, cot_r, targets)

            @pl.loop(0, 2)
            def _(f):
                state = tiles_of(f)
                for t, heads in windows:
                    b = block_diagonal(state, t, heads)
                    window_out(s1, t - base, dot(window(v, f, t), b, ((1,), (1,))))
                    window_out(s2, t - base, dot(window(k, f, t), b))
                total = adj[f] + dot(s1[...].astype(BF16), k_w[:, part], ((1,), (1,)))
                total = total + dot(s2[...].astype(BF16), v_w[:, part], ((1,), (1,)))
                if last:
                    adj_out[f] = total.astype(BF16)
                else:
                    adj[f] = total

        forward[0].finish()
        mix(0)
        forward[1].pair_back()
        backward[0].spread()
        give(place, out_send, out_recv, out_s, out_r, PARTS[0][3])
        forward[1].finish()
        mix(1)
        backward[0].group_sums()
        backward[1].spread()
        give(place, out_send, out_recv, out_s, out_r, PARTS[1][3])

        @pl.loop(0, 2)
        def _(f):
            total = None
            for i, (_, base, tiles, _) in enumerate(PARTS):
                part = slice(128 * base, 128 * (base + tiles))
                piece = dot(q_bar[i, f], q_w[:, part], ((1,), (1,)))
                total = piece if total is None else total + piece
            adj[f] = total

        backward[1].group_sums()
        backward[0].send_back()
        backward[1].send_back()
        backward[0].pair_back()
        backward[0].finish()
        backward[1].pair_back()
        settle(0, False)
        backward[1].finish()
        settle(1, True)

    wide = pltpu.VMEM((TOK, 640), F32)
    pl.run_scoped(
        mixing,
        pltpu.VMEM((4, 256, 256), BF16),
        wide,
        wide,
        wide,
        wide,
        wide,
        pltpu.VMEM((TOK, 640), BF16),
        pltpu.VMEM((2, 2, TOK, 640), BF16),
        pltpu.VMEM((2, TOK, D), F32),
    )

    @pl.loop(1, nsp)
    def _(i):
        s, _ = place.mate(i)
        arrived(out_recv.at[s], out_r.at[s])
        arrived(cot_recv.at[s], cot_r.at[s])

    @pl.loop(0, nsp)
    def _(s):
        for f in range(2):
            flow_out[f, s] = unpack(out_recv[s, 0, f].astype(F32)).astype(BF16)
            tangent_out[f, s] = unpack(out_recv[s, 1, f].astype(F32)).astype(BF16)
            rows = cot_recv[s, f].astype(F32)
            rest = rows[2 * HD : 2 * HD + 24]
            rest = jnp.concatenate([rest[:, 32 * j : 32 * j + 32] for j in range(3)], 0)
            lanes = jnp.concatenate([rows[:HD], rows[HD : 2 * HD], rest], 1)
            for j in range(4):
                cot_out[f, s, j] = lanes[:, HD * j : HD * j + HD]

    @pl.loop(1, nsp)
    def _(i):
        s, _ = place.mate(i)
        to_mate(place, po_send, po_recv, po_s, po_r, s).wait_send()
        init_move(i).wait_send()
        to_mate(place, out_send, out_recv, out_s, out_r, s).wait_send()
        to_mate(place, cot_send, cot_recv, cot_s, cot_r, s).wait_send()

    for scan in forward + backward:
        scan.drain()


def on_device(shape, video, conv_weight, embed_weight, q_weight, k_weight, v_weight, initial_state, probe_in, probe_out):
    ntm, nsp = shape
    dma = pltpu.SemaphoreType.DMA
    heads = jax.ShapeDtypeStruct((2, nsp, TOK, D // 4), BF16)
    rows = pltpu.VMEM((2, TOK, D), BF16)
    square = pltpu.VMEM((D, D), BF16)
    packed = pltpu.VMEM((nsp, 2, PACK, 128), BF16)
    twice = pltpu.VMEM((nsp, 2, 2, PACK, 128), BF16)
    cots = pltpu.VMEM((nsp, 2, COT, 128), BF16)
    four = dma((nsp,))
    flow, tangent, adjoint, cot = pl.pallas_call(
        functools.partial(kernel, shape),
        out_shape=[
            heads,
            heads,
            jax.ShapeDtypeStruct((2, TOK, D), BF16),
            jax.ShapeDtypeStruct((2, nsp, 4, HD, HD), F32),
        ],
        in_specs=[anywhere()] * 6 + [vmem()] + [anywhere()] * 2,
        out_specs=[vmem()] * 4,
        scratch_shapes=[
            pltpu.VMEM((4, TOK + 64, C), BF16),
            square,
            square,
            square,
            rows,
            rows,
            rows,
            rows,
            pltpu.VMEM((2 * TOK, D), BF16),
            packed,
            packed,
            rows,
            pltpu.VMEM((HD, 384), F32),
            pltpu.VMEM((nsp, HD, 384), F32),
            pltpu.VMEM((HD, D), F32),
            twice,
            twice,
            cots,
            cots,
            dma((5,)),
            dma((5,)),
            dma((7,)),
            dma,
            four,
            four,
            four,
            four,
            four,
            four,
            four,
            four,
        ]
        + scan_scratch(shape, 5 * 2 * HD) * 2
        + scan_scratch(shape, 5 * HD) * 2,
        compiler_params=pltpu.CompilerParams(
            collective_id=0, has_side_effects=True, vmem_limit_bytes=VMEM_LIMIT
        ),
        name="flow_layer",
    )(
        video.reshape(2, TOK, C),
        conv_weight.reshape(9, 3 * C, C),
        embed_weight,
        q_weight,
        k_weight,
        v_weight,
        initial_state,
        probe_in.reshape(2 * TOK, D),
        probe_out.reshape(2, 4 * TOK, D // 4),
    )
    full = (2, 32, 32, D // 4)
    return (
        flow.reshape(full),
        tangent.reshape(full),
        adjoint.reshape(2, 8, 32, D),
        cot.reshape(8, 4, HD, HD),
    )


def solution(mesh):
    by_rows = P("tm", "space", None, None)
    by_heads = P("tm", None, None, "space")
    return jax.shard_map(
        functools.partial(on_device, (mesh.shape["tm"], mesh.shape["space"])),
        mesh=mesh,
        in_specs=(by_rows, P(), P(), P(), P(), P(), P("space", None, None), by_rows, by_heads),
        out_specs=(by_heads, by_heads, by_rows, by_rows),
        check_vma=False,
    )
```

```python
import functools

import jax
import jax.numpy as jnp
from jax import lax
from jax.experimental import pallas as pl
from jax.experimental.pallas import tpu as pltpu
from jax.sharding import PartitionSpec as P

MESH = pl.DeviceIdType.MESH
F32 = jnp.float32
BF16 = jnp.bfloat16
D = 1152
HEADS = 16
HD = 72
C = 384
TOK = 256
TILES = D // 128
WINDOWS = (
    (0, (0, 1, 2)),
    (1, (3, 4)),
    (2, (5, 6)),
    (3, (7,)),
    (4, (8, 9)),
    (5, (10, 11)),
    (6, (12, 13)),
    (7, (14, 15)),
)
VMEM_LIMIT = 60 * 1024 * 1024


PARTS = ((WINDOWS[:4], 0, 5, (0, 1)), (WINDOWS[4:], 4, 5, (2, 3)))
COT = 176
PACK = 2 * TOK + TOK // 4


def vmem():
    return pl.BlockSpec(memory_space=pltpu.VMEM)


def anywhere():
    return pl.BlockSpec(memory_space=pl.ANY)


def dot(a, b, dims=((1,), (0,))):
    return lax.dot_general(a, b, (dims, ((), ())), preferred_element_type=F32)


def head_mask(h, tile, rows):
    lane = lax.broadcasted_iota(jnp.int32, (rows, 128), 1) + 128 * tile
    return (lane >= HD * h) & (lane < HD * (h + 1))


def compact_add(tiles, t, heads, g):
    for half in range(2):
        j = t + half
        for h in heads:
            if HD * h < 128 * (j + 1) and HD * (h + 1) > 128 * j:
                r = HD * h - 128 * t
                piece = g[r : r + HD, 128 * half : 128 * half + 128]
                piece = jnp.where(head_mask(h, j, HD), piece, 0.0)
                tiles[j] = tiles[j] + piece if j in tiles else piece


def block_diagonal(tiles, t, heads):
    halves = []
    for half in range(2):
        j = t + half
        parts = []
        at = 0
        for h in heads:
            r = HD * h - 128 * t
            if r > at:
                parts.append(jnp.zeros((r - at, 128), F32))
            if HD * h < 128 * (j + 1) and HD * (h + 1) > 128 * j:
                parts.append(jnp.where(head_mask(h, j, HD), tiles[j], 0.0))
            else:
                parts.append(jnp.zeros((HD, 128), F32))
            at = r + HD
        if at < 256:
            parts.append(jnp.zeros((256 - at, 128), F32))
        halves.append(jnp.concatenate(parts, 0))
    return jnp.concatenate(halves, 1).astype(BF16)


def same_head(t, heads):
    row = lax.broadcasted_iota(jnp.int32, (256, 256), 0) + 128 * t
    col = lax.broadcasted_iota(jnp.int32, (256, 256), 1) + 128 * t
    ok = None
    for h in heads:
        low, high = HD * h, HD * (h + 1)
        both = (row >= low) & (row < high) & (col >= low) & (col < high)
        ok = both if ok is None else ok | both
    return jnp.where(ok, 1.0, 0.0).astype(BF16)


def window_out(ref, t, value):
    if t == 0:
        ref[:, 0:256] = value
    else:
        ref[:, 128 * t : 128 * t + 128] = ref[:, 128 * t : 128 * t + 128] + value[:, :128]
        ref[:, 128 * t + 128 : 128 * t + 256] = value[:, 128:]


def pack(x):
    rest = x[:, 256:]
    rest = jnp.concatenate([rest[64 * i : 64 * i + 64] for i in range(4)], 1)
    return jnp.concatenate([x[:, :128], x[:, 128:256], rest], 0)


def unpack(x):
    rest = jnp.concatenate([x[2 * TOK :, 32 * i : 32 * i + 32] for i in range(4)], 0)
    return jnp.concatenate([x[:TOK], x[TOK : 2 * TOK], rest], 1)


def arrived(ref, sem):
    pltpu.make_async_copy(ref, ref, sem).wait()


def window(ref, f, t):
    return ref[f, :, 128 * t : 128 * t + 256]


class Place:
    def __init__(self, ntm, nsp):
        self.ntm, self.nsp = ntm, nsp
        self.nz, self.ny = min(4, ntm), nsp // 2
        self.tm, self.sp = lax.axis_index("tm"), lax.axis_index("space")
        self.peers, self.groups = self.nz * self.ny, ntm // self.nz
        self.group, self.z = self.tm // self.nz, self.tm % self.nz
        self.y, self.core = self.sp // 2, self.sp % 2
        self.me = self.z * self.ny + self.y
        self.twin = (self.tm, self.sp + 1 - 2 * self.core)

    def peer(self, k):
        p = lax.rem(self.me + k, self.peers)
        return p, (self.group * self.nz + p // self.ny, 2 * (p % self.ny) + self.core)

    def other(self, k):
        g = lax.rem(self.group + k, self.groups)
        return g, (g * self.nz + self.z, self.sp)

    def mate(self, k):
        s = lax.rem(self.sp + k, self.nsp)
        return s, (self.tm, s)


def remote(src, dst, send_sem, recv_sem, device):
    return pltpu.make_async_remote_copy(
        src_ref=src,
        dst_ref=dst,
        send_sem=send_sem,
        recv_sem=recv_sem,
        device_id=device,
        device_id_type=MESH,
    )


class Scan:
    def __init__(self, place, reverse, rows, blocks, out, pair, chip, got, sums, answer, back, theirs, totals, total,
                 s0, r0, s1, r1, s2, r2, s3, r3, s4, r4):
        self.place, self.reverse, self.rows = place, reverse, rows
        self.blocks, self.out, self.pair, self.chip, self.got = blocks, out, pair, chip, got
        self.sums, self.answer, self.back, self.theirs = sums, answer, back, theirs
        self.totals, self.total = totals, total
        self.s0, self.r0, self.s1, self.r1, self.s2, self.r2 = s0, r0, s1, r1, s2, r2
        self.s3, self.r3, self.s4, self.r4 = s3, r3, s4, r4
        self.share = got.shape[2]

    def half(self, c):
        n = self.chip.shape[1]
        return pl.ds(pl.multiple_of(c * n, n), n)

    def part(self, p):
        return pl.ds(pl.multiple_of(p * self.share, self.share), self.share)

    def used(self, p):
        return (self.place.core * self.place.peers + p) * self.share < self.rows

    def swap(self):
        return remote(
            self.blocks.at[:, self.half(1 - self.place.core)], self.pair, self.s0, self.r0, self.place.twin
        )

    def first(self, k):
        p, device = self.place.peer(k)
        me = self.place.me
        return remote(self.chip.at[:, self.part(p)], self.got.at[me], self.s1.at[p], self.r1.at[me], device)

    def second(self, k):
        g, device = self.place.other(k)
        mine = self.place.group
        return remote(self.total, self.totals.at[mine], self.s2.at[g], self.r2.at[mine], device)

    def third(self, k):
        p, device = self.place.peer(k)
        me = self.place.me
        return remote(self.answer.at[p], self.back.at[:, self.part(me)], self.s3.at[p], self.r3.at[me], device)

    def fourth(self):
        return remote(self.theirs, self.out.at[:, self.half(self.place.core)], self.s4, self.r4, self.place.twin)

    def start(self):
        self.swap().start()

    def spread(self):
        arrived(self.pair, self.r0)
        own = self.blocks[:, self.half(self.place.core)].astype(F32)
        self.chip[...] = (own + self.pair[...].astype(F32)).astype(BF16)

        @pl.loop(1, self.place.peers)
        def _(k):
            @pl.when(self.used(self.place.peer(k)[0]))
            def _():
                self.first(k).start()

    def group_sums(self):
        @pl.when(self.used(self.place.me))
        def _():
            self.got[self.place.me] = self.chip[:, self.part(self.place.me)]

            @pl.loop(1, self.place.peers)
            def _(k):
                p, _ = self.place.peer(k)
                arrived(self.got.at[p], self.r1.at[p])

            ny = self.place.ny
            running = jnp.zeros((self.share, 128), F32)
            order = [(zz * ny + y, f) for zz in range(self.place.nz) for f in range(2) for y in range(ny)]
            for p, f in reversed(order) if self.reverse else order:
                self.sums[p, f] = running
                running = running + self.got[p, f].astype(F32)
            self.total[...] = running.astype(BF16)

            @pl.loop(1, self.place.groups)
            def _(k):
                self.second(k).start()

            self.totals[self.place.group] = jnp.zeros((self.share, 128), BF16)

    def send_back(self):
        @pl.when(self.used(self.place.me))
        def _():
            @pl.loop(1, self.place.groups)
            def _(k):
                g, _ = self.place.other(k)
                arrived(self.totals.at[g], self.r2.at[g])

            group = self.place.group
            before = jnp.zeros((self.share, 128), F32)
            for g in range(self.place.groups):
                counts = g > group if self.reverse else g < group
                before = before + jnp.where(counts, self.totals[g].astype(F32), 0.0)
            for p in range(self.place.peers):
                self.answer[p] = (self.sums[p] + before[None]).astype(BF16)

            @pl.loop(1, self.place.peers)
            def _(k):
                self.third(k).start()

            self.back[:, self.part(self.place.me)] = self.answer[self.place.me]

    def pair_back(self):
        @pl.loop(1, self.place.peers)
        def _(k):
            p, _ = self.place.peer(k)

            @pl.when(self.used(p))
            def _():
                arrived(self.answer.at[p], self.r3.at[p])

        core = self.place.core
        here = self.half(core)
        before = self.back[...].astype(F32)
        own, pair = self.blocks[:, here].astype(F32), self.pair[...].astype(F32)
        after = core == (0 if self.reverse else 1)
        self.theirs[...] = (before + pair + jnp.where(after, 0.0, own)).astype(BF16)
        self.fourth().start()
        self.out[:, here] = (before + own + jnp.where(after, pair, 0.0)).astype(BF16)

    def finish(self):
        arrived(self.theirs, self.r4)

    def drain(self):
        self.swap().wait_send()
        self.fourth().wait_send()

        @pl.loop(1, self.place.peers)
        def _(k):
            @pl.when(self.used(self.place.peer(k)[0]))
            def _():
                self.first(k).wait_send()

        @pl.when(self.used(self.place.me))
        def _():
            @pl.loop(1, self.place.peers)
            def _(k):
                self.third(k).wait_send()

            @pl.loop(1, self.place.groups)
            def _(k):
                self.second(k).wait_send()


def scan_share(shape, rows):
    return -(-rows // (16 * 2 * min(4, shape[0]) * (shape[1] // 2))) * 16


def scan_scratch(shape, rows):
    ntm, nsp = shape
    nz = min(4, ntm)
    peers, groups = nz * (nsp // 2), ntm // nz
    share = scan_share(shape, rows)
    dma = pltpu.SemaphoreType.DMA
    full, half = pltpu.VMEM((2, 2 * peers * share, 128), BF16), pltpu.VMEM((2, peers * share, 128), BF16)
    shares = pltpu.VMEM((peers, 2, share, 128), BF16)
    return [
        full,
        full,
        half,
        half,
        shares,
        pltpu.VMEM((peers, 2, share, 128), F32),
        shares,
        half,
        half,
        pltpu.VMEM((groups, share, 128), BF16),
        pltpu.VMEM((share, 128), BF16),
        dma,
        dma,
        dma((peers,)),
        dma((peers,)),
        dma((groups,)),
        dma((groups,)),
        dma((peers,)),
        dma((peers,)),
        dma,
        dma,
    ]


def to_mate(place, send, recv, send_sem, recv_sem, s):
    me = place.sp
    return remote(send.at[s], recv.at[me], send_sem.at[s], recv_sem.at[me], (place.tm, s))


def give(place, send, recv, send_sem, recv_sem, targets):
    for s in targets:

        @pl.when(place.sp != s)
        def _():
            to_mate(place, send, recv, send_sem, recv_sem, s).start()

        @pl.when(place.sp == s)
        def _():
            recv[s] = send[s]


def piece(place, send, recv, send_sem, recv_sem, s, *at):
    me = (place.sp, *at)
    there = (s, *at)
    return remote(send.at[there], recv.at[me], send_sem.at[there], recv_sem.at[me], (place.tm, s))


def give_piece(place, send, recv, send_sem, recv_sem, s, *at):
    @pl.when(place.sp != s)
    def _():
        piece(place, send, recv, send_sem, recv_sem, s, *at).start()

    @pl.when(place.sp == s)
    def _():
        there = (s, *at)
        pltpu.make_async_copy(send.at[there], recv.at[there], recv_sem.at[there]).start()


def kernel(
    shape,
    video, conv_h, embed_h, q_h, k_h, v_h, init_in, probe_h, po_h,
    out_recv, pre_recv, cot_recv, adj_out,
    slab, q_w, k_w, v_w, q, qd, k, v, latent, po_send, po_recv, po, init_send, init_recv, init,
    out_send, cot_send, adj_send,
    halo_send, halo_recv, load, keep_sem, po_s, po_r, init_s, init_r, out_s, out_r, cot_s, cot_r, adj_s, pre_s, pre_r,
    *scans,
):
    ntm, nsp = shape
    place = Place(ntm, nsp)
    tm, sp = place.tm, place.sp
    n = len(scans) // 4
    forward = [Scan(place, False, 5 * 2 * HD, *scans[i * n : i * n + n]) for i in range(2)]
    backward = [Scan(place, True, 5 * HD, *scans[i * n : i * n + n]) for i in range(2, 4)]

    later, earlier = tm + 1 < ntm, tm > 0
    down, up = sp + 1 < nsp, sp > 0
    last, first = pl.ds(TOK - 32, 32), pl.ds(0, 32)
    top, mid, bottom = pl.ds(0, 32), pl.ds(32, TOK), pl.ds(32 + TOK, 32)
    whole = pl.ds(0, TOK)
    prev, own = pl.ds(0, 2), pl.ds(2, 2)
    moves = (
        (down, up, last, own, top, (tm, sp + 1), (tm, sp - 1)),
        (up, down, first, own, bottom, (tm, sp - 1), (tm, sp + 1)),
        (later, earlier, whole, prev, mid, (tm + 1, sp), (tm - 1, sp)),
        (down & later, up & earlier, last, prev, top, (tm + 1, sp + 1), (tm - 1, sp - 1)),
        (up & later, down & earlier, first, prev, bottom, (tm + 1, sp - 1), (tm - 1, sp + 1)),
    )

    barrier = pltpu.get_barrier_semaphore()
    for _, may_recv, _, _, _, _, source in moves:

        @pl.when(may_recv)
        def _():
            pl.semaphore_signal(barrier, inc=1, device_id=source, device_id_type=MESH)

    def greet(count, device_of):
        @pl.loop(1, count)
        def _(i):
            pl.semaphore_signal(barrier, inc=1, device_id=device_of(i)[1], device_id_type=MESH)

    greet(place.groups, place.other)
    greet(place.peers, place.peer)
    greet(nsp, place.mate)

    def encode(conv_w, embed_w, probe, po_i, taps, acc, kd, vd):
        loads = [
            pltpu.make_async_copy(src, dst, load.at[i])
            for i, (src, dst) in enumerate(
                (
                    (po_h, po_i),
                    (probe_h, probe),
                    (k_h, k_w),
                    (v_h, v_w),
                    (conv_h, conv_w),
                    (q_h, q_w),
                    (embed_h, embed_w),
                )
            )
        ]
        keep = pltpu.make_async_copy(video, slab.at[own, mid], keep_sem)
        keep.start()
        for one in loads:
            one.start()

        for _, may_recv, _, frames, there, _, _ in moves:

            @pl.when(jnp.logical_not(may_recv))
            def _():
                slab[frames, there] = jnp.zeros((2, there.size, C), BF16)

        heads = [init_in[j] for j in range(4)]
        init_send[...] = jnp.concatenate(heads + [jnp.zeros((HD, 96), F32)], 1)
        for scan in forward:
            at = 5 * 2 * HD
            scan.blocks[:, at:, :] = jnp.zeros((2, scan.blocks.shape[1] - at, 128), BF16)

        greeted = place.groups + place.peers + nsp - 3
        pl.semaphore_wait(barrier, sum(m[0].astype(jnp.int32) for m in moves) + greeted)

        copies = []
        for i, (may_send, _, rows, frames, there, target, _) in enumerate(moves):
            copy = remote(video.at[:, rows], slab.at[frames, there], halo_send.at[i], halo_recv.at[i], target)
            copies.append(copy)

            @pl.when(may_send)
            def _():
                copy.start()

        loads[0].wait()
        for s in range(nsp):
            for f in range(2):
                po_send[s, f] = pack(po_i[f, TOK * s : TOK * s + TOK, :].astype(F32)).astype(BF16)

        col = lax.broadcasted_iota(jnp.int32, (TOK + 64, C), 0) % 32

        def build(f):
            here = slab[f].astype(F32)
            left = jnp.where(col == 0, 0.0, pltpu.roll(here, 1, 0))
            right = jnp.where(col == 31, 0.0, pltpu.roll(here, TOK + 63, 0))
            taps[f, :, 0:C] = left.astype(BF16)
            taps[f, :, C : 2 * C] = slab[f]
            taps[f, :, 2 * C : 3 * C] = right.astype(BF16)

        def halo_wait(i):
            @pl.when(moves[i][1])
            def _():
                copies[i].wait_recv()

        def convolve(a, out):
            @pl.loop(0, 3)
            def _(b):
                rows = pl.ds(pl.multiple_of(b * 32, 32), TOK)
                x = taps[a + out[0] : a + out[-1] + 1, rows, :].reshape(len(out) * TOK, 3 * C)
                here = slice(out[0] * TOK, (out[-1] + 1) * TOK)
                acc[here] += dot(x, conv_w[3 * a + b])

        acc[...] = jnp.zeros_like(acc)
        keep.wait()
        halo_wait(0)
        halo_wait(1)
        build(2)
        build(3)

        loads[1].wait()
        direction = probe[...].astype(F32).astype(BF16)
        for one, weight, out in zip(loads[2:4], (k_w, v_w), (kd, vd)):
            one.wait()
            out[...] = dot(direction, weight[...]).astype(BF16).reshape(2, TOK, D)

        loads[4].wait()
        convolve(2, (0, 1))
        convolve(1, (1,))
        loads[5].wait()
        qd[...] = dot(direction, q_w[...]).astype(BF16).reshape(2, TOK, D)
        halo_wait(2)
        halo_wait(3)
        halo_wait(4)

        @pl.loop(1, nsp)
        def _(i):
            init_move(i).start()

        init_recv[sp] = init_send[...]
        give(place, po_send, po_recv, po_s, po_r, range(nsp))
        build(0)
        build(1)
        convolve(1, (0,))
        convolve(0, (0, 1))

        u = acc[...]
        active = (u / (1.0 + jnp.exp(-u))).astype(BF16)
        loads[6].wait()
        latent[...] = dot(active, embed_w[...]).astype(BF16)
        for weight, out in zip((k_w, v_w), (k, v)):
            out[...] = dot(latent[...], weight[...]).astype(BF16).reshape(2, TOK, D)

        for scan, (windows, base, tiles, _) in zip(forward, PARTS):

            @pl.loop(0, 2)
            def _(f):
                st, sd = {}, {}
                over = ((0,), (0,))
                for t, heads in windows:
                    kw, vw = window(k, f, t), window(v, f, t)
                    compact_add(st, t, heads, dot(kw, vw, over))
                    both = dot(window(kd, f, t), vw, over) + dot(kw, window(vd, f, t), over)
                    compact_add(sd, t, heads, both)
                for j in range(tiles):
                    both = jnp.concatenate([st[base + j], sd[base + j]], 0)
                    scan.blocks[f, 144 * j : 144 * j + 144, :] = both.astype(BF16)

            scan.start()

        forward[0].spread()
        q[...] = dot(latent[...], q_w[...]).astype(BF16).reshape(2, TOK, D)
        packed(0, q)
        for copy, (may_send, *_) in zip(copies, moves):

            @pl.when(may_send)
            def _():
                copy.wait_send()

    def packed(x, rows):
        @pl.loop(0, 2)
        def _(f):
            for s in range(nsp):
                out_send[s, x, f] = pack(rows[f, :, 288 * s : 288 * s + 288].astype(F32)).astype(BF16)

    def leave(x, f):
        for s in range(nsp):
            give_piece(place, out_send, out_recv, out_s, out_r, s, x, f)

    def prefix_piece(s):
        i = s // 2
        at = 144 * (2 * s - PARTS[i][1])
        return forward[i].out.at[:, at : at + 432]

    def prefix_move(s):
        return remote(prefix_piece(s), pre_recv.at[sp], pre_s.at[s], pre_r.at[sp], (tm, s))

    def prefixes(i):
        for s in PARTS[i][3]:

            @pl.when(sp != s)
            def _():
                prefix_move(s).start()

            @pl.when(sp == s)
            def _():
                pltpu.make_async_copy(prefix_piece(s), pre_recv.at[s], pre_r.at[s]).start()

    def init_move(i):
        _, device = place.mate(i)
        return remote(init_send, init_recv.at[sp], init_s.at[i], init_r.at[sp], device)

    pl.run_scoped(
        encode,
        pltpu.VMEM((9, 3 * C, C), BF16),
        pltpu.VMEM((C, D), BF16),
        pltpu.VMEM((2 * TOK, D), jnp.int32),
        pltpu.VMEM((2, 4 * TOK, D // 4), jnp.int32),
        pltpu.VMEM((4, TOK + 64, 3 * C), BF16),
        pltpu.VMEM((2 * TOK, C), F32),
        pltpu.VMEM((2, TOK, D), BF16),
        pltpu.VMEM((2, TOK, D), BF16),
    )

    forward[1].spread()
    forward[0].group_sums()
    forward[1].group_sums()
    packed(1, qd)
    leave(1, 0)

    @pl.loop(1, nsp)
    def _(i):
        s, _ = place.mate(i)
        arrived(po_recv.at[s], po_r.at[s])
        arrived(init_recv.at[s], init_r.at[s])

    for s in range(nsp):
        init[:, 288 * s : 288 * s + 288] = init_recv[s, :, 0:288]
        for f in range(2):
            po[f, :, 288 * s : 288 * s + 288] = unpack(po_recv[s, f].astype(F32)).astype(BF16)

    forward[0].send_back()
    forward[1].send_back()
    leave(1, 1)
    forward[0].pair_back()

    def mixing(bd, m_ref, s1, s2, s3, mbar, q_bar, adj):
        def mix(i):
            windows, base, tiles, targets = PARTS[i]
            prefix, blocks = forward[i].out, backward[i].blocks
            part = slice(128 * base, 128 * (base + tiles))

            @pl.loop(0, 2)
            def _(f):
                pt = {}
                for j in range(base, base + tiles):
                    both = prefix[f, 144 * (j - base) : 144 * (j - base) + 144, :].astype(F32)
                    pt[j] = both[:HD] + init[:, 128 * j : 128 * j + 128]
                for w, (t, heads) in enumerate(windows):
                    bd[w] = block_diagonal(pt, t, heads)
                    window_out(m_ref, t - base, dot(window(q, f, t), bd[w]))
                for t, heads in windows:
                    ones = same_head(t, heads)
                    lanes = slice(128 * (t - base), 128 * (t - base) + 256)
                    m, p = m_ref[:, lanes], window(po, f, t).astype(F32)
                    window_out(s1, t - base, dot((m * m).astype(BF16), ones))
                    window_out(s3, t - base, dot((m * p).astype(BF16), ones))
                m, p = m_ref[...], po[f, :, part].astype(F32)
                scale = lax.rsqrt(s1[...] * (1.0 / HD) + 1e-6)
                pulled = m * (scale * scale * scale) * (1.0 / HD)
                mbar[...] = (p * scale - pulled * s3[...]).astype(BF16)
                pb = {}
                for w, (t, heads) in enumerate(windows):
                    mw = mbar[:, 128 * (t - base) : 128 * (t - base) + 256]
                    window_out(s1, t - base, dot(mw, bd[w], ((1,), (1,))))
                    compact_add(pb, t, heads, dot(window(q, f, t), mw, ((0,), (0,))))
                q_bar[i, f] = s1[...].astype(BF16)
                pb = [pb[j] for j in range(base, base + tiles)]
                pb.append(jnp.zeros((blocks.shape[1] - tiles * HD, 128), F32))
                blocks[f] = jnp.concatenate(pb, 0).astype(BF16)

            backward[i].start()

        def settle(i, last):
            windows, base, tiles, targets = PARTS[i]
            sc = backward[i].out
            part = slice(128 * base, 128 * (base + tiles))

            def tiles_of(f):
                rows = sc[f].astype(F32)
                return {base + j: rows[HD * j : HD * j + HD] for j in range(tiles)}

            @pl.loop(0, 2)
            def _(f):
                state = tiles_of(f)
                for s in targets:
                    wide = jnp.concatenate([state[2 * s + j] for j in range(3)], 1)[:, 32 * s : 32 * s + 288]
                    rest = [wide[24 * j : 24 * j + 24, 256:] for j in range(3)]
                    rest = jnp.concatenate(rest + [jnp.zeros((24, 32), F32)], 1)
                    parts = [wide[:, :128], wide[:, 128:256], rest, jnp.zeros((8, 128), F32)]
                    cot_send[s, f] = jnp.concatenate(parts, 0).astype(BF16)

            for s in targets:
                give_piece(place, cot_send, cot_recv, cot_s, cot_r, s)

            @pl.loop(0, 2)
            def _(f):
                state = tiles_of(f)
                for t, heads in windows:
                    b = block_diagonal(state, t, heads)
                    window_out(s1, t - base, dot(window(v, f, t), b, ((1,), (1,))))
                    window_out(s2, t - base, dot(window(k, f, t), b))
                total = adj[f] + dot(s1[...].astype(BF16), k_w[:, part], ((1,), (1,)))
                total = total + dot(s2[...].astype(BF16), v_w[:, part], ((1,), (1,)))
                if last:
                    adj_send[f] = total.astype(BF16)
                    pltpu.make_async_copy(adj_send.at[f], adj_out.at[f], adj_s.at[f]).start()
                else:
                    adj[f] = total

        forward[0].finish()
        prefixes(0)
        mix(0)
        forward[1].pair_back()
        backward[0].spread()
        forward[1].finish()
        prefixes(1)
        mix(1)
        backward[0].group_sums()
        backward[1].spread()

        @pl.loop(0, 2)
        def _(f):
            total = None
            for i, (_, base, tiles, _) in enumerate(PARTS):
                part = slice(128 * base, 128 * (base + tiles))
                share = dot(q_bar[i, f], q_w[:, part], ((1,), (1,)))
                total = share if total is None else total + share
            adj[f] = total

        backward[1].group_sums()
        leave(0, 0)
        backward[0].send_back()
        backward[1].send_back()
        leave(0, 1)
        backward[0].pair_back()
        backward[0].finish()
        backward[1].pair_back()
        settle(0, False)
        backward[1].finish()
        settle(1, True)

    wide = pltpu.VMEM((TOK, 640), F32)
    pl.run_scoped(
        mixing,
        pltpu.VMEM((4, 256, 256), BF16),
        wide,
        wide,
        wide,
        wide,
        pltpu.VMEM((TOK, 640), BF16),
        pltpu.VMEM((2, 2, TOK, 640), BF16),
        pltpu.VMEM((2, TOK, D), F32),
    )

    @pl.loop(0, nsp)
    def _(s):
        for x in range(2):
            for f in range(2):
                arrived(out_recv.at[s, x, f], out_r.at[s, x, f])
        arrived(cot_recv.at[s], cot_r.at[s])
        arrived(pre_recv.at[s], pre_r.at[s])

    for s in range(nsp):

        @pl.when(sp != s)
        def _():
            prefix_move(s).wait_send()

    @pl.loop(1, nsp)
    def _(i):
        s, _ = place.mate(i)
        to_mate(place, po_send, po_recv, po_s, po_r, s).wait_send()
        init_move(i).wait_send()
        for x in range(2):
            for f in range(2):
                piece(place, out_send, out_recv, out_s, out_r, s, x, f).wait_send()
        piece(place, cot_send, cot_recv, cot_s, cot_r, s).wait_send()

    for f in range(2):
        pltpu.make_async_copy(adj_send.at[f], adj_out.at[f], adj_s.at[f]).wait()

    for scan in forward + backward:
        scan.drain()


OWN = ((0, (0, 1, 2)), (1, (3,)))


def flow_kernel(nsp, out_h, pre_h, cot_h, adj_h, init_in, flow_h, tangent_h, cot_out_h, adj_out_h,
                out, pre, cot, adj, flow, tangent, cots, m_ref, md_ref, s1, s2, sems, done, adj_s):
    sp = lax.axis_index("space")

    def loads(i):
        s, f = i // 2, i % 2
        return (
            pltpu.make_async_copy(out_h.at[s, :, f], out.at[i], sems.at[0, i]),
            pltpu.make_async_copy(pre_h.at[s, f], pre.at[i], sems.at[1, i]),
            pltpu.make_async_copy(cot_h.at[s, f], cot.at[i], sems.at[2, i]),
        )

    def stores(i):
        s, f = i // 2, i % 2
        return (
            pltpu.make_async_copy(flow.at[i], flow_h.at[f, s], done.at[0, i]),
            pltpu.make_async_copy(tangent.at[i], tangent_h.at[f, s], done.at[1, i]),
            pltpu.make_async_copy(cots.at[i], cot_out_h.at[f, s], done.at[2, i]),
        )

    for i in range(2 * nsp):
        for one in loads(i):
            one.start()
    take = pltpu.make_async_copy(adj_h, adj, adj_s.at[0])
    take.start()

    heads = [init_in[j] for j in range(4)]
    init = jnp.concatenate(heads + [jnp.zeros((HD, 96), F32)], 1)
    row = lax.broadcasted_iota(jnp.int32, (384, 384), 0)
    col = lax.broadcasted_iota(jnp.int32, (384, 384), 1)
    shift = jnp.where(row == col + 32 * sp, 1.0, 0.0).astype(BF16)
    ones = [same_head(t, group) for t, group in OWN]

    def queries(x):
        rest = x[2 * TOK :].astype(F32)
        rest = jnp.concatenate([rest[:, 32 * j : 32 * j + 32] for j in range(4)], 0)
        rest = jnp.concatenate([rest, jnp.zeros((TOK, 96), F32)], 1).astype(BF16)
        return jnp.concatenate([x[:TOK], x[TOK : 2 * TOK], rest], 1)

    @pl.loop(0, 2 * nsp)
    def _(i):
        for one in loads(i):
            one.wait()
        q, qd = queries(out[i, 0]), queries(out[i, 1])
        tiles = jnp.concatenate([pre[i, 144 * j : 144 * j + 144, :] for j in range(3)], 1)
        tiles = dot(tiles, shift)
        state, state_dot = tiles[:HD] + init, tiles[HD:]
        pt = {j: state[:, 128 * j : 128 * j + 128] for j in range(3)}
        pdt = {j: state_dot[:, 128 * j : 128 * j + 128] for j in range(3)}
        for t, group in OWN:
            lanes = slice(128 * t, 128 * t + 256)
            b, bd = block_diagonal(pt, t, group), block_diagonal(pdt, t, group)
            window_out(m_ref, t, dot(q[:, lanes], b))
            window_out(md_ref, t, dot(qd[:, lanes], b) + dot(q[:, lanes], bd))
        for (t, _), one in zip(OWN, ones):
            lanes = slice(128 * t, 128 * t + 256)
            m, md = m_ref[:, lanes], md_ref[:, lanes]
            window_out(s1, t, dot((m * m).astype(BF16), one))
            window_out(s2, t, dot((m * md).astype(BF16), one))
        m, md = m_ref[...], md_ref[...]
        scale = lax.rsqrt(s1[...] * (1.0 / HD) + 1e-6)
        flow[i] = (m * scale).astype(BF16)[:, :288]
        pulled = m * (scale * scale * scale) * (1.0 / HD)
        tangent[i] = (md * scale - pulled * s2[...]).astype(BF16)[:, :288]
        rows = cot[i].astype(F32)
        rest = rows[2 * HD : 2 * HD + 24]
        rest = jnp.concatenate([rest[:, 32 * j : 32 * j + 32] for j in range(3)], 0)
        lanes = jnp.concatenate([rows[:HD], rows[HD : 2 * HD], rest], 1)
        for j in range(4):
            cots[i, j] = lanes[:, HD * j : HD * j + HD]
        for one in stores(i):
            one.start()

    take.wait()
    put = pltpu.make_async_copy(adj, adj_out_h, adj_s.at[1])
    put.start()
    for i in range(2 * nsp):
        for one in stores(i):
            one.wait()
    put.wait()


def flows(nsp, out, pre, cot, adj, init):
    heads = jax.ShapeDtypeStruct((2, nsp, TOK, D // 4), BF16)
    n = 2 * nsp
    wide = pltpu.VMEM((TOK, 384), F32)
    return pl.pallas_call(
        functools.partial(flow_kernel, nsp),
        out_shape=[
            heads,
            heads,
            jax.ShapeDtypeStruct((2, nsp, 4, HD, HD), F32),
            jax.ShapeDtypeStruct(adj.shape, BF16),
        ],
        in_specs=[anywhere()] * 4 + [vmem()],
        out_specs=[anywhere()] * 4,
        scratch_shapes=[
            pltpu.VMEM((n, 2, PACK, 128), BF16),
            pltpu.VMEM((n, 432, 128), BF16),
            pltpu.VMEM((n, COT, 128), BF16),
            pltpu.VMEM(adj.shape, BF16),
            pltpu.VMEM((n, TOK, D // 4), BF16),
            pltpu.VMEM((n, TOK, D // 4), BF16),
            pltpu.VMEM((n, 4, HD, HD), F32),
            wide,
            wide,
            wide,
            wide,
            pltpu.SemaphoreType.DMA((3, n)),
            pltpu.SemaphoreType.DMA((3, n)),
            pltpu.SemaphoreType.DMA((2,)),
        ],
        compiler_params=pltpu.CompilerParams(vmem_limit_bytes=VMEM_LIMIT),
        name="flow",
    )(out, pre, cot, adj, init)


def on_device(shape, video, conv_weight, embed_weight, q_weight, k_weight, v_weight, initial_state, probe_in, probe_out):
    ntm, nsp = shape
    dma = pltpu.SemaphoreType.DMA
    rows = pltpu.VMEM((2, TOK, D), BF16)
    square = pltpu.VMEM((D, D), BF16)
    packed = pltpu.VMEM((nsp, 2, PACK, 128), BF16)
    four = dma((nsp,))
    out, pre, cot, adjoint = pl.pallas_call(
        functools.partial(kernel, shape),
        out_shape=[
            jax.ShapeDtypeStruct((nsp, 2, 2, PACK, 128), BF16),
            jax.ShapeDtypeStruct((nsp, 2, 432, 128), BF16),
            jax.ShapeDtypeStruct((nsp, 2, COT, 128), BF16),
            jax.ShapeDtypeStruct((2, TOK, D), BF16),
        ],
        in_specs=[anywhere()] * 6 + [vmem()] + [anywhere()] * 2,
        out_specs=[anywhere()] * 4,
        scratch_shapes=[
            pltpu.VMEM((4, TOK + 64, C), BF16),
            square,
            square,
            square,
            rows,
            rows,
            rows,
            rows,
            pltpu.VMEM((2 * TOK, D), BF16),
            packed,
            packed,
            rows,
            pltpu.VMEM((HD, 384), F32),
            pltpu.VMEM((nsp, HD, 384), F32),
            pltpu.VMEM((HD, D), F32),
            pltpu.VMEM((nsp, 2, 2, PACK, 128), BF16),
            pltpu.VMEM((nsp, 2, COT, 128), BF16),
            rows,
            dma((5,)),
            dma((5,)),
            dma((7,)),
            dma,
            four,
            four,
            four,
            four,
            dma((nsp, 2, 2)),
            dma((nsp, 2, 2)),
            four,
            four,
            dma((2,)),
            four,
            four,
        ]
        + scan_scratch(shape, 5 * 2 * HD) * 2
        + scan_scratch(shape, 5 * HD) * 2,
        compiler_params=pltpu.CompilerParams(
            collective_id=0, has_side_effects=True, vmem_limit_bytes=VMEM_LIMIT
        ),
        name="flow_layer",
    )(
        video.reshape(2, TOK, C),
        conv_weight.reshape(9, 3 * C, C),
        embed_weight,
        q_weight,
        k_weight,
        v_weight,
        initial_state,
        probe_in.reshape(2 * TOK, D),
        probe_out.reshape(2, 4 * TOK, D // 4),
    )
    flow, tangent, cot, adjoint = flows(nsp, out, pre, cot, adjoint, initial_state)
    full = (2, 32, 32, D // 4)
    return (
        flow.reshape(full),
        tangent.reshape(full),
        adjoint.reshape(2, 8, 32, D),
        cot.reshape(8, 4, HD, HD),
    )


def solution(mesh):
    by_rows = P("tm", "space", None, None)
    by_heads = P("tm", None, None, "space")
    return jax.shard_map(
        functools.partial(on_device, (mesh.shape["tm"], mesh.shape["space"])),
        mesh=mesh,
        in_specs=(by_rows, P(), P(), P(), P(), P(), P("space", None, None), by_rows, by_heads),
        out_specs=(by_heads, by_heads, by_rows, by_rows),
        check_vma=False,
    )
```

```python
import functools

import jax
import jax.numpy as jnp
from jax import lax
from jax.experimental import pallas as pl
from jax.experimental.pallas import tpu as pltpu
from jax.sharding import PartitionSpec as P

MESH = pl.DeviceIdType.MESH
F32 = jnp.float32
BF16 = jnp.bfloat16
D = 1152
HEADS = 16
HD = 72
C = 384
TOK = 256
TILES = D // 128
WINDOWS = (
    (0, (0, 1, 2)),
    (1, (3, 4)),
    (2, (5, 6)),
    (3, (7,)),
    (4, (8, 9)),
    (5, (10, 11)),
    (6, (12, 13)),
    (7, (14, 15)),
)
VMEM_LIMIT = 60 * 1024 * 1024


PARTS = ((WINDOWS[:4], 0, 5, (0, 1)), (WINDOWS[4:], 4, 5, (2, 3)))
COT = 176
PACK = 2 * TOK + TOK // 4


def vmem():
    return pl.BlockSpec(memory_space=pltpu.VMEM)


def anywhere():
    return pl.BlockSpec(memory_space=pl.ANY)


def dot(a, b, dims=((1,), (0,))):
    return lax.dot_general(a, b, (dims, ((), ())), preferred_element_type=F32)


def head_mask(h, tile, rows):
    lane = lax.broadcasted_iota(jnp.int32, (rows, 128), 1) + 128 * tile
    return (lane >= HD * h) & (lane < HD * (h + 1))


def compact_add(tiles, t, heads, g):
    for half in range(2):
        j = t + half
        for h in heads:
            if HD * h < 128 * (j + 1) and HD * (h + 1) > 128 * j:
                r = HD * h - 128 * t
                piece = g[r : r + HD, 128 * half : 128 * half + 128]
                piece = jnp.where(head_mask(h, j, HD), piece, 0.0)
                tiles[j] = tiles[j] + piece if j in tiles else piece


def block_diagonal(tiles, t, heads):
    halves = []
    for half in range(2):
        j = t + half
        parts = []
        at = 0
        for h in heads:
            r = HD * h - 128 * t
            if r > at:
                parts.append(jnp.zeros((r - at, 128), F32))
            if HD * h < 128 * (j + 1) and HD * (h + 1) > 128 * j:
                parts.append(jnp.where(head_mask(h, j, HD), tiles[j], 0.0))
            else:
                parts.append(jnp.zeros((HD, 128), F32))
            at = r + HD
        if at < 256:
            parts.append(jnp.zeros((256 - at, 128), F32))
        halves.append(jnp.concatenate(parts, 0))
    return jnp.concatenate(halves, 1).astype(BF16)


def same_head(t, heads):
    row = lax.broadcasted_iota(jnp.int32, (256, 256), 0) + 128 * t
    col = lax.broadcasted_iota(jnp.int32, (256, 256), 1) + 128 * t
    ok = None
    for h in heads:
        low, high = HD * h, HD * (h + 1)
        both = (row >= low) & (row < high) & (col >= low) & (col < high)
        ok = both if ok is None else ok | both
    return jnp.where(ok, 1.0, 0.0).astype(BF16)


def window_out(ref, t, value):
    if t == 0:
        ref[:, 0:256] = value
    else:
        ref[:, 128 * t : 128 * t + 128] = ref[:, 128 * t : 128 * t + 128] + value[:, :128]
        ref[:, 128 * t + 128 : 128 * t + 256] = value[:, 128:]


def pack(x):
    rest = x[:, 256:]
    rest = jnp.concatenate([rest[64 * i : 64 * i + 64] for i in range(4)], 1)
    return jnp.concatenate([x[:, :128], x[:, 128:256], rest], 0)


def unpack(x):
    rest = jnp.concatenate([x[2 * TOK :, 32 * i : 32 * i + 32] for i in range(4)], 0)
    return jnp.concatenate([x[:TOK], x[TOK : 2 * TOK], rest], 1)


def arrived(ref, sem):
    pltpu.make_async_copy(ref, ref, sem).wait()


def window(ref, f, t):
    return ref[f, :, 128 * t : 128 * t + 256]


class Place:
    def __init__(self, ntm, nsp):
        self.ntm, self.nsp = ntm, nsp
        self.nz, self.ny = min(4, ntm), nsp // 2
        self.tm, self.sp = lax.axis_index("tm"), lax.axis_index("space")
        self.peers, self.groups = self.nz * self.ny, ntm // self.nz
        self.group, self.z = self.tm // self.nz, self.tm % self.nz
        self.y, self.core = self.sp // 2, self.sp % 2
        self.me = self.z * self.ny + self.y
        self.twin = (self.tm, self.sp + 1 - 2 * self.core)

    def peer(self, k):
        p = lax.rem(self.me + k, self.peers)
        return p, (self.group * self.nz + p // self.ny, 2 * (p % self.ny) + self.core)

    def other(self, k):
        g = lax.rem(self.group + k, self.groups)
        return g, (g * self.nz + self.z, self.sp)

    def mate(self, k):
        s = lax.rem(self.sp + k, self.nsp)
        return s, (self.tm, s)


def remote(src, dst, send_sem, recv_sem, device):
    return pltpu.make_async_remote_copy(
        src_ref=src,
        dst_ref=dst,
        send_sem=send_sem,
        recv_sem=recv_sem,
        device_id=device,
        device_id_type=MESH,
    )


class Scan:
    def __init__(self, place, reverse, rows, blocks, out, pair, chip, got, sums, answer, back, theirs, totals, total,
                 s0, r0, s1, r1, s2, r2, s3, r3, s4, r4):
        self.place, self.reverse, self.rows = place, reverse, rows
        self.blocks, self.out, self.pair, self.chip, self.got = blocks, out, pair, chip, got
        self.sums, self.answer, self.back, self.theirs = sums, answer, back, theirs
        self.totals, self.total = totals, total
        self.s0, self.r0, self.s1, self.r1, self.s2, self.r2 = s0, r0, s1, r1, s2, r2
        self.s3, self.r3, self.s4, self.r4 = s3, r3, s4, r4
        self.share = got.shape[2]

    def half(self, c):
        n = self.chip.shape[1]
        return pl.ds(pl.multiple_of(c * n, n), n)

    def part(self, p):
        return pl.ds(pl.multiple_of(p * self.share, self.share), self.share)

    def used(self, p):
        return (self.place.core * self.place.peers + p) * self.share < self.rows

    def swap(self):
        return remote(
            self.blocks.at[:, self.half(1 - self.place.core)], self.pair, self.s0, self.r0, self.place.twin
        )

    def first(self, k):
        p, device = self.place.peer(k)
        me = self.place.me
        return remote(self.chip.at[:, self.part(p)], self.got.at[me], self.s1.at[p], self.r1.at[me], device)

    def second(self, k):
        g, device = self.place.other(k)
        mine = self.place.group
        return remote(self.total, self.totals.at[mine], self.s2.at[g], self.r2.at[mine], device)

    def third(self, k):
        p, device = self.place.peer(k)
        me = self.place.me
        return remote(self.answer.at[p], self.back.at[:, self.part(me)], self.s3.at[p], self.r3.at[me], device)

    def fourth(self):
        return remote(self.theirs, self.out.at[:, self.half(self.place.core)], self.s4, self.r4, self.place.twin)

    def start(self):
        self.swap().start()

    def spread(self):
        arrived(self.pair, self.r0)
        own = self.blocks[:, self.half(self.place.core)].astype(F32)
        self.chip[...] = (own + self.pair[...].astype(F32)).astype(BF16)

        @pl.loop(1, self.place.peers)
        def _(k):
            @pl.when(self.used(self.place.peer(k)[0]))
            def _():
                self.first(k).start()

    def group_sums(self):
        @pl.when(self.used(self.place.me))
        def _():
            self.got[self.place.me] = self.chip[:, self.part(self.place.me)]

            @pl.loop(1, self.place.peers)
            def _(k):
                p, _ = self.place.peer(k)
                arrived(self.got.at[p], self.r1.at[p])

            ny = self.place.ny
            running = jnp.zeros((self.share, 128), F32)
            order = [(zz * ny + y, f) for zz in range(self.place.nz) for f in range(2) for y in range(ny)]
            for p, f in reversed(order) if self.reverse else order:
                self.sums[p, f] = running
                running = running + self.got[p, f].astype(F32)
            self.total[...] = running.astype(BF16)

            @pl.loop(1, self.place.groups)
            def _(k):
                self.second(k).start()

            self.totals[self.place.group] = jnp.zeros((self.share, 128), BF16)

    def send_back(self):
        @pl.when(self.used(self.place.me))
        def _():
            @pl.loop(1, self.place.groups)
            def _(k):
                g, _ = self.place.other(k)
                arrived(self.totals.at[g], self.r2.at[g])

            group = self.place.group
            before = jnp.zeros((self.share, 128), F32)
            for g in range(self.place.groups):
                counts = g > group if self.reverse else g < group
                before = before + jnp.where(counts, self.totals[g].astype(F32), 0.0)
            for p in range(self.place.peers):
                self.answer[p] = (self.sums[p] + before[None]).astype(BF16)

            @pl.loop(1, self.place.peers)
            def _(k):
                self.third(k).start()

            self.back[:, self.part(self.place.me)] = self.answer[self.place.me]

    def pair_back(self):
        @pl.loop(1, self.place.peers)
        def _(k):
            p, _ = self.place.peer(k)

            @pl.when(self.used(p))
            def _():
                arrived(self.answer.at[p], self.r3.at[p])

        core = self.place.core
        here = self.half(core)
        before = self.back[...].astype(F32)
        own, pair = self.blocks[:, here].astype(F32), self.pair[...].astype(F32)
        after = core == (0 if self.reverse else 1)
        self.theirs[...] = (before + pair + jnp.where(after, 0.0, own)).astype(BF16)
        self.fourth().start()
        self.out[:, here] = (before + own + jnp.where(after, pair, 0.0)).astype(BF16)

    def finish(self):
        arrived(self.theirs, self.r4)

    def drain(self):
        self.swap().wait_send()
        self.fourth().wait_send()

        @pl.loop(1, self.place.peers)
        def _(k):
            @pl.when(self.used(self.place.peer(k)[0]))
            def _():
                self.first(k).wait_send()

        @pl.when(self.used(self.place.me))
        def _():
            @pl.loop(1, self.place.peers)
            def _(k):
                self.third(k).wait_send()

            @pl.loop(1, self.place.groups)
            def _(k):
                self.second(k).wait_send()


def scan_share(shape, rows):
    return -(-rows // (16 * 2 * min(4, shape[0]) * (shape[1] // 2))) * 16


def scan_scratch(shape, rows):
    ntm, nsp = shape
    nz = min(4, ntm)
    peers, groups = nz * (nsp // 2), ntm // nz
    share = scan_share(shape, rows)
    dma = pltpu.SemaphoreType.DMA
    full, half = pltpu.VMEM((2, 2 * peers * share, 128), BF16), pltpu.VMEM((2, peers * share, 128), BF16)
    shares = pltpu.VMEM((peers, 2, share, 128), BF16)
    return [
        full,
        full,
        half,
        half,
        shares,
        pltpu.VMEM((peers, 2, share, 128), F32),
        shares,
        half,
        half,
        pltpu.VMEM((groups, share, 128), BF16),
        pltpu.VMEM((share, 128), BF16),
        dma,
        dma,
        dma((peers,)),
        dma((peers,)),
        dma((groups,)),
        dma((groups,)),
        dma((peers,)),
        dma((peers,)),
        dma,
        dma,
    ]


def to_mate(place, send, recv, send_sem, recv_sem, s):
    me = place.sp
    return remote(send.at[s], recv.at[me], send_sem.at[s], recv_sem.at[me], (place.tm, s))


def give(place, send, recv, send_sem, recv_sem, targets):
    for s in targets:

        @pl.when(place.sp != s)
        def _():
            to_mate(place, send, recv, send_sem, recv_sem, s).start()

        @pl.when(place.sp == s)
        def _():
            recv[s] = send[s]


def piece(place, send, recv, send_sem, recv_sem, s, *at):
    me = (place.sp, *at)
    there = (s, *at)
    return remote(send.at[there], recv.at[me], send_sem.at[there], recv_sem.at[me], (place.tm, s))


def give_piece(place, send, recv, send_sem, recv_sem, s, *at):
    @pl.when(place.sp != s)
    def _():
        piece(place, send, recv, send_sem, recv_sem, s, *at).start()

    @pl.when(place.sp == s)
    def _():
        there = (s, *at)
        pltpu.make_async_copy(send.at[there], recv.at[there], recv_sem.at[there]).start()


def kernel(
    shape,
    video, conv_h, embed_h, q_h, k_h, v_h, init_in, probe_h, po_h,
    out_recv, cot_recv, adj_out,
    slab, q_w, k_w, v_w, q, qd, k, v, latent, po_send, po_recv, po, init_send, init_recv, init,
    out_send, cot_send, adj_send,
    halo_send, halo_recv, load, keep_sem, po_s, po_r, init_s, init_r, out_s, out_r, cot_s, cot_r, adj_s,
    *scans,
):
    ntm, nsp = shape
    place = Place(ntm, nsp)
    tm, sp = place.tm, place.sp
    n = len(scans) // 4
    forward = [Scan(place, False, 5 * 2 * HD, *scans[i * n : i * n + n]) for i in range(2)]
    backward = [Scan(place, True, 5 * HD, *scans[i * n : i * n + n]) for i in range(2, 4)]

    later, earlier = tm + 1 < ntm, tm > 0
    down, up = sp + 1 < nsp, sp > 0
    last, first = pl.ds(TOK - 32, 32), pl.ds(0, 32)
    top, mid, bottom = pl.ds(0, 32), pl.ds(32, TOK), pl.ds(32 + TOK, 32)
    whole = pl.ds(0, TOK)
    prev, own = pl.ds(0, 2), pl.ds(2, 2)
    moves = (
        (down, up, last, own, top, (tm, sp + 1), (tm, sp - 1)),
        (up, down, first, own, bottom, (tm, sp - 1), (tm, sp + 1)),
        (later, earlier, whole, prev, mid, (tm + 1, sp), (tm - 1, sp)),
        (down & later, up & earlier, last, prev, top, (tm + 1, sp + 1), (tm - 1, sp - 1)),
        (up & later, down & earlier, first, prev, bottom, (tm + 1, sp - 1), (tm - 1, sp + 1)),
    )

    barrier = pltpu.get_barrier_semaphore()
    for _, may_recv, _, _, _, _, source in moves:

        @pl.when(may_recv)
        def _():
            pl.semaphore_signal(barrier, inc=1, device_id=source, device_id_type=MESH)

    def greet(count, device_of):
        @pl.loop(1, count)
        def _(i):
            pl.semaphore_signal(barrier, inc=1, device_id=device_of(i)[1], device_id_type=MESH)

    greet(place.groups, place.other)
    greet(place.peers, place.peer)
    greet(nsp, place.mate)

    def encode(conv_w, embed_w, probe, po_i, taps, acc, kd, vd):
        loads = [
            pltpu.make_async_copy(src, dst, load.at[i])
            for i, (src, dst) in enumerate(
                (
                    (po_h, po_i),
                    (probe_h, probe),
                    (k_h, k_w),
                    (v_h, v_w),
                    (conv_h, conv_w),
                    (q_h, q_w),
                    (embed_h, embed_w),
                )
            )
        ]
        keep = pltpu.make_async_copy(video, slab.at[own, mid], keep_sem)
        keep.start()
        for one in loads:
            one.start()

        for _, may_recv, _, frames, there, _, _ in moves:

            @pl.when(jnp.logical_not(may_recv))
            def _():
                slab[frames, there] = jnp.zeros((2, there.size, C), BF16)

        heads = [init_in[j] for j in range(4)]
        init_send[...] = jnp.concatenate(heads + [jnp.zeros((HD, 96), F32)], 1)
        for scan in forward:
            at = 5 * 2 * HD
            scan.blocks[:, at:, :] = jnp.zeros((2, scan.blocks.shape[1] - at, 128), BF16)

        greeted = place.groups + place.peers + nsp - 3
        pl.semaphore_wait(barrier, sum(m[0].astype(jnp.int32) for m in moves) + greeted)

        copies = []
        for i, (may_send, _, rows, frames, there, target, _) in enumerate(moves):
            copy = remote(video.at[:, rows], slab.at[frames, there], halo_send.at[i], halo_recv.at[i], target)
            copies.append(copy)

            @pl.when(may_send)
            def _():
                copy.start()

        loads[0].wait()
        for s in range(nsp):
            for f in range(2):
                po_send[s, f] = pack(po_i[f, TOK * s : TOK * s + TOK, :].astype(F32)).astype(BF16)

        col = lax.broadcasted_iota(jnp.int32, (TOK + 64, C), 0) % 32

        def build(f):
            here = slab[f].astype(F32)
            left = jnp.where(col == 0, 0.0, pltpu.roll(here, 1, 0))
            right = jnp.where(col == 31, 0.0, pltpu.roll(here, TOK + 63, 0))
            taps[f, :, 0:C] = left.astype(BF16)
            taps[f, :, C : 2 * C] = slab[f]
            taps[f, :, 2 * C : 3 * C] = right.astype(BF16)

        def halo_wait(i):
            @pl.when(moves[i][1])
            def _():
                copies[i].wait_recv()

        def convolve(a, out):
            @pl.loop(0, 3)
            def _(b):
                rows = pl.ds(pl.multiple_of(b * 32, 32), TOK)
                x = taps[a + out[0] : a + out[-1] + 1, rows, :].reshape(len(out) * TOK, 3 * C)
                here = slice(out[0] * TOK, (out[-1] + 1) * TOK)
                acc[here] += dot(x, conv_w[3 * a + b])

        acc[...] = jnp.zeros_like(acc)
        keep.wait()
        halo_wait(0)
        halo_wait(1)
        build(2)
        build(3)

        loads[1].wait()
        direction = probe[...].astype(F32).astype(BF16)
        for one, weight, out in zip(loads[2:4], (k_w, v_w), (kd, vd)):
            one.wait()
            out[...] = dot(direction, weight[...]).astype(BF16).reshape(2, TOK, D)

        loads[4].wait()
        convolve(2, (0, 1))
        convolve(1, (1,))
        loads[5].wait()
        qd[...] = dot(direction, q_w[...]).astype(BF16).reshape(2, TOK, D)
        halo_wait(2)
        halo_wait(3)
        halo_wait(4)

        @pl.loop(1, nsp)
        def _(i):
            init_move(i).start()

        init_recv[sp] = init_send[...]
        give(place, po_send, po_recv, po_s, po_r, range(nsp))
        build(0)
        build(1)
        convolve(1, (0,))
        convolve(0, (0, 1))

        u = acc[...]
        active = (u / (1.0 + jnp.exp(-u))).astype(BF16)
        loads[6].wait()
        latent[...] = dot(active, embed_w[...]).astype(BF16)
        for weight, out in zip((k_w, v_w), (k, v)):
            out[...] = dot(latent[...], weight[...]).astype(BF16).reshape(2, TOK, D)

        for scan, (windows, base, tiles, _) in zip(forward, PARTS):

            @pl.loop(0, 2)
            def _(f):
                st, sd = {}, {}
                over = ((0,), (0,))
                for t, heads in windows:
                    kw, vw = window(k, f, t), window(v, f, t)
                    compact_add(st, t, heads, dot(kw, vw, over))
                    both = dot(window(kd, f, t), vw, over) + dot(kw, window(vd, f, t), over)
                    compact_add(sd, t, heads, both)
                for j in range(tiles):
                    both = jnp.concatenate([st[base + j], sd[base + j]], 0)
                    scan.blocks[f, 144 * j : 144 * j + 144, :] = both.astype(BF16)

            scan.start()

        forward[0].spread()
        q[...] = dot(latent[...], q_w[...]).astype(BF16).reshape(2, TOK, D)
        for copy, (may_send, *_) in zip(copies, moves):

            @pl.when(may_send)
            def _():
                copy.wait_send()

    def init_move(i):
        _, device = place.mate(i)
        return remote(init_send, init_recv.at[sp], init_s.at[i], init_r.at[sp], device)

    pl.run_scoped(
        encode,
        pltpu.VMEM((9, 3 * C, C), BF16),
        pltpu.VMEM((C, D), BF16),
        pltpu.VMEM((2 * TOK, D), jnp.int32),
        pltpu.VMEM((2, 4 * TOK, D // 4), jnp.int32),
        pltpu.VMEM((4, TOK + 64, 3 * C), BF16),
        pltpu.VMEM((2 * TOK, C), F32),
        pltpu.VMEM((2, TOK, D), BF16),
        pltpu.VMEM((2, TOK, D), BF16),
    )

    forward[1].spread()
    forward[0].group_sums()
    forward[1].group_sums()

    @pl.loop(1, nsp)
    def _(i):
        s, _ = place.mate(i)
        arrived(po_recv.at[s], po_r.at[s])
        arrived(init_recv.at[s], init_r.at[s])

    for s in range(nsp):
        init[:, 288 * s : 288 * s + 288] = init_recv[s, :, 0:288]
        for f in range(2):
            po[f, :, 288 * s : 288 * s + 288] = unpack(po_recv[s, f].astype(F32)).astype(BF16)

    forward[0].send_back()
    forward[1].send_back()
    forward[0].pair_back()

    def mixing(bd, m_ref, md_ref, s1, s2, s3, mbar, q_bar, adj):
        def leave(x, f, across):
            for s in range(nsp):
                there = place.y != s // 2

                @pl.when(there if across else jnp.logical_not(there))
                def _():
                    give_piece(place, out_send, out_recv, out_s, out_r, s, x, f)

        def mix(i, early):
            windows, base, tiles, targets = PARTS[i]
            prefix, blocks = forward[i].out, backward[i].blocks
            part = slice(128 * base, 128 * (base + tiles))

            @pl.loop(0, 2)
            def _(f):
                pt, pdt = {}, {}
                for j in range(base, base + tiles):
                    both = prefix[f, 144 * (j - base) : 144 * (j - base) + 144, :].astype(F32)
                    pt[j] = both[:HD] + init[:, 128 * j : 128 * j + 128]
                    pdt[j] = both[HD:]
                for w, (t, heads) in enumerate(windows):
                    bd[w] = block_diagonal(pt, t, heads)
                    bdd = block_diagonal(pdt, t, heads)
                    qw, qdw = window(q, f, t), window(qd, f, t)
                    window_out(m_ref, t - base, dot(qw, bd[w]))
                    window_out(md_ref, t - base, dot(qdw, bd[w]) + dot(qw, bdd))
                for t, heads in windows:
                    ones = same_head(t, heads)
                    lanes = slice(128 * (t - base), 128 * (t - base) + 256)
                    m, md, p = m_ref[:, lanes], md_ref[:, lanes], window(po, f, t).astype(F32)
                    window_out(s1, t - base, dot((m * m).astype(BF16), ones))
                    window_out(s2, t - base, dot((m * md).astype(BF16), ones))
                    window_out(s3, t - base, dot((m * p).astype(BF16), ones))
                m, md, p = m_ref[...], md_ref[...], po[f, :, part].astype(F32)
                scale = lax.rsqrt(s1[...] * (1.0 / HD) + 1e-6)
                pulled = m * (scale * scale * scale) * (1.0 / HD)
                mbar[...] = (p * scale - pulled * s3[...]).astype(BF16)
                fl = m * scale
                tg = md * scale - pulled * s2[...]
                for s in targets:
                    at = 288 * s - 128 * base
                    out_send[s, 0, f] = pack(fl[:, at : at + 288]).astype(BF16)
                    out_send[s, 1, f] = pack(tg[:, at : at + 288]).astype(BF16)
                if early:

                    @pl.when(f == 0)
                    def _():
                        leave(0, 0, True)
                        leave(1, 0, True)

                pb = {}
                for w, (t, heads) in enumerate(windows):
                    mw = mbar[:, 128 * (t - base) : 128 * (t - base) + 256]
                    window_out(s1, t - base, dot(mw, bd[w], ((1,), (1,))))
                    compact_add(pb, t, heads, dot(window(q, f, t), mw, ((0,), (0,))))
                q_bar[i, f] = s1[...].astype(BF16)
                pb = [pb[j] for j in range(base, base + tiles)]
                pb.append(jnp.zeros((blocks.shape[1] - tiles * HD, 128), F32))
                blocks[f] = jnp.concatenate(pb, 0).astype(BF16)

            backward[i].start()

        def settle(i, last):
            windows, base, tiles, targets = PARTS[i]
            sc = backward[i].out
            part = slice(128 * base, 128 * (base + tiles))

            def tiles_of(f):
                rows = sc[f].astype(F32)
                return {base + j: rows[HD * j : HD * j + HD] for j in range(tiles)}

            @pl.loop(0, 2)
            def _(f):
                state = tiles_of(f)
                for s in targets:
                    wide = jnp.concatenate([state[2 * s + j] for j in range(3)], 1)[:, 32 * s : 32 * s + 288]
                    rest = [wide[24 * j : 24 * j + 24, 256:] for j in range(3)]
                    rest = jnp.concatenate(rest + [jnp.zeros((24, 32), F32)], 1)
                    parts = [wide[:, :128], wide[:, 128:256], rest, jnp.zeros((8, 128), F32)]
                    cot_send[s, f] = jnp.concatenate(parts, 0).astype(BF16)

            for s in targets:
                give_piece(place, cot_send, cot_recv, cot_s, cot_r, s)

            @pl.loop(0, 2)
            def _(f):
                state = tiles_of(f)
                for t, heads in windows:
                    b = block_diagonal(state, t, heads)
                    window_out(s1, t - base, dot(window(v, f, t), b, ((1,), (1,))))
                    window_out(s2, t - base, dot(window(k, f, t), b))
                total = adj[f] + dot(s1[...].astype(BF16), k_w[:, part], ((1,), (1,)))
                total = total + dot(s2[...].astype(BF16), v_w[:, part], ((1,), (1,)))
                if last:
                    adj_send[f] = total.astype(BF16)
                    pltpu.make_async_copy(adj_send.at[f], adj_out.at[f], adj_s.at[f]).start()
                else:
                    adj[f] = total

        forward[0].finish()

        @pl.when(place.y == 1)
        def _():
            mix(0, True)

        forward[1].pair_back()
        forward[1].finish()

        @pl.when(place.y == 0)
        def _():
            mix(1, True)
            mix(0, False)

        @pl.when(place.y == 1)
        def _():
            mix(1, False)

        backward[0].spread()
        backward[1].spread()
        leave(0, 1, True)
        for f in range(2):
            leave(0, f, False)
            leave(1, f, False)

        @pl.loop(0, 2)
        def _(f):
            total = None
            for i, (_, base, tiles, _) in enumerate(PARTS):
                part = slice(128 * base, 128 * (base + tiles))
                share = dot(q_bar[i, f], q_w[:, part], ((1,), (1,)))
                total = share if total is None else total + share
            adj[f] = total

        backward[0].group_sums()
        backward[1].group_sums()
        backward[0].send_back()
        backward[1].send_back()
        leave(1, 1, True)
        backward[0].pair_back()
        backward[0].finish()
        backward[1].pair_back()
        settle(0, False)
        backward[1].finish()
        settle(1, True)

    wide = pltpu.VMEM((TOK, 640), F32)
    pl.run_scoped(
        mixing,
        pltpu.VMEM((4, 256, 256), BF16),
        wide,
        wide,
        wide,
        wide,
        wide,
        pltpu.VMEM((TOK, 640), BF16),
        pltpu.VMEM((2, 2, TOK, 640), BF16),
        pltpu.VMEM((2, TOK, D), F32),
    )

    @pl.loop(0, nsp)
    def _(s):
        for x in range(2):
            for f in range(2):
                arrived(out_recv.at[s, x, f], out_r.at[s, x, f])
        arrived(cot_recv.at[s], cot_r.at[s])

    @pl.loop(1, nsp)
    def _(i):
        s, _ = place.mate(i)
        to_mate(place, po_send, po_recv, po_s, po_r, s).wait_send()
        init_move(i).wait_send()
        for x in range(2):
            for f in range(2):
                piece(place, out_send, out_recv, out_s, out_r, s, x, f).wait_send()
        piece(place, cot_send, cot_recv, cot_s, cot_r, s).wait_send()

    for f in range(2):
        pltpu.make_async_copy(adj_send.at[f], adj_out.at[f], adj_s.at[f]).wait()

    for scan in forward + backward:
        scan.drain()


def unpack_kernel(nsp, out_h, cot_h, adj_h, flow_h, tangent_h, cot_out_h, adj_out_h,
                  out, cot, flow, tangent, cots, sems, done, adj_s):
    def loads(i):
        s, f = i // 2, i % 2
        return (
            pltpu.make_async_copy(out_h.at[s, :, f], out.at[i], sems.at[0, i]),
            pltpu.make_async_copy(cot_h.at[s, f], cot.at[i], sems.at[1, i]),
        )

    def stores(i):
        s, f = i // 2, i % 2
        return (
            pltpu.make_async_copy(flow.at[i], flow_h.at[f, s], done.at[0, i]),
            pltpu.make_async_copy(tangent.at[i], tangent_h.at[f, s], done.at[1, i]),
            pltpu.make_async_copy(cots.at[i], cot_out_h.at[f, s], done.at[2, i]),
        )

    for i in range(2 * nsp):
        for one in loads(i):
            one.start()
    through = pltpu.make_async_copy(adj_h, adj_out_h, adj_s)
    through.start()

    @pl.loop(0, 2 * nsp)
    def _(i):
        for one in loads(i):
            one.wait()
        for x, to in enumerate((flow, tangent)):
            to[i, :, 0:128] = out[i, x, 0:TOK]
            to[i, :, 128:256] = out[i, x, TOK : 2 * TOK]
            rest = out[i, x, 2 * TOK :]
            for j in range(4):
                to[i, 64 * j : 64 * j + 64, 256:288] = rest[:, 32 * j : 32 * j + 32]
        rows = cot[i].astype(F32)
        rest = rows[2 * HD : 2 * HD + 24]
        rest = jnp.concatenate([rest[:, 32 * j : 32 * j + 32] for j in range(3)], 0)
        lanes = jnp.concatenate([rows[:HD], rows[HD : 2 * HD], rest], 1)
        for j in range(4):
            cots[i, j] = lanes[:, HD * j : HD * j + HD]
        for one in stores(i):
            one.start()

    for i in range(2 * nsp):
        for one in stores(i):
            one.wait()
    through.wait()


def unpacked(nsp, out, cot, adj):
    heads = jax.ShapeDtypeStruct((2, nsp, TOK, D // 4), BF16)
    n = 2 * nsp
    return pl.pallas_call(
        functools.partial(unpack_kernel, nsp),
        out_shape=[
            heads,
            heads,
            jax.ShapeDtypeStruct((2, nsp, 4, HD, HD), F32),
            jax.ShapeDtypeStruct(adj.shape, BF16),
        ],
        in_specs=[anywhere()] * 3,
        out_specs=[anywhere()] * 4,
        scratch_shapes=[
            pltpu.VMEM((n, 2, PACK, 128), BF16),
            pltpu.VMEM((n, COT, 128), BF16),
            pltpu.VMEM((n, TOK, D // 4), BF16),
            pltpu.VMEM((n, TOK, D // 4), BF16),
            pltpu.VMEM((n, 4, HD, HD), F32),
            pltpu.SemaphoreType.DMA((2, n)),
            pltpu.SemaphoreType.DMA((3, n)),
            pltpu.SemaphoreType.DMA,
        ],
        compiler_params=pltpu.CompilerParams(vmem_limit_bytes=VMEM_LIMIT),
        name="unpack",
    )(out, cot, adj)


def on_device(shape, video, conv_weight, embed_weight, q_weight, k_weight, v_weight, initial_state, probe_in, probe_out):
    ntm, nsp = shape
    dma = pltpu.SemaphoreType.DMA
    rows = pltpu.VMEM((2, TOK, D), BF16)
    square = pltpu.VMEM((D, D), BF16)
    packed = pltpu.VMEM((nsp, 2, PACK, 128), BF16)
    four = dma((nsp,))
    out, cot, adjoint = pl.pallas_call(
        functools.partial(kernel, shape),
        out_shape=[
            jax.ShapeDtypeStruct((nsp, 2, 2, PACK, 128), BF16),
            jax.ShapeDtypeStruct((nsp, 2, COT, 128), BF16),
            jax.ShapeDtypeStruct((2, TOK, D), BF16),
        ],
        in_specs=[anywhere()] * 6 + [vmem()] + [anywhere()] * 2,
        out_specs=[anywhere()] * 3,
        scratch_shapes=[
            pltpu.VMEM((4, TOK + 64, C), BF16),
            square,
            square,
            square,
            rows,
            rows,
            rows,
            rows,
            pltpu.VMEM((2 * TOK, D), BF16),
            packed,
            packed,
            rows,
            pltpu.VMEM((HD, 384), F32),
            pltpu.VMEM((nsp, HD, 384), F32),
            pltpu.VMEM((HD, D), F32),
            pltpu.VMEM((nsp, 2, 2, PACK, 128), BF16),
            pltpu.VMEM((nsp, 2, COT, 128), BF16),
            rows,
            dma((5,)),
            dma((5,)),
            dma((7,)),
            dma,
            four,
            four,
            four,
            four,
            dma((nsp, 2, 2)),
            dma((nsp, 2, 2)),
            four,
            four,
            dma((2,)),
        ]
        + scan_scratch(shape, 5 * 2 * HD) * 2
        + scan_scratch(shape, 5 * HD) * 2,
        compiler_params=pltpu.CompilerParams(
            collective_id=0, has_side_effects=True, vmem_limit_bytes=VMEM_LIMIT
        ),
        name="flow_layer",
    )(
        video.reshape(2, TOK, C),
        conv_weight.reshape(9, 3 * C, C),
        embed_weight,
        q_weight,
        k_weight,
        v_weight,
        initial_state,
        probe_in.reshape(2 * TOK, D),
        probe_out.reshape(2, 4 * TOK, D // 4),
    )
    flow, tangent, cot, adjoint = unpacked(nsp, out, cot, adjoint)
    full = (2, 32, 32, D // 4)
    return (
        flow.reshape(full),
        tangent.reshape(full),
        adjoint.reshape(2, 8, 32, D),
        cot.reshape(8, 4, HD, HD),
    )


def solution(mesh):
    by_rows = P("tm", "space", None, None)
    by_heads = P("tm", None, None, "space")
    return jax.shard_map(
        functools.partial(on_device, (mesh.shape["tm"], mesh.shape["space"])),
        mesh=mesh,
        in_specs=(by_rows, P(), P(), P(), P(), P(), P("space", None, None), by_rows, by_heads),
        out_specs=(by_heads, by_heads, by_rows, by_rows),
        check_vma=False,
    )
```

```python
import functools

import jax
import jax.numpy as jnp
from jax import lax
from jax.experimental import pallas as pl
from jax.experimental.pallas import tpu as pltpu
from jax.sharding import PartitionSpec as P

MESH = pl.DeviceIdType.MESH
F32 = jnp.float32
BF16 = jnp.bfloat16
D = 1152
HEADS = 16
HD = 72
C = 384
TOK = 256
TILES = D // 128
WINDOWS = (
    (0, (0, 1, 2)),
    (1, (3, 4)),
    (2, (5, 6)),
    (3, (7,)),
    (4, (8, 9)),
    (5, (10, 11)),
    (6, (12, 13)),
    (7, (14, 15)),
)
VMEM_LIMIT = 60 * 1024 * 1024


PARTS = ((WINDOWS[:4], 0, 5, (0, 1)), (WINDOWS[4:], 4, 5, (2, 3)))
COT = 176
PACK = 2 * TOK + TOK // 4


def vmem():
    return pl.BlockSpec(memory_space=pltpu.VMEM)


def anywhere():
    return pl.BlockSpec(memory_space=pl.ANY)


def dot(a, b, dims=((1,), (0,))):
    return lax.dot_general(a, b, (dims, ((), ())), preferred_element_type=F32)


def head_mask(h, tile, rows):
    lane = lax.broadcasted_iota(jnp.int32, (rows, 128), 1) + 128 * tile
    return (lane >= HD * h) & (lane < HD * (h + 1))


def compact_add(tiles, t, heads, g):
    for half in range(2):
        j = t + half
        for h in heads:
            if HD * h < 128 * (j + 1) and HD * (h + 1) > 128 * j:
                r = HD * h - 128 * t
                piece = g[r : r + HD, 128 * half : 128 * half + 128]
                piece = jnp.where(head_mask(h, j, HD), piece, 0.0)
                tiles[j] = tiles[j] + piece if j in tiles else piece


def block_diagonal(tiles, t, heads):
    halves = []
    for half in range(2):
        j = t + half
        parts = []
        at = 0
        for h in heads:
            r = HD * h - 128 * t
            if r > at:
                parts.append(jnp.zeros((r - at, 128), F32))
            if HD * h < 128 * (j + 1) and HD * (h + 1) > 128 * j:
                parts.append(jnp.where(head_mask(h, j, HD), tiles[j], 0.0))
            else:
                parts.append(jnp.zeros((HD, 128), F32))
            at = r + HD
        if at < 256:
            parts.append(jnp.zeros((256 - at, 128), F32))
        halves.append(jnp.concatenate(parts, 0))
    return jnp.concatenate(halves, 1).astype(BF16)


def same_head(t, heads):
    row = lax.broadcasted_iota(jnp.int32, (256, 256), 0) + 128 * t
    col = lax.broadcasted_iota(jnp.int32, (256, 256), 1) + 128 * t
    ok = None
    for h in heads:
        low, high = HD * h, HD * (h + 1)
        both = (row >= low) & (row < high) & (col >= low) & (col < high)
        ok = both if ok is None else ok | both
    return jnp.where(ok, 1.0, 0.0).astype(BF16)


def window_out(ref, t, value):
    if t == 0:
        ref[:, 0:256] = value
    else:
        ref[:, 128 * t : 128 * t + 128] = ref[:, 128 * t : 128 * t + 128] + value[:, :128]
        ref[:, 128 * t + 128 : 128 * t + 256] = value[:, 128:]


def pack(x):
    rest = x[:, 256:]
    rest = jnp.concatenate([rest[64 * i : 64 * i + 64] for i in range(4)], 1)
    return jnp.concatenate([x[:, :128], x[:, 128:256], rest], 0)


def unpack(x):
    rest = jnp.concatenate([x[2 * TOK :, 32 * i : 32 * i + 32] for i in range(4)], 0)
    return jnp.concatenate([x[:TOK], x[TOK : 2 * TOK], rest], 1)


def arrived(ref, sem):
    pltpu.make_async_copy(ref, ref, sem).wait()


def window(ref, f, t):
    return ref[f, :, 128 * t : 128 * t + 256]


class Place:
    def __init__(self, ntm, nsp):
        self.ntm, self.nsp = ntm, nsp
        self.nz, self.ny = min(4, ntm), nsp // 2
        self.tm, self.sp = lax.axis_index("tm"), lax.axis_index("space")
        self.peers, self.groups = self.nz * self.ny, ntm // self.nz
        self.group, self.z = self.tm // self.nz, self.tm % self.nz
        self.y, self.core = self.sp // 2, self.sp % 2
        self.me = self.z * self.ny + self.y
        self.twin = (self.tm, self.sp + 1 - 2 * self.core)

    def peer(self, k):
        p = lax.rem(self.me + k, self.peers)
        return p, (self.group * self.nz + p // self.ny, 2 * (p % self.ny) + self.core)

    def other(self, k):
        g = lax.rem(self.group + k, self.groups)
        return g, (g * self.nz + self.z, self.sp)

    def mate(self, k):
        s = lax.rem(self.sp + k, self.nsp)
        return s, (self.tm, s)


def remote(src, dst, send_sem, recv_sem, device):
    return pltpu.make_async_remote_copy(
        src_ref=src,
        dst_ref=dst,
        send_sem=send_sem,
        recv_sem=recv_sem,
        device_id=device,
        device_id_type=MESH,
    )


class Scan:
    def __init__(self, place, reverse, rows, blocks, out, pair, chip, got, sums, answer, back, theirs, totals, total,
                 s0, r0, s1, r1, s2, r2, s3, r3, s4, r4):
        self.place, self.reverse, self.rows = place, reverse, rows
        self.blocks, self.out, self.pair, self.chip, self.got = blocks, out, pair, chip, got
        self.sums, self.answer, self.back, self.theirs = sums, answer, back, theirs
        self.totals, self.total = totals, total
        self.s0, self.r0, self.s1, self.r1, self.s2, self.r2 = s0, r0, s1, r1, s2, r2
        self.s3, self.r3, self.s4, self.r4 = s3, r3, s4, r4
        self.share = got.shape[2]

    def half(self, c):
        n = self.chip.shape[1]
        return pl.ds(pl.multiple_of(c * n, n), n)

    def part(self, p):
        return pl.ds(pl.multiple_of(p * self.share, self.share), self.share)

    def used(self, p):
        return (self.place.core * self.place.peers + p) * self.share < self.rows

    def swap(self):
        return remote(
            self.blocks.at[:, self.half(1 - self.place.core)], self.pair, self.s0, self.r0, self.place.twin
        )

    def first(self, k):
        p, device = self.place.peer(k)
        me = self.place.me
        return remote(self.chip.at[:, self.part(p)], self.got.at[me], self.s1.at[p], self.r1.at[me], device)

    def second(self, k):
        g, device = self.place.other(k)
        mine = self.place.group
        return remote(self.total, self.totals.at[mine], self.s2.at[g], self.r2.at[mine], device)

    def third(self, k):
        p, device = self.place.peer(k)
        me = self.place.me
        return remote(self.answer.at[p], self.back.at[:, self.part(me)], self.s3.at[p], self.r3.at[me], device)

    def fourth(self):
        return remote(self.theirs, self.out.at[:, self.half(self.place.core)], self.s4, self.r4, self.place.twin)

    def start(self):
        self.swap().start()

    def spread(self):
        arrived(self.pair, self.r0)
        own = self.blocks[:, self.half(self.place.core)].astype(F32)
        self.chip[...] = (own + self.pair[...].astype(F32)).astype(BF16)

        @pl.loop(1, self.place.peers)
        def _(k):
            @pl.when(self.used(self.place.peer(k)[0]))
            def _():
                self.first(k).start()

    def group_sums(self):
        @pl.when(self.used(self.place.me))
        def _():
            self.got[self.place.me] = self.chip[:, self.part(self.place.me)]

            @pl.loop(1, self.place.peers)
            def _(k):
                p, _ = self.place.peer(k)
                arrived(self.got.at[p], self.r1.at[p])

            ny = self.place.ny
            running = jnp.zeros((self.share, 128), F32)
            order = [(zz * ny + y, f) for zz in range(self.place.nz) for f in range(2) for y in range(ny)]
            for p, f in reversed(order) if self.reverse else order:
                self.sums[p, f] = running
                running = running + self.got[p, f].astype(F32)
            self.total[...] = running.astype(BF16)

            @pl.loop(1, self.place.groups)
            def _(k):
                self.second(k).start()

            self.totals[self.place.group] = jnp.zeros((self.share, 128), BF16)

    def send_back(self):
        @pl.when(self.used(self.place.me))
        def _():
            @pl.loop(1, self.place.groups)
            def _(k):
                g, _ = self.place.other(k)
                arrived(self.totals.at[g], self.r2.at[g])

            group = self.place.group
            before = jnp.zeros((self.share, 128), F32)
            for g in range(self.place.groups):
                counts = g > group if self.reverse else g < group
                before = before + jnp.where(counts, self.totals[g].astype(F32), 0.0)
            for p in range(self.place.peers):
                self.answer[p] = (self.sums[p] + before[None]).astype(BF16)

            @pl.loop(1, self.place.peers)
            def _(k):
                self.third(k).start()

            self.back[:, self.part(self.place.me)] = self.answer[self.place.me]

    def pair_back(self):
        @pl.loop(1, self.place.peers)
        def _(k):
            p, _ = self.place.peer(k)

            @pl.when(self.used(p))
            def _():
                arrived(self.answer.at[p], self.r3.at[p])

        core = self.place.core
        here = self.half(core)
        before = self.back[...].astype(F32)
        own, pair = self.blocks[:, here].astype(F32), self.pair[...].astype(F32)
        after = core == (0 if self.reverse else 1)
        self.theirs[...] = (before + pair + jnp.where(after, 0.0, own)).astype(BF16)
        self.fourth().start()
        self.out[:, here] = (before + own + jnp.where(after, pair, 0.0)).astype(BF16)

    def finish(self):
        arrived(self.theirs, self.r4)

    def drain(self):
        self.swap().wait_send()
        self.fourth().wait_send()

        @pl.loop(1, self.place.peers)
        def _(k):
            @pl.when(self.used(self.place.peer(k)[0]))
            def _():
                self.first(k).wait_send()

        @pl.when(self.used(self.place.me))
        def _():
            @pl.loop(1, self.place.peers)
            def _(k):
                self.third(k).wait_send()

            @pl.loop(1, self.place.groups)
            def _(k):
                self.second(k).wait_send()


def scan_share(shape, rows):
    return -(-rows // (16 * 2 * min(4, shape[0]) * (shape[1] // 2))) * 16


def scan_scratch(shape, rows):
    ntm, nsp = shape
    nz = min(4, ntm)
    peers, groups = nz * (nsp // 2), ntm // nz
    share = scan_share(shape, rows)
    dma = pltpu.SemaphoreType.DMA
    full, half = pltpu.VMEM((2, 2 * peers * share, 128), BF16), pltpu.VMEM((2, peers * share, 128), BF16)
    shares = pltpu.VMEM((peers, 2, share, 128), BF16)
    return [
        full,
        full,
        half,
        half,
        shares,
        pltpu.VMEM((peers, 2, share, 128), F32),
        shares,
        half,
        half,
        pltpu.VMEM((groups, share, 128), BF16),
        pltpu.VMEM((share, 128), BF16),
        dma,
        dma,
        dma((peers,)),
        dma((peers,)),
        dma((groups,)),
        dma((groups,)),
        dma((peers,)),
        dma((peers,)),
        dma,
        dma,
    ]


def to_mate(place, send, recv, send_sem, recv_sem, s):
    me = place.sp
    return remote(send.at[s], recv.at[me], send_sem.at[s], recv_sem.at[me], (place.tm, s))


def give(place, send, recv, send_sem, recv_sem, targets):
    for s in targets:

        @pl.when(place.sp != s)
        def _():
            to_mate(place, send, recv, send_sem, recv_sem, s).start()

        @pl.when(place.sp == s)
        def _():
            recv[s] = send[s]


def piece(place, send, recv, send_sem, recv_sem, s, *at):
    me = (place.sp, *at)
    there = (s, *at)
    return remote(send.at[there], recv.at[me], send_sem.at[there], recv_sem.at[me], (place.tm, s))


def give_piece(place, send, recv, send_sem, recv_sem, s, *at):
    @pl.when(place.sp != s)
    def _():
        piece(place, send, recv, send_sem, recv_sem, s, *at).start()

    @pl.when(place.sp == s)
    def _():
        there = (s, *at)
        pltpu.make_async_copy(send.at[there], recv.at[there], recv_sem.at[there]).start()


def kernel(
    shape,
    video, conv_h, embed_h, q_h, k_h, v_h, init_in, probe_h, po_h,
    out_recv, cot_recv, adj_out,
    slab, q_w, k_w, v_w, q, qd, k, v, latent, po_send, po_recv, po, init_send, init_recv, init,
    out_send, cot_send, adj_send,
    halo_send, halo_recv, load, keep_sem, po_s, po_r, init_s, init_r, out_s, out_r, cot_s, cot_r, adj_s,
    *scans,
):
    ntm, nsp = shape
    place = Place(ntm, nsp)
    tm, sp = place.tm, place.sp
    n = len(scans) // 4
    forward = [Scan(place, False, 5 * 2 * HD, *scans[i * n : i * n + n]) for i in range(2)]
    backward = [Scan(place, True, 5 * HD, *scans[i * n : i * n + n]) for i in range(2, 4)]

    later, earlier = tm + 1 < ntm, tm > 0
    down, up = sp + 1 < nsp, sp > 0
    last, first = pl.ds(TOK - 32, 32), pl.ds(0, 32)
    top, mid, bottom = pl.ds(0, 32), pl.ds(32, TOK), pl.ds(32 + TOK, 32)
    whole = pl.ds(0, TOK)
    prev, own = pl.ds(0, 2), pl.ds(2, 2)
    moves = (
        (down, up, last, own, top, (tm, sp + 1), (tm, sp - 1)),
        (up, down, first, own, bottom, (tm, sp - 1), (tm, sp + 1)),
        (later, earlier, whole, prev, mid, (tm + 1, sp), (tm - 1, sp)),
        (down & later, up & earlier, last, prev, top, (tm + 1, sp + 1), (tm - 1, sp - 1)),
        (up & later, down & earlier, first, prev, bottom, (tm + 1, sp - 1), (tm - 1, sp + 1)),
    )

    barrier = pltpu.get_barrier_semaphore()
    for _, may_recv, _, _, _, _, source in moves:

        @pl.when(may_recv)
        def _():
            pl.semaphore_signal(barrier, inc=1, device_id=source, device_id_type=MESH)

    def greet(count, device_of):
        @pl.loop(1, count)
        def _(i):
            pl.semaphore_signal(barrier, inc=1, device_id=device_of(i)[1], device_id_type=MESH)

    greet(place.groups, place.other)
    greet(place.peers, place.peer)
    greet(nsp, place.mate)

    def encode(conv_w, embed_w, probe, po_i, taps, acc, kd, vd):
        loads = [
            pltpu.make_async_copy(src, dst, load.at[i])
            for i, (src, dst) in enumerate(
                (
                    (po_h, po_i),
                    (probe_h, probe),
                    (k_h, k_w),
                    (v_h, v_w),
                    (conv_h, conv_w),
                    (q_h, q_w),
                    (embed_h, embed_w),
                )
            )
        ]
        keep = pltpu.make_async_copy(video, slab.at[own, mid], keep_sem)
        keep.start()
        for one in loads:
            one.start()

        for _, may_recv, _, frames, there, _, _ in moves:

            @pl.when(jnp.logical_not(may_recv))
            def _():
                slab[frames, there] = jnp.zeros((2, there.size, C), BF16)

        heads = [init_in[j] for j in range(4)]
        init_send[...] = jnp.concatenate(heads + [jnp.zeros((HD, 96), F32)], 1)
        for scan in forward:
            at = 5 * 2 * HD
            scan.blocks[:, at:, :] = jnp.zeros((2, scan.blocks.shape[1] - at, 128), BF16)

        greeted = place.groups + place.peers + nsp - 3
        pl.semaphore_wait(barrier, sum(m[0].astype(jnp.int32) for m in moves) + greeted)

        copies = []
        for i, (may_send, _, rows, frames, there, target, _) in enumerate(moves):
            copy = remote(video.at[:, rows], slab.at[frames, there], halo_send.at[i], halo_recv.at[i], target)
            copies.append(copy)

            @pl.when(may_send)
            def _():
                copy.start()

        loads[0].wait()
        for s in range(nsp):
            for f in range(2):
                po_send[s, f] = pack(po_i[f, TOK * s : TOK * s + TOK, :].astype(F32)).astype(BF16)

        col = lax.broadcasted_iota(jnp.int32, (TOK + 64, C), 0) % 32

        def build(f):
            here = slab[f].astype(F32)
            left = jnp.where(col == 0, 0.0, pltpu.roll(here, 1, 0))
            right = jnp.where(col == 31, 0.0, pltpu.roll(here, TOK + 63, 0))
            taps[f, :, 0:C] = left.astype(BF16)
            taps[f, :, C : 2 * C] = slab[f]
            taps[f, :, 2 * C : 3 * C] = right.astype(BF16)

        def halo_wait(i):
            @pl.when(moves[i][1])
            def _():
                copies[i].wait_recv()

        def convolve(a, out):
            @pl.loop(0, 3)
            def _(b):
                rows = pl.ds(pl.multiple_of(b * 32, 32), TOK)
                x = taps[a + out[0] : a + out[-1] + 1, rows, :].reshape(len(out) * TOK, 3 * C)
                here = slice(out[0] * TOK, (out[-1] + 1) * TOK)
                acc[here] += dot(x, conv_w[3 * a + b])

        acc[...] = jnp.zeros_like(acc)
        keep.wait()
        halo_wait(0)
        halo_wait(1)
        build(2)
        build(3)

        loads[1].wait()
        direction = probe[...].astype(F32).astype(BF16)
        for one, weight, out in zip(loads[2:4], (k_w, v_w), (kd, vd)):
            one.wait()
            out[...] = dot(direction, weight[...]).astype(BF16).reshape(2, TOK, D)

        loads[4].wait()
        convolve(2, (0, 1))
        convolve(1, (1,))
        loads[5].wait()
        qd[...] = dot(direction, q_w[...]).astype(BF16).reshape(2, TOK, D)
        halo_wait(2)
        halo_wait(3)
        halo_wait(4)

        @pl.loop(1, nsp)
        def _(i):
            init_move(i).start()

        init_recv[sp] = init_send[...]
        give(place, po_send, po_recv, po_s, po_r, range(nsp))
        build(0)
        build(1)
        convolve(1, (0,))
        convolve(0, (0, 1))

        u = acc[...]
        active = (u / (1.0 + jnp.exp(-u))).astype(BF16)
        loads[6].wait()
        latent[...] = dot(active, embed_w[...]).astype(BF16)
        for weight, out in zip((k_w, v_w), (k, v)):
            out[...] = dot(latent[...], weight[...]).astype(BF16).reshape(2, TOK, D)

        for scan, (windows, base, tiles, _) in zip(forward, PARTS):

            @pl.loop(0, 2)
            def _(f):
                st, sd = {}, {}
                over = ((0,), (0,))
                for t, heads in windows:
                    kw, vw = window(k, f, t), window(v, f, t)
                    compact_add(st, t, heads, dot(kw, vw, over))
                    both = dot(window(kd, f, t), vw, over) + dot(kw, window(vd, f, t), over)
                    compact_add(sd, t, heads, both)
                for j in range(tiles):
                    both = jnp.concatenate([st[base + j], sd[base + j]], 0)
                    scan.blocks[f, 144 * j : 144 * j + 144, :] = both.astype(BF16)

            scan.start()

        forward[0].spread()
        q[...] = dot(latent[...], q_w[...]).astype(BF16).reshape(2, TOK, D)
        for copy, (may_send, *_) in zip(copies, moves):

            @pl.when(may_send)
            def _():
                copy.wait_send()

    def init_move(i):
        _, device = place.mate(i)
        return remote(init_send, init_recv.at[sp], init_s.at[i], init_r.at[sp], device)

    pl.run_scoped(
        encode,
        pltpu.VMEM((9, 3 * C, C), BF16),
        pltpu.VMEM((C, D), BF16),
        pltpu.VMEM((2 * TOK, D), jnp.int32),
        pltpu.VMEM((2, 4 * TOK, D // 4), jnp.int32),
        pltpu.VMEM((4, TOK + 64, 3 * C), BF16),
        pltpu.VMEM((2 * TOK, C), F32),
        pltpu.VMEM((2, TOK, D), BF16),
        pltpu.VMEM((2, TOK, D), BF16),
    )

    forward[1].spread()
    forward[0].group_sums()
    forward[1].group_sums()

    @pl.loop(1, nsp)
    def _(i):
        s, _ = place.mate(i)
        arrived(po_recv.at[s], po_r.at[s])
        arrived(init_recv.at[s], init_r.at[s])

    for s in range(nsp):
        init[:, 288 * s : 288 * s + 288] = init_recv[s, :, 0:288]
        for f in range(2):
            po[f, :, 288 * s : 288 * s + 288] = unpack(po_recv[s, f].astype(F32)).astype(BF16)

    forward[0].send_back()
    forward[1].send_back()
    forward[0].pair_back()

    def mixing(bd, m_ref, md_ref, s1, s2, s3, mbar, q_bar, adj):
        def leave(x, f, across):
            for s in range(nsp):
                there = place.y != s // 2

                @pl.when(there if across else jnp.logical_not(there))
                def _():
                    give_piece(place, out_send, out_recv, out_s, out_r, s, x, f)

        def mix(i, early):
            windows, base, tiles, targets = PARTS[i]
            prefix, blocks = forward[i].out, backward[i].blocks
            part = slice(128 * base, 128 * (base + tiles))

            @pl.loop(0, 2)
            def _(f):
                pt, pdt = {}, {}
                for j in range(base, base + tiles):
                    both = prefix[f, 144 * (j - base) : 144 * (j - base) + 144, :].astype(F32)
                    pt[j] = both[:HD] + init[:, 128 * j : 128 * j + 128]
                    pdt[j] = both[HD:]
                for w, (t, heads) in enumerate(windows):
                    bd[w] = block_diagonal(pt, t, heads)
                    bdd = block_diagonal(pdt, t, heads)
                    qw, qdw = window(q, f, t), window(qd, f, t)
                    window_out(m_ref, t - base, dot(qw, bd[w]))
                    window_out(md_ref, t - base, dot(qdw, bd[w]) + dot(qw, bdd))
                for t, heads in windows:
                    ones = same_head(t, heads)
                    lanes = slice(128 * (t - base), 128 * (t - base) + 256)
                    m, md, p = m_ref[:, lanes], md_ref[:, lanes], window(po, f, t).astype(F32)
                    window_out(s1, t - base, dot((m * m).astype(BF16), ones))
                    window_out(s2, t - base, dot((m * md).astype(BF16), ones))
                    window_out(s3, t - base, dot((m * p).astype(BF16), ones))
                m, md, p = m_ref[...], md_ref[...], po[f, :, part].astype(F32)
                scale = lax.rsqrt(s1[...] * (1.0 / HD) + 1e-6)
                pulled = m * (scale * scale * scale) * (1.0 / HD)
                mbar[...] = (p * scale - pulled * s3[...]).astype(BF16)
                fl = m * scale
                tg = md * scale - pulled * s2[...]
                for s in targets:
                    at = 288 * s - 128 * base
                    out_send[s, 0, f] = pack(fl[:, at : at + 288]).astype(BF16)
                    out_send[s, 1, f] = pack(tg[:, at : at + 288]).astype(BF16)
                if early:

                    @pl.when(f == 0)
                    def _():
                        leave(0, 0, True)
                        leave(1, 0, True)

                pb = {}
                for w, (t, heads) in enumerate(windows):
                    mw = mbar[:, 128 * (t - base) : 128 * (t - base) + 256]
                    window_out(s1, t - base, dot(mw, bd[w], ((1,), (1,))))
                    compact_add(pb, t, heads, dot(window(q, f, t), mw, ((0,), (0,))))
                q_bar[i, f] = s1[...].astype(BF16)
                pb = [pb[j] for j in range(base, base + tiles)]
                pb.append(jnp.zeros((blocks.shape[1] - tiles * HD, 128), F32))
                blocks[f] = jnp.concatenate(pb, 0).astype(BF16)

            backward[i].start()

        def settle(i, last):
            windows, base, tiles, targets = PARTS[i]
            sc = backward[i].out
            part = slice(128 * base, 128 * (base + tiles))

            def tiles_of(f):
                rows = sc[f].astype(F32)
                return {base + j: rows[HD * j : HD * j + HD] for j in range(tiles)}

            @pl.loop(0, 2)
            def _(f):
                state = tiles_of(f)
                for s in targets:
                    wide = jnp.concatenate([state[2 * s + j] for j in range(3)], 1)[:, 32 * s : 32 * s + 288]
                    rest = [wide[24 * j : 24 * j + 24, 256:] for j in range(3)]
                    rest = jnp.concatenate(rest + [jnp.zeros((24, 32), F32)], 1)
                    parts = [wide[:, :128], wide[:, 128:256], rest, jnp.zeros((8, 128), F32)]
                    cot_send[s, f] = jnp.concatenate(parts, 0).astype(BF16)

            for s in targets:
                give_piece(place, cot_send, cot_recv, cot_s, cot_r, s)

            @pl.loop(0, 2)
            def _(f):
                state = tiles_of(f)
                for t, heads in windows:
                    b = block_diagonal(state, t, heads)
                    window_out(s1, t - base, dot(window(v, f, t), b, ((1,), (1,))))
                    window_out(s2, t - base, dot(window(k, f, t), b))
                total = adj[f] + dot(s1[...].astype(BF16), k_w[:, part], ((1,), (1,)))
                total = total + dot(s2[...].astype(BF16), v_w[:, part], ((1,), (1,)))
                if last:
                    adj_send[f] = total.astype(BF16)
                    pltpu.make_async_copy(adj_send.at[f], adj_out.at[f], adj_s.at[f]).start()
                else:
                    adj[f] = total

        forward[0].finish()

        @pl.when(place.y == 1)
        def _():
            mix(0, True)

        forward[1].pair_back()
        forward[1].finish()

        @pl.when(place.y == 0)
        def _():
            mix(1, True)
            mix(0, False)

        @pl.when(place.y == 1)
        def _():
            mix(1, False)

        backward[0].spread()
        backward[1].spread()
        leave(0, 1, True)
        for f in range(2):
            leave(0, f, False)
            leave(1, f, False)

        @pl.loop(0, 2)
        def _(f):
            total = None
            for i, (_, base, tiles, _) in enumerate(PARTS):
                part = slice(128 * base, 128 * (base + tiles))
                share = dot(q_bar[i, f], q_w[:, part], ((1,), (1,)))
                total = share if total is None else total + share
            adj[f] = total

        backward[0].group_sums()
        backward[1].group_sums()
        backward[0].send_back()
        backward[1].send_back()
        leave(1, 1, True)
        backward[0].pair_back()
        backward[0].finish()
        backward[1].pair_back()
        settle(0, False)
        backward[1].finish()
        settle(1, True)

    wide = pltpu.VMEM((TOK, 640), F32)
    pl.run_scoped(
        mixing,
        pltpu.VMEM((4, 256, 256), BF16),
        wide,
        wide,
        wide,
        wide,
        wide,
        pltpu.VMEM((TOK, 640), BF16),
        pltpu.VMEM((2, 2, TOK, 640), BF16),
        pltpu.VMEM((2, TOK, D), F32),
    )

    @pl.loop(0, nsp)
    def _(s):
        for x in range(2):
            for f in range(2):
                arrived(out_recv.at[s, x, f], out_r.at[s, x, f])
        arrived(cot_recv.at[s], cot_r.at[s])

    @pl.loop(1, nsp)
    def _(i):
        s, _ = place.mate(i)
        to_mate(place, po_send, po_recv, po_s, po_r, s).wait_send()
        init_move(i).wait_send()
        for x in range(2):
            for f in range(2):
                piece(place, out_send, out_recv, out_s, out_r, s, x, f).wait_send()
        piece(place, cot_send, cot_recv, cot_s, cot_r, s).wait_send()

    for f in range(2):
        pltpu.make_async_copy(adj_send.at[f], adj_out.at[f], adj_s.at[f]).wait()

    for scan in forward + backward:
        scan.drain()


def unpack_kernel(nsp, out_h, cot_h, adj_h, flow_h, tangent_h, cot_out_h, adj_out_h,
                  out, cot, adj, flow, tangent, cots, sems, done, adj_s):
    def loads(i):
        s, f = i // 2, i % 2
        return (
            pltpu.make_async_copy(out_h.at[s, :, f], out.at[i], sems.at[0, i]),
            pltpu.make_async_copy(cot_h.at[s, f], cot.at[i], sems.at[1, i]),
        )

    def stores(i):
        s, f = i // 2, i % 2
        return (
            pltpu.make_async_copy(flow.at[i], flow_h.at[f, s], done.at[0, i]),
            pltpu.make_async_copy(tangent.at[i], tangent_h.at[f, s], done.at[1, i]),
            pltpu.make_async_copy(cots.at[i], cot_out_h.at[f, s], done.at[2, i]),
        )

    take = pltpu.make_async_copy(adj_h, adj, adj_s.at[0])
    put = pltpu.make_async_copy(adj, adj_out_h, adj_s.at[1])
    take.start()
    for i in range(2 * nsp):
        for one in loads(i):
            one.start()
    take.wait()
    put.start()

    @pl.loop(0, 2 * nsp)
    def _(i):
        for one in loads(i):
            one.wait()
        for x, to in enumerate((flow, tangent)):
            to[i, :, 0:128] = out[i, x, 0:TOK]
            to[i, :, 128:256] = out[i, x, TOK : 2 * TOK]
            rest = out[i, x, 2 * TOK :]
            for j in range(4):
                to[i, 64 * j : 64 * j + 64, 256:288] = rest[:, 32 * j : 32 * j + 32]
        rows = cot[i].astype(F32)
        rest = rows[2 * HD : 2 * HD + 24]
        rest = jnp.concatenate([rest[:, 32 * j : 32 * j + 32] for j in range(3)], 0)
        lanes = jnp.concatenate([rows[:HD], rows[HD : 2 * HD], rest], 1)
        for j in range(4):
            cots[i, j] = lanes[:, HD * j : HD * j + HD]
        for one in stores(i):
            one.start()

    for i in range(2 * nsp):
        for one in stores(i):
            one.wait()
    put.wait()


def unpacked(nsp, out, cot, adj):
    heads = jax.ShapeDtypeStruct((2, nsp, TOK, D // 4), BF16)
    n = 2 * nsp
    return pl.pallas_call(
        functools.partial(unpack_kernel, nsp),
        out_shape=[
            heads,
            heads,
            jax.ShapeDtypeStruct((2, nsp, 4, HD, HD), F32),
            jax.ShapeDtypeStruct(adj.shape, BF16),
        ],
        in_specs=[anywhere()] * 3,
        out_specs=[anywhere()] * 4,
        scratch_shapes=[
            pltpu.VMEM((n, 2, PACK, 128), BF16),
            pltpu.VMEM((n, COT, 128), BF16),
            pltpu.VMEM(adj.shape, BF16),
            pltpu.VMEM((n, TOK, D // 4), BF16),
            pltpu.VMEM((n, TOK, D // 4), BF16),
            pltpu.VMEM((n, 4, HD, HD), F32),
            pltpu.SemaphoreType.DMA((2, n)),
            pltpu.SemaphoreType.DMA((3, n)),
            pltpu.SemaphoreType.DMA((2,)),
        ],
        compiler_params=pltpu.CompilerParams(vmem_limit_bytes=VMEM_LIMIT),
        name="unpack",
    )(out, cot, adj)


def on_device(shape, video, conv_weight, embed_weight, q_weight, k_weight, v_weight, initial_state, probe_in, probe_out):
    ntm, nsp = shape
    dma = pltpu.SemaphoreType.DMA
    rows = pltpu.VMEM((2, TOK, D), BF16)
    square = pltpu.VMEM((D, D), BF16)
    packed = pltpu.VMEM((nsp, 2, PACK, 128), BF16)
    four = dma((nsp,))
    out, cot, adjoint = pl.pallas_call(
        functools.partial(kernel, shape),
        out_shape=[
            jax.ShapeDtypeStruct((nsp, 2, 2, PACK, 128), BF16),
            jax.ShapeDtypeStruct((nsp, 2, COT, 128), BF16),
            jax.ShapeDtypeStruct((2, TOK, D), BF16),
        ],
        in_specs=[anywhere()] * 6 + [vmem()] + [anywhere()] * 2,
        out_specs=[anywhere()] * 3,
        scratch_shapes=[
            pltpu.VMEM((4, TOK + 64, C), BF16),
            square,
            square,
            square,
            rows,
            rows,
            rows,
            rows,
            pltpu.VMEM((2 * TOK, D), BF16),
            packed,
            packed,
            rows,
            pltpu.VMEM((HD, 384), F32),
            pltpu.VMEM((nsp, HD, 384), F32),
            pltpu.VMEM((HD, D), F32),
            pltpu.VMEM((nsp, 2, 2, PACK, 128), BF16),
            pltpu.VMEM((nsp, 2, COT, 128), BF16),
            rows,
            dma((5,)),
            dma((5,)),
            dma((7,)),
            dma,
            four,
            four,
            four,
            four,
            dma((nsp, 2, 2)),
            dma((nsp, 2, 2)),
            four,
            four,
            dma((2,)),
        ]
        + scan_scratch(shape, 5 * 2 * HD) * 2
        + scan_scratch(shape, 5 * HD) * 2,
        compiler_params=pltpu.CompilerParams(
            collective_id=0, has_side_effects=True, vmem_limit_bytes=VMEM_LIMIT
        ),
        name="flow_layer",
    )(
        video.reshape(2, TOK, C),
        conv_weight.reshape(9, 3 * C, C),
        embed_weight,
        q_weight,
        k_weight,
        v_weight,
        initial_state,
        probe_in.reshape(2 * TOK, D),
        probe_out.reshape(2, 4 * TOK, D // 4),
    )
    flow, tangent, cot, adjoint = unpacked(nsp, out, cot, adjoint)
    full = (2, 32, 32, D // 4)
    return (
        flow.reshape(full),
        tangent.reshape(full),
        adjoint.reshape(2, 8, 32, D),
        cot.reshape(8, 4, HD, HD),
    )


def solution(mesh):
    by_rows = P("tm", "space", None, None)
    by_heads = P("tm", None, None, "space")
    return jax.shard_map(
        functools.partial(on_device, (mesh.shape["tm"], mesh.shape["space"])),
        mesh=mesh,
        in_specs=(by_rows, P(), P(), P(), P(), P(), P("space", None, None), by_rows, by_heads),
        out_specs=(by_heads, by_heads, by_rows, by_rows),
        check_vma=False,
    )
```

```python
import functools

import jax
import jax.numpy as jnp
from jax import lax
from jax.experimental import pallas as pl
from jax.experimental.pallas import tpu as pltpu
from jax.sharding import PartitionSpec as P

MESH = pl.DeviceIdType.MESH
F32 = jnp.float32
BF16 = jnp.bfloat16
D = 1152
HEADS = 16
HD = 72
C = 384
TOK = 256
TILES = D // 128
WINDOWS = (
    (0, (0, 1, 2)),
    (1, (3, 4)),
    (2, (5, 6)),
    (3, (7,)),
    (4, (8, 9)),
    (5, (10, 11)),
    (6, (12, 13)),
    (7, (14, 15)),
)
VMEM_LIMIT = 60 * 1024 * 1024


PARTS = ((WINDOWS[:4], 0, 5, (0, 1)), (WINDOWS[4:], 4, 5, (2, 3)))
COT = 176
PACK = 2 * TOK + TOK // 4


def vmem():
    return pl.BlockSpec(memory_space=pltpu.VMEM)


def anywhere():
    return pl.BlockSpec(memory_space=pl.ANY)


def dot(a, b, dims=((1,), (0,))):
    return lax.dot_general(a, b, (dims, ((), ())), preferred_element_type=F32)


def head_mask(h, tile, rows):
    lane = lax.broadcasted_iota(jnp.int32, (rows, 128), 1) + 128 * tile
    return (lane >= HD * h) & (lane < HD * (h + 1))


def compact_add(tiles, t, heads, g):
    for half in range(2):
        j = t + half
        for h in heads:
            if HD * h < 128 * (j + 1) and HD * (h + 1) > 128 * j:
                r = HD * h - 128 * t
                piece = g[r : r + HD, 128 * half : 128 * half + 128]
                piece = jnp.where(head_mask(h, j, HD), piece, 0.0)
                tiles[j] = tiles[j] + piece if j in tiles else piece


def block_diagonal(tiles, t, heads):
    halves = []
    for half in range(2):
        j = t + half
        parts = []
        at = 0
        for h in heads:
            r = HD * h - 128 * t
            if r > at:
                parts.append(jnp.zeros((r - at, 128), F32))
            if HD * h < 128 * (j + 1) and HD * (h + 1) > 128 * j:
                parts.append(jnp.where(head_mask(h, j, HD), tiles[j], 0.0))
            else:
                parts.append(jnp.zeros((HD, 128), F32))
            at = r + HD
        if at < 256:
            parts.append(jnp.zeros((256 - at, 128), F32))
        halves.append(jnp.concatenate(parts, 0))
    return jnp.concatenate(halves, 1).astype(BF16)


def same_head(t, heads):
    row = lax.broadcasted_iota(jnp.int32, (256, 256), 0) + 128 * t
    col = lax.broadcasted_iota(jnp.int32, (256, 256), 1) + 128 * t
    ok = None
    for h in heads:
        low, high = HD * h, HD * (h + 1)
        both = (row >= low) & (row < high) & (col >= low) & (col < high)
        ok = both if ok is None else ok | both
    return jnp.where(ok, 1.0, 0.0).astype(BF16)


def window_out(ref, t, value):
    if t == 0:
        ref[:, 0:256] = value
    else:
        ref[:, 128 * t : 128 * t + 128] = ref[:, 128 * t : 128 * t + 128] + value[:, :128]
        ref[:, 128 * t + 128 : 128 * t + 256] = value[:, 128:]


def pack(x):
    rest = x[:, 256:]
    rest = jnp.concatenate([rest[64 * i : 64 * i + 64] for i in range(4)], 1)
    return jnp.concatenate([x[:, :128], x[:, 128:256], rest], 0)


def unpack(x):
    rest = jnp.concatenate([x[2 * TOK :, 32 * i : 32 * i + 32] for i in range(4)], 0)
    return jnp.concatenate([x[:TOK], x[TOK : 2 * TOK], rest], 1)


def arrived(ref, sem):
    pltpu.make_async_copy(ref, ref, sem).wait()


def window(ref, f, t):
    return ref[f, :, 128 * t : 128 * t + 256]


class Place:
    def __init__(self, ntm, nsp):
        self.ntm, self.nsp = ntm, nsp
        self.nz, self.ny = min(4, ntm), nsp // 2
        self.tm, self.sp = lax.axis_index("tm"), lax.axis_index("space")
        self.peers, self.groups = self.nz * self.ny, ntm // self.nz
        self.group, self.z = self.tm // self.nz, self.tm % self.nz
        self.y, self.core = self.sp // 2, self.sp % 2
        self.me = self.z * self.ny + self.y
        self.twin = (self.tm, self.sp + 1 - 2 * self.core)

    def peer(self, k):
        p = lax.rem(self.me + k, self.peers)
        return p, (self.group * self.nz + p // self.ny, 2 * (p % self.ny) + self.core)

    def other(self, k):
        g = lax.rem(self.group + k, self.groups)
        return g, (g * self.nz + self.z, self.sp)

    def mate(self, k):
        s = lax.rem(self.sp + k, self.nsp)
        return s, (self.tm, s)


def remote(src, dst, send_sem, recv_sem, device):
    return pltpu.make_async_remote_copy(
        src_ref=src,
        dst_ref=dst,
        send_sem=send_sem,
        recv_sem=recv_sem,
        device_id=device,
        device_id_type=MESH,
    )


class Scan:
    def __init__(self, place, reverse, rows, blocks, out, pair, chip, got, sums, answer, back, theirs, totals, total,
                 s0, r0, s1, r1, s2, r2, s3, r3, s4, r4):
        self.place, self.reverse, self.rows = place, reverse, rows
        self.blocks, self.out, self.pair, self.chip, self.got = blocks, out, pair, chip, got
        self.sums, self.answer, self.back, self.theirs = sums, answer, back, theirs
        self.totals, self.total = totals, total
        self.s0, self.r0, self.s1, self.r1, self.s2, self.r2 = s0, r0, s1, r1, s2, r2
        self.s3, self.r3, self.s4, self.r4 = s3, r3, s4, r4
        self.share = got.shape[2]

    def half(self, c):
        n = self.chip.shape[1]
        return pl.ds(pl.multiple_of(c * n, n), n)

    def part(self, p):
        return pl.ds(pl.multiple_of(p * self.share, self.share), self.share)

    def used(self, p):
        return (self.place.core * self.place.peers + p) * self.share < self.rows

    def swap(self):
        return remote(
            self.blocks.at[:, self.half(1 - self.place.core)], self.pair, self.s0, self.r0, self.place.twin
        )

    def first(self, k):
        p, device = self.place.peer(k)
        me = self.place.me
        return remote(self.chip.at[:, self.part(p)], self.got.at[me], self.s1.at[p], self.r1.at[me], device)

    def second(self, k):
        g, device = self.place.other(k)
        mine = self.place.group
        return remote(self.total, self.totals.at[mine], self.s2.at[g], self.r2.at[mine], device)

    def third(self, k):
        p, device = self.place.peer(k)
        me = self.place.me
        return remote(self.answer.at[p], self.back.at[:, self.part(me)], self.s3.at[p], self.r3.at[me], device)

    def fourth(self):
        return remote(self.theirs, self.out.at[:, self.half(self.place.core)], self.s4, self.r4, self.place.twin)

    def start(self):
        self.swap().start()

    def spread(self):
        arrived(self.pair, self.r0)
        own = self.blocks[:, self.half(self.place.core)].astype(F32)
        self.chip[...] = (own + self.pair[...].astype(F32)).astype(BF16)

        @pl.loop(1, self.place.peers)
        def _(k):
            @pl.when(self.used(self.place.peer(k)[0]))
            def _():
                self.first(k).start()

    def group_sums(self):
        @pl.when(self.used(self.place.me))
        def _():
            self.got[self.place.me] = self.chip[:, self.part(self.place.me)]

            @pl.loop(1, self.place.peers)
            def _(k):
                p, _ = self.place.peer(k)
                arrived(self.got.at[p], self.r1.at[p])

            ny = self.place.ny
            running = jnp.zeros((self.share, 128), F32)
            order = [(zz * ny + y, f) for zz in range(self.place.nz) for f in range(2) for y in range(ny)]
            for p, f in reversed(order) if self.reverse else order:
                self.sums[p, f] = running
                running = running + self.got[p, f].astype(F32)
            self.total[...] = running.astype(BF16)

            @pl.loop(1, self.place.groups)
            def _(k):
                self.second(k).start()

            self.totals[self.place.group] = jnp.zeros((self.share, 128), BF16)

    def send_back(self):
        @pl.when(self.used(self.place.me))
        def _():
            @pl.loop(1, self.place.groups)
            def _(k):
                g, _ = self.place.other(k)
                arrived(self.totals.at[g], self.r2.at[g])

            group = self.place.group
            before = jnp.zeros((self.share, 128), F32)
            for g in range(self.place.groups):
                counts = g > group if self.reverse else g < group
                before = before + jnp.where(counts, self.totals[g].astype(F32), 0.0)
            for p in range(self.place.peers):
                self.answer[p] = (self.sums[p] + before[None]).astype(BF16)

            @pl.loop(1, self.place.peers)
            def _(k):
                self.third(k).start()

            self.back[:, self.part(self.place.me)] = self.answer[self.place.me]

    def pair_back(self):
        @pl.loop(1, self.place.peers)
        def _(k):
            p, _ = self.place.peer(k)

            @pl.when(self.used(p))
            def _():
                arrived(self.answer.at[p], self.r3.at[p])

        core = self.place.core
        here = self.half(core)
        before = self.back[...].astype(F32)
        own, pair = self.blocks[:, here].astype(F32), self.pair[...].astype(F32)
        after = core == (0 if self.reverse else 1)
        self.theirs[...] = (before + pair + jnp.where(after, 0.0, own)).astype(BF16)
        self.fourth().start()
        self.out[:, here] = (before + own + jnp.where(after, pair, 0.0)).astype(BF16)

    def finish(self):
        arrived(self.theirs, self.r4)

    def drain(self):
        self.swap().wait_send()
        self.fourth().wait_send()

        @pl.loop(1, self.place.peers)
        def _(k):
            @pl.when(self.used(self.place.peer(k)[0]))
            def _():
                self.first(k).wait_send()

        @pl.when(self.used(self.place.me))
        def _():
            @pl.loop(1, self.place.peers)
            def _(k):
                self.third(k).wait_send()

            @pl.loop(1, self.place.groups)
            def _(k):
                self.second(k).wait_send()


def scan_share(shape, rows):
    return -(-rows // (16 * 2 * min(4, shape[0]) * (shape[1] // 2))) * 16


def scan_scratch(shape, rows):
    ntm, nsp = shape
    nz = min(4, ntm)
    peers, groups = nz * (nsp // 2), ntm // nz
    share = scan_share(shape, rows)
    dma = pltpu.SemaphoreType.DMA
    full, half = pltpu.VMEM((2, 2 * peers * share, 128), BF16), pltpu.VMEM((2, peers * share, 128), BF16)
    shares = pltpu.VMEM((peers, 2, share, 128), BF16)
    return [
        full,
        full,
        half,
        half,
        shares,
        pltpu.VMEM((peers, 2, share, 128), F32),
        shares,
        half,
        half,
        pltpu.VMEM((groups, share, 128), BF16),
        pltpu.VMEM((share, 128), BF16),
        dma,
        dma,
        dma((peers,)),
        dma((peers,)),
        dma((groups,)),
        dma((groups,)),
        dma((peers,)),
        dma((peers,)),
        dma,
        dma,
    ]


def to_mate(place, send, recv, send_sem, recv_sem, s):
    me = place.sp
    return remote(send.at[s], recv.at[me], send_sem.at[s], recv_sem.at[me], (place.tm, s))


def give(place, send, recv, send_sem, recv_sem, targets):
    for s in targets:

        @pl.when(place.sp != s)
        def _():
            to_mate(place, send, recv, send_sem, recv_sem, s).start()

        @pl.when(place.sp == s)
        def _():
            recv[s] = send[s]


def piece(place, send, recv, send_sem, recv_sem, s, *at):
    me = (place.sp, *at)
    there = (s, *at)
    return remote(send.at[there], recv.at[me], send_sem.at[there], recv_sem.at[me], (place.tm, s))


def give_piece(place, send, recv, send_sem, recv_sem, s, *at):
    @pl.when(place.sp != s)
    def _():
        piece(place, send, recv, send_sem, recv_sem, s, *at).start()

    @pl.when(place.sp == s)
    def _():
        there = (s, *at)
        pltpu.make_async_copy(send.at[there], recv.at[there], recv_sem.at[there]).start()


def kernel(
    shape,
    video, conv_h, embed_h, q_h, k_h, v_h, init_in, probe_h, po_h,
    out_recv, cot_recv, adj_out,
    slab, q_w, k_w, v_w, q, qd, k, v, latent, po_send, po_recv, po, init_send, init_recv, init,
    out_send, cot_send, adj_send,
    halo_send, halo_recv, load, keep_sem, po_s, po_r, init_s, init_r, out_s, out_r, cot_s, cot_r, adj_s,
    *scans,
):
    ntm, nsp = shape
    place = Place(ntm, nsp)
    tm, sp = place.tm, place.sp
    n = len(scans) // 4
    forward = [Scan(place, False, 5 * 2 * HD, *scans[i * n : i * n + n]) for i in range(2)]
    backward = [Scan(place, True, 5 * HD, *scans[i * n : i * n + n]) for i in range(2, 4)]

    later, earlier = tm + 1 < ntm, tm > 0
    down, up = sp + 1 < nsp, sp > 0
    last, first = pl.ds(TOK - 32, 32), pl.ds(0, 32)
    top, mid, bottom = pl.ds(0, 32), pl.ds(32, TOK), pl.ds(32 + TOK, 32)
    whole = pl.ds(0, TOK)
    prev, own = pl.ds(0, 2), pl.ds(2, 2)
    moves = (
        (down, up, last, own, top, (tm, sp + 1), (tm, sp - 1)),
        (up, down, first, own, bottom, (tm, sp - 1), (tm, sp + 1)),
        (later, earlier, whole, prev, mid, (tm + 1, sp), (tm - 1, sp)),
        (down & later, up & earlier, last, prev, top, (tm + 1, sp + 1), (tm - 1, sp - 1)),
        (up & later, down & earlier, first, prev, bottom, (tm + 1, sp - 1), (tm - 1, sp + 1)),
    )

    barrier = pltpu.get_barrier_semaphore()
    for _, may_recv, _, _, _, _, source in moves:

        @pl.when(may_recv)
        def _():
            pl.semaphore_signal(barrier, inc=1, device_id=source, device_id_type=MESH)

    def greet(count, device_of):
        @pl.loop(1, count)
        def _(i):
            pl.semaphore_signal(barrier, inc=1, device_id=device_of(i)[1], device_id_type=MESH)

    greet(place.groups, place.other)
    greet(place.peers, place.peer)
    greet(nsp, place.mate)

    def encode(conv_w, embed_w, probe, po_i, taps, acc, kd, vd):
        loads = [
            pltpu.make_async_copy(src, dst, load.at[i])
            for i, (src, dst) in enumerate(
                (
                    (po_h, po_i),
                    (probe_h, probe),
                    (k_h, k_w),
                    (v_h, v_w),
                    (conv_h, conv_w),
                    (q_h, q_w),
                    (embed_h, embed_w),
                )
            )
        ]
        keep = pltpu.make_async_copy(video, slab.at[own, mid], keep_sem)
        keep.start()
        for one in loads:
            one.start()

        for _, may_recv, _, frames, there, _, _ in moves:

            @pl.when(jnp.logical_not(may_recv))
            def _():
                slab[frames, there] = jnp.zeros((2, there.size, C), BF16)

        heads = [init_in[j] for j in range(4)]
        init_send[...] = jnp.concatenate(heads + [jnp.zeros((HD, 96), F32)], 1)
        for scan in forward:
            at = 5 * 2 * HD
            scan.blocks[:, at:, :] = jnp.zeros((2, scan.blocks.shape[1] - at, 128), BF16)

        greeted = place.groups + place.peers + nsp - 3
        pl.semaphore_wait(barrier, sum(m[0].astype(jnp.int32) for m in moves) + greeted)

        copies = []
        for i, (may_send, _, rows, frames, there, target, _) in enumerate(moves):
            copy = remote(video.at[:, rows], slab.at[frames, there], halo_send.at[i], halo_recv.at[i], target)
            copies.append(copy)

            @pl.when(may_send)
            def _():
                copy.start()

        loads[0].wait()
        for s in range(nsp):
            for f in range(2):
                po_send[s, f] = pack(po_i[f, TOK * s : TOK * s + TOK, :].astype(F32)).astype(BF16)

        col = lax.broadcasted_iota(jnp.int32, (TOK + 64, C), 0) % 32

        def build(f):
            here = slab[f].astype(F32)
            left = jnp.where(col == 0, 0.0, pltpu.roll(here, 1, 0))
            right = jnp.where(col == 31, 0.0, pltpu.roll(here, TOK + 63, 0))
            taps[f, :, 0:C] = left.astype(BF16)
            taps[f, :, C : 2 * C] = slab[f]
            taps[f, :, 2 * C : 3 * C] = right.astype(BF16)

        def halo_wait(i):
            @pl.when(moves[i][1])
            def _():
                copies[i].wait_recv()

        def convolve(a, out):
            @pl.loop(0, 3)
            def _(b):
                rows = pl.ds(pl.multiple_of(b * 32, 32), TOK)
                x = taps[a + out[0] : a + out[-1] + 1, rows, :].reshape(len(out) * TOK, 3 * C)
                here = slice(out[0] * TOK, (out[-1] + 1) * TOK)
                acc[here] += dot(x, conv_w[3 * a + b])

        acc[...] = jnp.zeros_like(acc)
        keep.wait()
        halo_wait(0)
        halo_wait(1)
        build(2)
        build(3)

        loads[1].wait()
        direction = probe[...].astype(F32).astype(BF16)
        for one, weight, out in zip(loads[2:4], (k_w, v_w), (kd, vd)):
            one.wait()
            out[...] = dot(direction, weight[...]).astype(BF16).reshape(2, TOK, D)

        loads[4].wait()
        convolve(2, (0, 1))
        convolve(1, (1,))
        loads[5].wait()
        qd[...] = dot(direction, q_w[...]).astype(BF16).reshape(2, TOK, D)
        halo_wait(2)
        halo_wait(3)
        halo_wait(4)

        @pl.loop(1, nsp)
        def _(i):
            init_move(i).start()

        init_recv[sp] = init_send[...]
        give(place, po_send, po_recv, po_s, po_r, range(nsp))
        build(0)
        build(1)
        convolve(1, (0,))
        convolve(0, (0, 1))

        u = acc[...]
        active = (u / (1.0 + jnp.exp(-u))).astype(BF16)
        loads[6].wait()
        latent[...] = dot(active, embed_w[...]).astype(BF16)
        for weight, out in zip((k_w, v_w), (k, v)):
            out[...] = dot(latent[...], weight[...]).astype(BF16).reshape(2, TOK, D)

        for scan, (windows, base, tiles, _) in zip(forward, PARTS):

            @pl.loop(0, 2)
            def _(f):
                st, sd = {}, {}
                over = ((0,), (0,))
                for t, heads in windows:
                    kw, vw = window(k, f, t), window(v, f, t)
                    compact_add(st, t, heads, dot(kw, vw, over))
                    both = dot(window(kd, f, t), vw, over) + dot(kw, window(vd, f, t), over)
                    compact_add(sd, t, heads, both)
                for j in range(tiles):
                    both = jnp.concatenate([st[base + j], sd[base + j]], 0)
                    scan.blocks[f, 144 * j : 144 * j + 144, :] = both.astype(BF16)

            scan.start()

        forward[0].spread()
        forward[1].spread()
        q[...] = dot(latent[...], q_w[...]).astype(BF16).reshape(2, TOK, D)
        for copy, (may_send, *_) in zip(copies, moves):

            @pl.when(may_send)
            def _():
                copy.wait_send()

    def init_move(i):
        _, device = place.mate(i)
        return remote(init_send, init_recv.at[sp], init_s.at[i], init_r.at[sp], device)

    pl.run_scoped(
        encode,
        pltpu.VMEM((9, 3 * C, C), BF16),
        pltpu.VMEM((C, D), BF16),
        pltpu.VMEM((2 * TOK, D), jnp.int32),
        pltpu.VMEM((2, 4 * TOK, D // 4), jnp.int32),
        pltpu.VMEM((4, TOK + 64, 3 * C), BF16),
        pltpu.VMEM((2 * TOK, C), F32),
        pltpu.VMEM((2, TOK, D), BF16),
        pltpu.VMEM((2, TOK, D), BF16),
    )

    forward[0].group_sums()
    forward[1].group_sums()

    @pl.loop(1, nsp)
    def _(i):
        s, _ = place.mate(i)
        arrived(po_recv.at[s], po_r.at[s])
        arrived(init_recv.at[s], init_r.at[s])

    for s in range(nsp):
        init[:, 288 * s : 288 * s + 288] = init_recv[s, :, 0:288]
        for f in range(2):
            po[f, :, 288 * s : 288 * s + 288] = unpack(po_recv[s, f].astype(F32)).astype(BF16)

    forward[0].send_back()
    forward[1].send_back()
    forward[0].pair_back()

    def mixing(bd, m_ref, md_ref, s1, s2, s3, mbar, q_bar, adj):
        def leave(x, f, across):
            for s in range(nsp):
                there = place.y != s // 2

                @pl.when(there if across else jnp.logical_not(there))
                def _():
                    give_piece(place, out_send, out_recv, out_s, out_r, s, x, f)

        def mix(i, early):
            windows, base, tiles, targets = PARTS[i]
            prefix, blocks = forward[i].out, backward[i].blocks
            part = slice(128 * base, 128 * (base + tiles))

            @pl.loop(0, 2)
            def _(f):
                pt, pdt = {}, {}
                for j in range(base, base + tiles):
                    both = prefix[f, 144 * (j - base) : 144 * (j - base) + 144, :].astype(F32)
                    pt[j] = both[:HD] + init[:, 128 * j : 128 * j + 128]
                    pdt[j] = both[HD:]
                for w, (t, heads) in enumerate(windows):
                    bd[w] = block_diagonal(pt, t, heads)
                    bdd = block_diagonal(pdt, t, heads)
                    qw, qdw = window(q, f, t), window(qd, f, t)
                    window_out(m_ref, t - base, dot(qw, bd[w]))
                    window_out(md_ref, t - base, dot(qdw, bd[w]) + dot(qw, bdd))
                for t, heads in windows:
                    ones = same_head(t, heads)
                    lanes = slice(128 * (t - base), 128 * (t - base) + 256)
                    m, md, p = m_ref[:, lanes], md_ref[:, lanes], window(po, f, t).astype(F32)
                    window_out(s1, t - base, dot((m * m).astype(BF16), ones))
                    window_out(s2, t - base, dot((m * md).astype(BF16), ones))
                    window_out(s3, t - base, dot((m * p).astype(BF16), ones))
                m, md, p = m_ref[...], md_ref[...], po[f, :, part].astype(F32)
                scale = lax.rsqrt(s1[...] * (1.0 / HD) + 1e-6)
                pulled = m * (scale * scale * scale) * (1.0 / HD)
                mbar[...] = (p * scale - pulled * s3[...]).astype(BF16)
                fl = m * scale
                tg = md * scale - pulled * s2[...]
                for s in targets:
                    at = 288 * s - 128 * base
                    out_send[s, 0, f] = pack(fl[:, at : at + 288]).astype(BF16)
                    out_send[s, 1, f] = pack(tg[:, at : at + 288]).astype(BF16)
                if early:

                    @pl.when(f == 0)
                    def _():
                        leave(0, 0, True)
                        leave(1, 0, True)

                pb = {}
                for w, (t, heads) in enumerate(windows):
                    mw = mbar[:, 128 * (t - base) : 128 * (t - base) + 256]
                    window_out(s1, t - base, dot(mw, bd[w], ((1,), (1,))))
                    compact_add(pb, t, heads, dot(window(q, f, t), mw, ((0,), (0,))))
                q_bar[i, f] = s1[...].astype(BF16)
                pb = [pb[j] for j in range(base, base + tiles)]
                pb.append(jnp.zeros((blocks.shape[1] - tiles * HD, 128), F32))
                blocks[f] = jnp.concatenate(pb, 0).astype(BF16)

            backward[i].start()

        def settle(i, last):
            windows, base, tiles, targets = PARTS[i]
            sc = backward[i].out
            part = slice(128 * base, 128 * (base + tiles))

            def tiles_of(f):
                rows = sc[f].astype(F32)
                return {base + j: rows[HD * j : HD * j + HD] for j in range(tiles)}

            @pl.loop(0, 2)
            def _(f):
                state = tiles_of(f)
                for s in targets:
                    wide = jnp.concatenate([state[2 * s + j] for j in range(3)], 1)[:, 32 * s : 32 * s + 288]
                    rest = [wide[24 * j : 24 * j + 24, 256:] for j in range(3)]
                    rest = jnp.concatenate(rest + [jnp.zeros((24, 32), F32)], 1)
                    parts = [wide[:, :128], wide[:, 128:256], rest, jnp.zeros((8, 128), F32)]
                    cot_send[s, f] = jnp.concatenate(parts, 0).astype(BF16)

            for s in targets:
                give_piece(place, cot_send, cot_recv, cot_s, cot_r, s)

            @pl.loop(0, 2)
            def _(f):
                state = tiles_of(f)
                for t, heads in windows:
                    b = block_diagonal(state, t, heads)
                    window_out(s1, t - base, dot(window(v, f, t), b, ((1,), (1,))))
                    window_out(s2, t - base, dot(window(k, f, t), b))
                total = adj[f] + dot(s1[...].astype(BF16), k_w[:, part], ((1,), (1,)))
                total = total + dot(s2[...].astype(BF16), v_w[:, part], ((1,), (1,)))
                if last:
                    adj_send[f] = total.astype(BF16)
                    pltpu.make_async_copy(adj_send.at[f], adj_out.at[f], adj_s.at[f]).start()
                else:
                    adj[f] = total

        forward[0].finish()

        @pl.when(place.y == 1)
        def _():
            mix(0, True)

        forward[1].pair_back()
        forward[1].finish()

        @pl.when(place.y == 0)
        def _():
            mix(1, True)
            mix(0, False)

        @pl.when(place.y == 1)
        def _():
            mix(1, False)

        backward[0].spread()
        backward[1].spread()
        leave(0, 1, True)
        for f in range(2):
            leave(0, f, False)
            leave(1, f, False)

        @pl.loop(0, 2)
        def _(f):
            total = None
            for i, (_, base, tiles, _) in enumerate(PARTS):
                part = slice(128 * base, 128 * (base + tiles))
                share = dot(q_bar[i, f], q_w[:, part], ((1,), (1,)))
                total = share if total is None else total + share
            adj[f] = total

        backward[0].group_sums()
        backward[1].group_sums()
        backward[0].send_back()
        backward[1].send_back()
        leave(1, 1, True)
        backward[0].pair_back()
        backward[0].finish()
        backward[1].pair_back()
        settle(0, False)
        backward[1].finish()
        settle(1, True)

    wide = pltpu.VMEM((TOK, 640), F32)
    pl.run_scoped(
        mixing,
        pltpu.VMEM((4, 256, 256), BF16),
        wide,
        wide,
        wide,
        wide,
        wide,
        pltpu.VMEM((TOK, 640), BF16),
        pltpu.VMEM((2, 2, TOK, 640), BF16),
        pltpu.VMEM((2, TOK, D), F32),
    )

    @pl.loop(0, nsp)
    def _(s):
        for x in range(2):
            for f in range(2):
                arrived(out_recv.at[s, x, f], out_r.at[s, x, f])
        arrived(cot_recv.at[s], cot_r.at[s])

    @pl.loop(1, nsp)
    def _(i):
        s, _ = place.mate(i)
        to_mate(place, po_send, po_recv, po_s, po_r, s).wait_send()
        init_move(i).wait_send()
        for x in range(2):
            for f in range(2):
                piece(place, out_send, out_recv, out_s, out_r, s, x, f).wait_send()
        piece(place, cot_send, cot_recv, cot_s, cot_r, s).wait_send()

    for f in range(2):
        pltpu.make_async_copy(adj_send.at[f], adj_out.at[f], adj_s.at[f]).wait()

    for scan in forward + backward:
        scan.drain()


def unpack_kernel(nsp, out_h, cot_h, adj_h, flow_h, tangent_h, cot_out_h, adj_out_h,
                  out, cot, adj, flow, tangent, cots, sems, done, adj_s):
    def loads(i):
        s, f = i // 2, i % 2
        return (
            pltpu.make_async_copy(out_h.at[s, :, f], out.at[i], sems.at[0, i]),
            pltpu.make_async_copy(cot_h.at[s, f], cot.at[i], sems.at[1, i]),
        )

    def stores(i):
        s, f = i // 2, i % 2
        return (
            pltpu.make_async_copy(flow.at[i], flow_h.at[f, s], done.at[0, i]),
            pltpu.make_async_copy(tangent.at[i], tangent_h.at[f, s], done.at[1, i]),
            pltpu.make_async_copy(cots.at[i], cot_out_h.at[f, s], done.at[2, i]),
        )

    take = pltpu.make_async_copy(adj_h, adj, adj_s.at[0])
    put = pltpu.make_async_copy(adj, adj_out_h, adj_s.at[1])
    take.start()
    for i in range(2 * nsp):
        for one in loads(i):
            one.start()
    take.wait()
    put.start()

    @pl.loop(0, 2 * nsp)
    def _(i):
        for one in loads(i):
            one.wait()
        for x, to in enumerate((flow, tangent)):
            to[i, :, 0:128] = out[i, x, 0:TOK]
            to[i, :, 128:256] = out[i, x, TOK : 2 * TOK]
            rest = out[i, x, 2 * TOK :]
            for j in range(4):
                to[i, 64 * j : 64 * j + 64, 256:288] = rest[:, 32 * j : 32 * j + 32]
        rows = cot[i].astype(F32)
        rest = rows[2 * HD : 2 * HD + 24]
        rest = jnp.concatenate([rest[:, 32 * j : 32 * j + 32] for j in range(3)], 0)
        lanes = jnp.concatenate([rows[:HD], rows[HD : 2 * HD], rest], 1)
        for j in range(4):
            cots[i, j] = lanes[:, HD * j : HD * j + HD]
        for one in stores(i):
            one.start()

    for i in range(2 * nsp):
        for one in stores(i):
            one.wait()
    put.wait()


def unpacked(nsp, out, cot, adj):
    heads = jax.ShapeDtypeStruct((2, nsp, TOK, D // 4), BF16)
    n = 2 * nsp
    return pl.pallas_call(
        functools.partial(unpack_kernel, nsp),
        out_shape=[
            heads,
            heads,
            jax.ShapeDtypeStruct((2, nsp, 4, HD, HD), F32),
            jax.ShapeDtypeStruct(adj.shape, BF16),
        ],
        in_specs=[anywhere()] * 3,
        out_specs=[anywhere()] * 4,
        scratch_shapes=[
            pltpu.VMEM((n, 2, PACK, 128), BF16),
            pltpu.VMEM((n, COT, 128), BF16),
            pltpu.VMEM(adj.shape, BF16),
            pltpu.VMEM((n, TOK, D // 4), BF16),
            pltpu.VMEM((n, TOK, D // 4), BF16),
            pltpu.VMEM((n, 4, HD, HD), F32),
            pltpu.SemaphoreType.DMA((2, n)),
            pltpu.SemaphoreType.DMA((3, n)),
            pltpu.SemaphoreType.DMA((2,)),
        ],
        compiler_params=pltpu.CompilerParams(vmem_limit_bytes=VMEM_LIMIT),
        name="unpack",
    )(out, cot, adj)


def on_device(shape, video, conv_weight, embed_weight, q_weight, k_weight, v_weight, initial_state, probe_in, probe_out):
    ntm, nsp = shape
    dma = pltpu.SemaphoreType.DMA
    rows = pltpu.VMEM((2, TOK, D), BF16)
    square = pltpu.VMEM((D, D), BF16)
    packed = pltpu.VMEM((nsp, 2, PACK, 128), BF16)
    four = dma((nsp,))
    out, cot, adjoint = pl.pallas_call(
        functools.partial(kernel, shape),
        out_shape=[
            jax.ShapeDtypeStruct((nsp, 2, 2, PACK, 128), BF16),
            jax.ShapeDtypeStruct((nsp, 2, COT, 128), BF16),
            jax.ShapeDtypeStruct((2, TOK, D), BF16),
        ],
        in_specs=[anywhere()] * 6 + [vmem()] + [anywhere()] * 2,
        out_specs=[anywhere()] * 3,
        scratch_shapes=[
            pltpu.VMEM((4, TOK + 64, C), BF16),
            square,
            square,
            square,
            rows,
            rows,
            rows,
            rows,
            pltpu.VMEM((2 * TOK, D), BF16),
            packed,
            packed,
            rows,
            pltpu.VMEM((HD, 384), F32),
            pltpu.VMEM((nsp, HD, 384), F32),
            pltpu.VMEM((HD, D), F32),
            pltpu.VMEM((nsp, 2, 2, PACK, 128), BF16),
            pltpu.VMEM((nsp, 2, COT, 128), BF16),
            rows,
            dma((5,)),
            dma((5,)),
            dma((7,)),
            dma,
            four,
            four,
            four,
            four,
            dma((nsp, 2, 2)),
            dma((nsp, 2, 2)),
            four,
            four,
            dma((2,)),
        ]
        + scan_scratch(shape, 5 * 2 * HD) * 2
        + scan_scratch(shape, 5 * HD) * 2,
        compiler_params=pltpu.CompilerParams(
            collective_id=0, has_side_effects=True, vmem_limit_bytes=VMEM_LIMIT
        ),
        name="flow_layer",
    )(
        video.reshape(2, TOK, C),
        conv_weight.reshape(9, 3 * C, C),
        embed_weight,
        q_weight,
        k_weight,
        v_weight,
        initial_state,
        probe_in.reshape(2 * TOK, D),
        probe_out.reshape(2, 4 * TOK, D // 4),
    )
    flow, tangent, cot, adjoint = unpacked(nsp, out, cot, adjoint)
    full = (2, 32, 32, D // 4)
    return (
        flow.reshape(full),
        tangent.reshape(full),
        adjoint.reshape(2, 8, 32, D),
        cot.reshape(8, 4, HD, HD),
    )


def solution(mesh):
    by_rows = P("tm", "space", None, None)
    by_heads = P("tm", None, None, "space")
    return jax.shard_map(
        functools.partial(on_device, (mesh.shape["tm"], mesh.shape["space"])),
        mesh=mesh,
        in_specs=(by_rows, P(), P(), P(), P(), P(), P("space", None, None), by_rows, by_heads),
        out_specs=(by_heads, by_heads, by_rows, by_rows),
        check_vma=False,
    )
```

```python
import functools

import jax
import jax.numpy as jnp
from jax import lax
from jax.experimental import pallas as pl
from jax.experimental.pallas import tpu as pltpu
from jax.sharding import PartitionSpec as P

MESH = pl.DeviceIdType.MESH
F32 = jnp.float32
BF16 = jnp.bfloat16
D = 1152
HEADS = 16
HD = 72
C = 384
TOK = 256
TILES = D // 128
WINDOWS = (
    (0, (0, 1, 2)),
    (1, (3, 4)),
    (2, (5, 6)),
    (3, (7,)),
    (4, (8, 9)),
    (5, (10, 11)),
    (6, (12, 13)),
    (7, (14, 15)),
)
VMEM_LIMIT = 60 * 1024 * 1024


PARTS = ((WINDOWS[:4], 0, 5, (0, 1)), (WINDOWS[4:], 4, 5, (2, 3)))
COT = 176
PACK = 2 * TOK + TOK // 4


def vmem():
    return pl.BlockSpec(memory_space=pltpu.VMEM)


def anywhere():
    return pl.BlockSpec(memory_space=pl.ANY)


def dot(a, b, dims=((1,), (0,))):
    return lax.dot_general(a, b, (dims, ((), ())), preferred_element_type=F32)


def head_mask(h, tile, rows):
    lane = lax.broadcasted_iota(jnp.int32, (rows, 128), 1) + 128 * tile
    return (lane >= HD * h) & (lane < HD * (h + 1))


def compact_add(tiles, t, heads, g):
    for half in range(2):
        j = t + half
        for h in heads:
            if HD * h < 128 * (j + 1) and HD * (h + 1) > 128 * j:
                r = HD * h - 128 * t
                piece = g[r : r + HD, 128 * half : 128 * half + 128]
                piece = jnp.where(head_mask(h, j, HD), piece, 0.0)
                tiles[j] = tiles[j] + piece if j in tiles else piece


def block_diagonal(tiles, t, heads):
    halves = []
    for half in range(2):
        j = t + half
        parts = []
        at = 0
        for h in heads:
            r = HD * h - 128 * t
            if r > at:
                parts.append(jnp.zeros((r - at, 128), F32))
            if HD * h < 128 * (j + 1) and HD * (h + 1) > 128 * j:
                parts.append(jnp.where(head_mask(h, j, HD), tiles[j], 0.0))
            else:
                parts.append(jnp.zeros((HD, 128), F32))
            at = r + HD
        if at < 256:
            parts.append(jnp.zeros((256 - at, 128), F32))
        halves.append(jnp.concatenate(parts, 0))
    return jnp.concatenate(halves, 1).astype(BF16)


def same_head(t, heads):
    row = lax.broadcasted_iota(jnp.int32, (256, 256), 0) + 128 * t
    col = lax.broadcasted_iota(jnp.int32, (256, 256), 1) + 128 * t
    ok = None
    for h in heads:
        low, high = HD * h, HD * (h + 1)
        both = (row >= low) & (row < high) & (col >= low) & (col < high)
        ok = both if ok is None else ok | both
    return jnp.where(ok, 1.0, 0.0).astype(BF16)


def window_out(ref, t, value):
    if t == 0:
        ref[:, 0:256] = value
    else:
        ref[:, 128 * t : 128 * t + 128] = ref[:, 128 * t : 128 * t + 128] + value[:, :128]
        ref[:, 128 * t + 128 : 128 * t + 256] = value[:, 128:]


def pack(x):
    rest = x[:, 256:]
    rest = jnp.concatenate([rest[64 * i : 64 * i + 64] for i in range(4)], 1)
    return jnp.concatenate([x[:, :128], x[:, 128:256], rest], 0)


def unpack(x):
    rest = jnp.concatenate([x[2 * TOK :, 32 * i : 32 * i + 32] for i in range(4)], 0)
    return jnp.concatenate([x[:TOK], x[TOK : 2 * TOK], rest], 1)


def arrived(ref, sem):
    pltpu.make_async_copy(ref, ref, sem).wait()


def window(ref, f, t):
    return ref[f, :, 128 * t : 128 * t + 256]


class Place:
    def __init__(self, ntm, nsp):
        self.ntm, self.nsp = ntm, nsp
        self.nz, self.ny = min(4, ntm), nsp // 2
        self.tm, self.sp = lax.axis_index("tm"), lax.axis_index("space")
        self.peers, self.groups = self.nz * self.ny, ntm // self.nz
        self.group, self.z = self.tm // self.nz, self.tm % self.nz
        self.y, self.core = self.sp // 2, self.sp % 2
        self.me = self.z * self.ny + self.y
        self.twin = (self.tm, self.sp + 1 - 2 * self.core)

    def peer(self, k):
        p = lax.rem(self.me + k, self.peers)
        return p, (self.group * self.nz + p // self.ny, 2 * (p % self.ny) + self.core)

    def other(self, k):
        g = lax.rem(self.group + k, self.groups)
        return g, (g * self.nz + self.z, self.sp)

    def mate(self, k):
        s = lax.rem(self.sp + k, self.nsp)
        return s, (self.tm, s)


def remote(src, dst, send_sem, recv_sem, device):
    return pltpu.make_async_remote_copy(
        src_ref=src,
        dst_ref=dst,
        send_sem=send_sem,
        recv_sem=recv_sem,
        device_id=device,
        device_id_type=MESH,
    )


class Scan:
    def __init__(self, place, reverse, rows, blocks, out, pair, chip, got, sums, answer, back, theirs, totals, total,
                 s0, r0, s1, r1, s2, r2, s3, r3, s4, r4):
        self.place, self.reverse, self.rows = place, reverse, rows
        self.blocks, self.out, self.pair, self.chip, self.got = blocks, out, pair, chip, got
        self.sums, self.answer, self.back, self.theirs = sums, answer, back, theirs
        self.totals, self.total = totals, total
        self.s0, self.r0, self.s1, self.r1, self.s2, self.r2 = s0, r0, s1, r1, s2, r2
        self.s3, self.r3, self.s4, self.r4 = s3, r3, s4, r4
        self.share = got.shape[2]

    def half(self, c):
        n = self.chip.shape[1]
        return pl.ds(pl.multiple_of(c * n, n), n)

    def part(self, p):
        return pl.ds(pl.multiple_of(p * self.share, self.share), self.share)

    def used(self, p):
        return (self.place.core * self.place.peers + p) * self.share < self.rows

    def swap(self):
        return remote(
            self.blocks.at[:, self.half(1 - self.place.core)], self.pair, self.s0, self.r0, self.place.twin
        )

    def first(self, k):
        p, device = self.place.peer(k)
        me = self.place.me
        return remote(self.chip.at[:, self.part(p)], self.got.at[me], self.s1.at[p], self.r1.at[me], device)

    def second(self, k):
        g, device = self.place.other(k)
        mine = self.place.group
        return remote(self.total, self.totals.at[mine], self.s2.at[g], self.r2.at[mine], device)

    def third(self, k):
        p, device = self.place.peer(k)
        me = self.place.me
        return remote(self.answer.at[p], self.back.at[:, self.part(me)], self.s3.at[p], self.r3.at[me], device)

    def fourth(self):
        return remote(self.theirs, self.out.at[:, self.half(self.place.core)], self.s4, self.r4, self.place.twin)

    def start(self):
        self.swap().start()

    def spread(self):
        arrived(self.pair, self.r0)
        own = self.blocks[:, self.half(self.place.core)].astype(F32)
        self.chip[...] = (own + self.pair[...].astype(F32)).astype(BF16)

        @pl.loop(1, self.place.peers)
        def _(k):
            @pl.when(self.used(self.place.peer(k)[0]))
            def _():
                self.first(k).start()

    def group_sums(self):
        @pl.when(self.used(self.place.me))
        def _():
            self.got[self.place.me] = self.chip[:, self.part(self.place.me)]

            @pl.loop(1, self.place.peers)
            def _(k):
                p, _ = self.place.peer(k)
                arrived(self.got.at[p], self.r1.at[p])

            ny = self.place.ny
            running = jnp.zeros((self.share, 128), F32)
            order = [(zz * ny + y, f) for zz in range(self.place.nz) for f in range(2) for y in range(ny)]
            for p, f in reversed(order) if self.reverse else order:
                self.sums[p, f] = running
                running = running + self.got[p, f].astype(F32)
            self.total[...] = running.astype(BF16)

            @pl.loop(1, self.place.groups)
            def _(k):
                self.second(k).start()

            self.totals[self.place.group] = jnp.zeros((self.share, 128), BF16)

    def send_back(self):
        @pl.when(self.used(self.place.me))
        def _():
            @pl.loop(1, self.place.groups)
            def _(k):
                g, _ = self.place.other(k)
                arrived(self.totals.at[g], self.r2.at[g])

            group = self.place.group
            before = jnp.zeros((self.share, 128), F32)
            for g in range(self.place.groups):
                counts = g > group if self.reverse else g < group
                before = before + jnp.where(counts, self.totals[g].astype(F32), 0.0)
            for p in range(self.place.peers):
                self.answer[p] = (self.sums[p] + before[None]).astype(BF16)

            @pl.loop(1, self.place.peers)
            def _(k):
                self.third(k).start()

            self.back[:, self.part(self.place.me)] = self.answer[self.place.me]

    def pair_back(self):
        @pl.loop(1, self.place.peers)
        def _(k):
            p, _ = self.place.peer(k)

            @pl.when(self.used(p))
            def _():
                arrived(self.answer.at[p], self.r3.at[p])

        core = self.place.core
        here = self.half(core)
        before = self.back[...].astype(F32)
        own, pair = self.blocks[:, here].astype(F32), self.pair[...].astype(F32)
        after = core == (0 if self.reverse else 1)
        self.theirs[...] = (before + pair + jnp.where(after, 0.0, own)).astype(BF16)
        self.fourth().start()
        self.out[:, here] = (before + own + jnp.where(after, pair, 0.0)).astype(BF16)

    def finish(self):
        arrived(self.theirs, self.r4)

    def drain(self):
        self.swap().wait_send()
        self.fourth().wait_send()

        @pl.loop(1, self.place.peers)
        def _(k):
            @pl.when(self.used(self.place.peer(k)[0]))
            def _():
                self.first(k).wait_send()

        @pl.when(self.used(self.place.me))
        def _():
            @pl.loop(1, self.place.peers)
            def _(k):
                self.third(k).wait_send()

            @pl.loop(1, self.place.groups)
            def _(k):
                self.second(k).wait_send()


def scan_share(shape, rows):
    return -(-rows // (16 * 2 * min(4, shape[0]) * (shape[1] // 2))) * 16


def scan_scratch(shape, rows):
    ntm, nsp = shape
    nz = min(4, ntm)
    peers, groups = nz * (nsp // 2), ntm // nz
    share = scan_share(shape, rows)
    dma = pltpu.SemaphoreType.DMA
    full, half = pltpu.VMEM((2, 2 * peers * share, 128), BF16), pltpu.VMEM((2, peers * share, 128), BF16)
    shares = pltpu.VMEM((peers, 2, share, 128), BF16)
    return [
        full,
        full,
        half,
        half,
        shares,
        pltpu.VMEM((peers, 2, share, 128), F32),
        shares,
        half,
        half,
        pltpu.VMEM((groups, share, 128), BF16),
        pltpu.VMEM((share, 128), BF16),
        dma,
        dma,
        dma((peers,)),
        dma((peers,)),
        dma((groups,)),
        dma((groups,)),
        dma((peers,)),
        dma((peers,)),
        dma,
        dma,
    ]


def to_mate(place, send, recv, send_sem, recv_sem, s):
    me = place.sp
    return remote(send.at[s], recv.at[me], send_sem.at[s], recv_sem.at[me], (place.tm, s))


def give(place, send, recv, send_sem, recv_sem, targets):
    for s in targets:

        @pl.when(place.sp != s)
        def _():
            to_mate(place, send, recv, send_sem, recv_sem, s).start()

        @pl.when(place.sp == s)
        def _():
            recv[s] = send[s]


def piece(place, send, recv, send_sem, recv_sem, s, *at):
    me = (place.sp, *at)
    there = (s, *at)
    return remote(send.at[there], recv.at[me], send_sem.at[there], recv_sem.at[me], (place.tm, s))


def give_piece(place, send, recv, send_sem, recv_sem, s, *at):
    @pl.when(place.sp != s)
    def _():
        piece(place, send, recv, send_sem, recv_sem, s, *at).start()

    @pl.when(place.sp == s)
    def _():
        there = (s, *at)
        pltpu.make_async_copy(send.at[there], recv.at[there], recv_sem.at[there]).start()


def kernel(
    shape,
    video, conv_h, embed_h, q_h, k_h, v_h, init_in, probe_h, po_h,
    out_recv, cot_recv, adj_out,
    slab, q_w, k_w, v_w, q, qd, k, v, latent, po_send, po_recv, po, init_send, init_recv, init,
    out_send, cot_send, adj_send,
    halo_send, halo_recv, load, keep_sem, po_s, po_r, init_s, init_r, out_s, out_r, cot_s, cot_r, adj_s,
    *scans,
):
    ntm, nsp = shape
    place = Place(ntm, nsp)
    tm, sp = place.tm, place.sp
    n = len(scans) // 4
    forward = [Scan(place, False, 5 * 2 * HD, *scans[i * n : i * n + n]) for i in range(2)]
    backward = [Scan(place, True, 5 * HD, *scans[i * n : i * n + n]) for i in range(2, 4)]

    later, earlier = tm + 1 < ntm, tm > 0
    down, up = sp + 1 < nsp, sp > 0
    last, first = pl.ds(TOK - 32, 32), pl.ds(0, 32)
    top, mid, bottom = pl.ds(0, 32), pl.ds(32, TOK), pl.ds(32 + TOK, 32)
    whole = pl.ds(0, TOK)
    prev, own = pl.ds(0, 2), pl.ds(2, 2)
    moves = (
        (down, up, last, own, top, (tm, sp + 1), (tm, sp - 1)),
        (up, down, first, own, bottom, (tm, sp - 1), (tm, sp + 1)),
        (later, earlier, whole, prev, mid, (tm + 1, sp), (tm - 1, sp)),
        (down & later, up & earlier, last, prev, top, (tm + 1, sp + 1), (tm - 1, sp - 1)),
        (up & later, down & earlier, first, prev, bottom, (tm + 1, sp - 1), (tm - 1, sp + 1)),
    )

    barrier = pltpu.get_barrier_semaphore()
    for _, may_recv, _, _, _, _, source in moves:

        @pl.when(may_recv)
        def _():
            pl.semaphore_signal(barrier, inc=1, device_id=source, device_id_type=MESH)

    def greet(count, device_of):
        @pl.loop(1, count)
        def _(i):
            pl.semaphore_signal(barrier, inc=1, device_id=device_of(i)[1], device_id_type=MESH)

    greet(place.groups, place.other)
    greet(place.peers, place.peer)
    greet(nsp, place.mate)

    def encode(conv_w, embed_w, probe, po_i, taps, acc, kd, vd):
        loads = [
            pltpu.make_async_copy(src, dst, load.at[i])
            for i, (src, dst) in enumerate(
                (
                    (po_h, po_i),
                    (probe_h, probe),
                    (k_h, k_w),
                    (v_h, v_w),
                    (conv_h, conv_w),
                    (q_h, q_w),
                    (embed_h, embed_w),
                )
            )
        ]
        keep = pltpu.make_async_copy(video, slab.at[own, mid], keep_sem)
        keep.start()
        for one in loads:
            one.start()

        for _, may_recv, _, frames, there, _, _ in moves:

            @pl.when(jnp.logical_not(may_recv))
            def _():
                slab[frames, there] = jnp.zeros((2, there.size, C), BF16)

        heads = [init_in[j] for j in range(4)]
        init_send[...] = jnp.concatenate(heads + [jnp.zeros((HD, 96), F32)], 1)
        for scan in forward:
            at = 5 * 2 * HD
            scan.blocks[:, at:, :] = jnp.zeros((2, scan.blocks.shape[1] - at, 128), BF16)

        greeted = place.groups + place.peers + nsp - 3
        pl.semaphore_wait(barrier, sum(m[0].astype(jnp.int32) for m in moves) + greeted)

        copies = []
        for i, (may_send, _, rows, frames, there, target, _) in enumerate(moves):
            copy = remote(video.at[:, rows], slab.at[frames, there], halo_send.at[i], halo_recv.at[i], target)
            copies.append(copy)

            @pl.when(may_send)
            def _():
                copy.start()

        loads[0].wait()
        for s in range(nsp):
            for f in range(2):
                po_send[s, f] = pack(po_i[f, TOK * s : TOK * s + TOK, :].astype(F32)).astype(BF16)

        col = lax.broadcasted_iota(jnp.int32, (TOK + 64, C), 0) % 32

        def build(f):
            here = slab[f].astype(F32)
            left = jnp.where(col == 0, 0.0, pltpu.roll(here, 1, 0))
            right = jnp.where(col == 31, 0.0, pltpu.roll(here, TOK + 63, 0))
            taps[f, :, 0:C] = left.astype(BF16)
            taps[f, :, C : 2 * C] = slab[f]
            taps[f, :, 2 * C : 3 * C] = right.astype(BF16)

        def halo_wait(i):
            @pl.when(moves[i][1])
            def _():
                copies[i].wait_recv()

        def convolve(a, out):
            @pl.loop(0, 3)
            def _(b):
                rows = pl.ds(pl.multiple_of(b * 32, 32), TOK)
                x = taps[a + out[0] : a + out[-1] + 1, rows, :].reshape(len(out) * TOK, 3 * C)
                here = slice(out[0] * TOK, (out[-1] + 1) * TOK)
                acc[here] += dot(x, conv_w[3 * a + b])

        acc[...] = jnp.zeros_like(acc)
        keep.wait()
        halo_wait(0)
        halo_wait(1)
        build(2)
        build(3)

        loads[1].wait()
        direction = probe[...].astype(F32).astype(BF16)
        for one, weight, out in zip(loads[2:4], (k_w, v_w), (kd, vd)):
            one.wait()
            out[...] = dot(direction, weight[...]).astype(BF16).reshape(2, TOK, D)

        loads[4].wait()
        convolve(2, (0, 1))
        convolve(1, (1,))
        loads[5].wait()
        qd[...] = dot(direction, q_w[...]).astype(BF16).reshape(2, TOK, D)
        halo_wait(2)
        halo_wait(3)
        halo_wait(4)

        @pl.loop(1, nsp)
        def _(i):
            init_move(i).start()

        init_recv[sp] = init_send[...]
        give(place, po_send, po_recv, po_s, po_r, range(nsp))
        build(0)
        build(1)
        convolve(1, (0,))
        convolve(0, (0, 1))

        u = acc[...]
        active = (u / (1.0 + jnp.exp(-u))).astype(BF16)
        loads[6].wait()
        latent[...] = dot(active, embed_w[...]).astype(BF16)
        for weight, out in zip((k_w, v_w), (k, v)):
            out[...] = dot(latent[...], weight[...]).astype(BF16).reshape(2, TOK, D)

        for scan, (windows, base, tiles, _) in zip(forward, PARTS):

            @pl.loop(0, 2)
            def _(f):
                st, sd = {}, {}
                over = ((0,), (0,))
                for t, heads in windows:
                    kw, vw = window(k, f, t), window(v, f, t)
                    compact_add(st, t, heads, dot(kw, vw, over))
                    both = dot(window(kd, f, t), vw, over) + dot(kw, window(vd, f, t), over)
                    compact_add(sd, t, heads, both)
                for j in range(tiles):
                    both = jnp.concatenate([st[base + j], sd[base + j]], 0)
                    scan.blocks[f, 144 * j : 144 * j + 144, :] = both.astype(BF16)

            scan.start()

        forward[0].spread()
        q[...] = dot(latent[...], q_w[...]).astype(BF16).reshape(2, TOK, D)
        for copy, (may_send, *_) in zip(copies, moves):

            @pl.when(may_send)
            def _():
                copy.wait_send()

    def init_move(i):
        _, device = place.mate(i)
        return remote(init_send, init_recv.at[sp], init_s.at[i], init_r.at[sp], device)

    pl.run_scoped(
        encode,
        pltpu.VMEM((9, 3 * C, C), BF16),
        pltpu.VMEM((C, D), BF16),
        pltpu.VMEM((2 * TOK, D), jnp.int32),
        pltpu.VMEM((2, 4 * TOK, D // 4), jnp.int32),
        pltpu.VMEM((4, TOK + 64, 3 * C), BF16),
        pltpu.VMEM((2 * TOK, C), F32),
        pltpu.VMEM((2, TOK, D), BF16),
        pltpu.VMEM((2, TOK, D), BF16),
    )

    forward[1].spread()
    forward[0].group_sums()
    forward[1].group_sums()

    @pl.loop(1, nsp)
    def _(i):
        s, _ = place.mate(i)
        arrived(po_recv.at[s], po_r.at[s])
        arrived(init_recv.at[s], init_r.at[s])

    for s in range(nsp):
        init[:, 288 * s : 288 * s + 288] = init_recv[s, :, 0:288]
        for f in range(2):
            po[f, :, 288 * s : 288 * s + 288] = unpack(po_recv[s, f].astype(F32)).astype(BF16)

    forward[0].send_back()
    forward[1].send_back()
    forward[0].pair_back()

    def mixing(bd, m_ref, md_ref, s1, s2, s3, mbar, q_bar, adj):
        def leave(x, f, across):
            for s in range(nsp):
                there = place.y != s // 2

                @pl.when(there if across else jnp.logical_not(there))
                def _():
                    give_piece(place, out_send, out_recv, out_s, out_r, s, x, f)

        def mix(i, early):
            windows, base, tiles, targets = PARTS[i]
            prefix, blocks = forward[i].out, backward[i].blocks
            part = slice(128 * base, 128 * (base + tiles))

            @pl.loop(0, 2)
            def _(f):
                pt, pdt = {}, {}
                for j in range(base, base + tiles):
                    both = prefix[f, 144 * (j - base) : 144 * (j - base) + 144, :].astype(F32)
                    pt[j] = both[:HD] + init[:, 128 * j : 128 * j + 128]
                    pdt[j] = both[HD:]
                for w, (t, heads) in enumerate(windows):
                    bd[w] = block_diagonal(pt, t, heads)
                    bdd = block_diagonal(pdt, t, heads)
                    qw, qdw = window(q, f, t), window(qd, f, t)
                    window_out(m_ref, t - base, dot(qw, bd[w]))
                    window_out(md_ref, t - base, dot(qdw, bd[w]) + dot(qw, bdd))
                for t, heads in windows:
                    ones = same_head(t, heads)
                    lanes = slice(128 * (t - base), 128 * (t - base) + 256)
                    m, md, p = m_ref[:, lanes], md_ref[:, lanes], window(po, f, t).astype(F32)
                    window_out(s1, t - base, dot((m * m).astype(BF16), ones))
                    window_out(s2, t - base, dot((m * md).astype(BF16), ones))
                    window_out(s3, t - base, dot((m * p).astype(BF16), ones))
                m, md, p = m_ref[...], md_ref[...], po[f, :, part].astype(F32)
                scale = lax.rsqrt(s1[...] * (1.0 / HD) + 1e-6)
                pulled = m * (scale * scale * scale) * (1.0 / HD)
                mbar[...] = (p * scale - pulled * s3[...]).astype(BF16)
                fl = m * scale
                tg = md * scale - pulled * s2[...]
                for s in targets:
                    at = 288 * s - 128 * base
                    out_send[s, 0, f] = pack(fl[:, at : at + 288]).astype(BF16)
                    out_send[s, 1, f] = pack(tg[:, at : at + 288]).astype(BF16)
                if early:

                    @pl.when(f == 0)
                    def _():
                        leave(0, 0, True)

                pb = {}
                for w, (t, heads) in enumerate(windows):
                    mw = mbar[:, 128 * (t - base) : 128 * (t - base) + 256]
                    window_out(s1, t - base, dot(mw, bd[w], ((1,), (1,))))
                    compact_add(pb, t, heads, dot(window(q, f, t), mw, ((0,), (0,))))
                q_bar[i, f] = s1[...].astype(BF16)
                pb = [pb[j] for j in range(base, base + tiles)]
                pb.append(jnp.zeros((blocks.shape[1] - tiles * HD, 128), F32))
                blocks[f] = jnp.concatenate(pb, 0).astype(BF16)

            backward[i].start()

        def settle(i, last):
            windows, base, tiles, targets = PARTS[i]
            sc = backward[i].out
            part = slice(128 * base, 128 * (base + tiles))

            def tiles_of(f):
                rows = sc[f].astype(F32)
                return {base + j: rows[HD * j : HD * j + HD] for j in range(tiles)}

            @pl.loop(0, 2)
            def _(f):
                state = tiles_of(f)
                for s in targets:
                    wide = jnp.concatenate([state[2 * s + j] for j in range(3)], 1)[:, 32 * s : 32 * s + 288]
                    rest = [wide[24 * j : 24 * j + 24, 256:] for j in range(3)]
                    rest = jnp.concatenate(rest + [jnp.zeros((24, 32), F32)], 1)
                    parts = [wide[:, :128], wide[:, 128:256], rest, jnp.zeros((8, 128), F32)]
                    cot_send[s, f] = jnp.concatenate(parts, 0).astype(BF16)

            for s in targets:
                give_piece(place, cot_send, cot_recv, cot_s, cot_r, s)

            @pl.loop(0, 2)
            def _(f):
                state = tiles_of(f)
                for t, heads in windows:
                    b = block_diagonal(state, t, heads)
                    window_out(s1, t - base, dot(window(v, f, t), b, ((1,), (1,))))
                    window_out(s2, t - base, dot(window(k, f, t), b))
                total = adj[f] + dot(s1[...].astype(BF16), k_w[:, part], ((1,), (1,)))
                total = total + dot(s2[...].astype(BF16), v_w[:, part], ((1,), (1,)))
                if last:
                    adj_send[f] = total.astype(BF16)
                    pltpu.make_async_copy(adj_send.at[f], adj_out.at[f], adj_s.at[f]).start()
                else:
                    adj[f] = total

        forward[0].finish()

        @pl.when(place.y == 1)
        def _():
            mix(0, True)

        forward[1].pair_back()
        forward[1].finish()

        @pl.when(place.y == 0)
        def _():
            mix(1, True)
            mix(0, False)

        @pl.when(place.y == 1)
        def _():
            mix(1, False)

        backward[0].spread()
        backward[1].spread()
        leave(1, 0, True)
        for f in range(2):
            leave(0, f, False)
            leave(1, f, False)

        @pl.loop(0, 2)
        def _(f):
            total = None
            for i, (_, base, tiles, _) in enumerate(PARTS):
                part = slice(128 * base, 128 * (base + tiles))
                share = dot(q_bar[i, f], q_w[:, part], ((1,), (1,)))
                total = share if total is None else total + share
            adj[f] = total

        backward[0].group_sums()
        backward[1].group_sums()
        backward[0].send_back()
        backward[1].send_back()
        leave(0, 1, True)
        leave(1, 1, True)
        backward[0].pair_back()
        backward[0].finish()
        backward[1].pair_back()
        settle(0, False)
        backward[1].finish()
        settle(1, True)

    wide = pltpu.VMEM((TOK, 640), F32)
    pl.run_scoped(
        mixing,
        pltpu.VMEM((4, 256, 256), BF16),
        wide,
        wide,
        wide,
        wide,
        wide,
        pltpu.VMEM((TOK, 640), BF16),
        pltpu.VMEM((2, 2, TOK, 640), BF16),
        pltpu.VMEM((2, TOK, D), F32),
    )

    @pl.loop(0, nsp)
    def _(s):
        for x in range(2):
            for f in range(2):
                arrived(out_recv.at[s, x, f], out_r.at[s, x, f])
        arrived(cot_recv.at[s], cot_r.at[s])

    @pl.loop(1, nsp)
    def _(i):
        s, _ = place.mate(i)
        to_mate(place, po_send, po_recv, po_s, po_r, s).wait_send()
        init_move(i).wait_send()
        for x in range(2):
            for f in range(2):
                piece(place, out_send, out_recv, out_s, out_r, s, x, f).wait_send()
        piece(place, cot_send, cot_recv, cot_s, cot_r, s).wait_send()

    for f in range(2):
        pltpu.make_async_copy(adj_send.at[f], adj_out.at[f], adj_s.at[f]).wait()

    for scan in forward + backward:
        scan.drain()


def unpack_kernel(nsp, out_h, cot_h, adj_h, flow_h, tangent_h, cot_out_h, adj_out_h,
                  out, cot, adj, flow, tangent, cots, sems, done, adj_s):
    def loads(i):
        s, f = i // 2, i % 2
        return (
            pltpu.make_async_copy(out_h.at[s, :, f], out.at[i], sems.at[0, i]),
            pltpu.make_async_copy(cot_h.at[s, f], cot.at[i], sems.at[1, i]),
        )

    def stores(i):
        s, f = i // 2, i % 2
        return (
            pltpu.make_async_copy(flow.at[i], flow_h.at[f, s], done.at[0, i]),
            pltpu.make_async_copy(tangent.at[i], tangent_h.at[f, s], done.at[1, i]),
            pltpu.make_async_copy(cots.at[i], cot_out_h.at[f, s], done.at[2, i]),
        )

    take = pltpu.make_async_copy(adj_h, adj, adj_s.at[0])
    put = pltpu.make_async_copy(adj, adj_out_h, adj_s.at[1])
    take.start()
    for i in range(2 * nsp):
        for one in loads(i):
            one.start()
    take.wait()
    put.start()

    @pl.loop(0, 2 * nsp)
    def _(i):
        for one in loads(i):
            one.wait()
        for x, to in enumerate((flow, tangent)):
            to[i, :, 0:128] = out[i, x, 0:TOK]
            to[i, :, 128:256] = out[i, x, TOK : 2 * TOK]
            rest = out[i, x, 2 * TOK :]
            for j in range(4):
                to[i, 64 * j : 64 * j + 64, 256:288] = rest[:, 32 * j : 32 * j + 32]
        rows = cot[i].astype(F32)
        rest = rows[2 * HD : 2 * HD + 24]
        rest = jnp.concatenate([rest[:, 32 * j : 32 * j + 32] for j in range(3)], 0)
        lanes = jnp.concatenate([rows[:HD], rows[HD : 2 * HD], rest], 1)
        for j in range(4):
            cots[i, j] = lanes[:, HD * j : HD * j + HD]
        for one in stores(i):
            one.start()

    for i in range(2 * nsp):
        for one in stores(i):
            one.wait()
    put.wait()


def unpacked(nsp, out, cot, adj):
    heads = jax.ShapeDtypeStruct((2, nsp, TOK, D // 4), BF16)
    n = 2 * nsp
    return pl.pallas_call(
        functools.partial(unpack_kernel, nsp),
        out_shape=[
            heads,
            heads,
            jax.ShapeDtypeStruct((2, nsp, 4, HD, HD), F32),
            jax.ShapeDtypeStruct(adj.shape, BF16),
        ],
        in_specs=[anywhere()] * 3,
        out_specs=[anywhere()] * 4,
        scratch_shapes=[
            pltpu.VMEM((n, 2, PACK, 128), BF16),
            pltpu.VMEM((n, COT, 128), BF16),
            pltpu.VMEM(adj.shape, BF16),
            pltpu.VMEM((n, TOK, D // 4), BF16),
            pltpu.VMEM((n, TOK, D // 4), BF16),
            pltpu.VMEM((n, 4, HD, HD), F32),
            pltpu.SemaphoreType.DMA((2, n)),
            pltpu.SemaphoreType.DMA((3, n)),
            pltpu.SemaphoreType.DMA((2,)),
        ],
        compiler_params=pltpu.CompilerParams(vmem_limit_bytes=VMEM_LIMIT),
        name="unpack",
    )(out, cot, adj)


def on_device(shape, video, conv_weight, embed_weight, q_weight, k_weight, v_weight, initial_state, probe_in, probe_out):
    ntm, nsp = shape
    dma = pltpu.SemaphoreType.DMA
    rows = pltpu.VMEM((2, TOK, D), BF16)
    square = pltpu.VMEM((D, D), BF16)
    packed = pltpu.VMEM((nsp, 2, PACK, 128), BF16)
    four = dma((nsp,))
    out, cot, adjoint = pl.pallas_call(
        functools.partial(kernel, shape),
        out_shape=[
            jax.ShapeDtypeStruct((nsp, 2, 2, PACK, 128), BF16),
            jax.ShapeDtypeStruct((nsp, 2, COT, 128), BF16),
            jax.ShapeDtypeStruct((2, TOK, D), BF16),
        ],
        in_specs=[anywhere()] * 6 + [vmem()] + [anywhere()] * 2,
        out_specs=[anywhere()] * 3,
        scratch_shapes=[
            pltpu.VMEM((4, TOK + 64, C), BF16),
            square,
            square,
            square,
            rows,
            rows,
            rows,
            rows,
            pltpu.VMEM((2 * TOK, D), BF16),
            packed,
            packed,
            rows,
            pltpu.VMEM((HD, 384), F32),
            pltpu.VMEM((nsp, HD, 384), F32),
            pltpu.VMEM((HD, D), F32),
            pltpu.VMEM((nsp, 2, 2, PACK, 128), BF16),
            pltpu.VMEM((nsp, 2, COT, 128), BF16),
            rows,
            dma((5,)),
            dma((5,)),
            dma((7,)),
            dma,
            four,
            four,
            four,
            four,
            dma((nsp, 2, 2)),
            dma((nsp, 2, 2)),
            four,
            four,
            dma((2,)),
        ]
        + scan_scratch(shape, 5 * 2 * HD) * 2
        + scan_scratch(shape, 5 * HD) * 2,
        compiler_params=pltpu.CompilerParams(
            collective_id=0, has_side_effects=True, vmem_limit_bytes=VMEM_LIMIT
        ),
        name="flow_layer",
    )(
        video.reshape(2, TOK, C),
        conv_weight.reshape(9, 3 * C, C),
        embed_weight,
        q_weight,
        k_weight,
        v_weight,
        initial_state,
        probe_in.reshape(2 * TOK, D),
        probe_out.reshape(2, 4 * TOK, D // 4),
    )
    flow, tangent, cot, adjoint = unpacked(nsp, out, cot, adjoint)
    full = (2, 32, 32, D // 4)
    return (
        flow.reshape(full),
        tangent.reshape(full),
        adjoint.reshape(2, 8, 32, D),
        cot.reshape(8, 4, HD, HD),
    )


def solution(mesh):
    by_rows = P("tm", "space", None, None)
    by_heads = P("tm", None, None, "space")
    return jax.shard_map(
        functools.partial(on_device, (mesh.shape["tm"], mesh.shape["space"])),
        mesh=mesh,
        in_specs=(by_rows, P(), P(), P(), P(), P(), P("space", None, None), by_rows, by_heads),
        out_specs=(by_heads, by_heads, by_rows, by_rows),
        check_vma=False,
    )
```
